128 devices in a mesh: pipe: 2 (over z_lo), dp: 16 (over z_hi, y, core), tensor: 4 (over x).
Axes of the slice: x: 4, y: 4, z: 4 (z_hi: 2, z_lo: 2; z = z_hi * 2 + z_lo), core: 2. Of those that a mesh axis runs over, the one named last changes fastest.
Arguments:
- inputs: bfloat16 [32, 1024, 1024], P('dp', 'tensor'), may hold values from -6 to 6
- out_grad: bfloat16 [32, 1024, 1024], P('dp', 'tensor'), may hold values from -6 to 6
- norm_gain: float32 [2, 1024], P('pipe'), may hold values from 0.5 to 1.5
- in_gate_x: bfloat16 [2, 1024, 2, 2048], P('pipe', 'dp', None, 'tensor'), may hold values from -0.1875 to 0.1875
- in_read_write: bfloat16 [2, 1024, 256], P('pipe', 'dp'), may hold values from -0.1875 to 0.1875
- in_step: bfloat16 [2, 1024, 32], P('pipe', 'dp', 'tensor'), may hold values from -0.1875 to 0.1875
- conv_main: float32 [2, 5, 2048], P('pipe', None, 'tensor'), may hold values from -3 to 3
- conv_state: float32 [2, 5, 256], P('pipe'), may hold values from -3 to 3
- step_bias: float32 [2, 32], P('pipe', 'tensor'), may hold values from -9 to -3
- log_rate: float32 [2, 32], P('pipe', 'tensor'), may hold values from 0 to 2.77
- skip_gain: float32 [2, 32], P('pipe', 'tensor'), may hold values from 0.5 to 1.5
- gate_gain: float32 [2, 2048], P('pipe', 'tensor'), may hold values from 0.5 to 1.5
- out_weight: bfloat16 [2, 1024, 2048], P('pipe', 'dp', 'tensor'), may hold values from -0.125 to 0.125
Outputs:
- activations: float32 [2, 32, 1024, 1024], P('pipe', 'dp', 'tensor')
- input_grads: float32 [2, 32, 1024, 1024], P('pipe', 'dp', 'tensor')
- grad_norm_gain: float32 [2, 1024], P('pipe')
- grad_in_gate_x: float32 [2, 1024, 2, 2048], P('pipe', 'dp', None, 'tensor')
- grad_in_read_write: float32 [2, 1024, 256], P('pipe', ('dp', 'tensor'))
- grad_in_step: float32 [2, 1024, 32], P('pipe', 'dp', 'tensor')
- grad_conv_main: float32 [2, 5, 2048], P('pipe', None, 'tensor')
- grad_conv_state: float32 [2, 5, 256], P('pipe')
- grad_step_bias: float32 [2, 32], P('pipe', 'tensor')
- grad_log_rate: float32 [2, 32], P('pipe', 'tensor')
- grad_skip_gain: float32 [2, 32], P('pipe', 'tensor')
- grad_gate_gain: float32 [2, 2048], P('pipe', 'tensor')
- grad_out_weight: float32 [2, 1024, 2048], P('pipe', 'dp', 'tensor')
The draws below stay inside these ranges and needn't reach their ends.
All inputs are finite; a program needn't handle non-finite values.
Results may differ from the reference program's by a relative error of at most 0.02.
Values may be sent and summed in bfloat16 or wider, within the bound.
A program may use at most 256 MiB of HBM per device.

```python
from functools import partial
import jax
import jax.numpy as jnp
from jax import lax

D = 1024
HEADS = 32
HEAD_DIM = 64
STATE = 128
CONV = 4
BLOCK = 256
LENGTH = 1024
INNER = 2048
BATCH = 32


def shard_levels(stream_key, shape, cuts, least, high):
    level, own = 1.0, jax.random.fold_in(stream_key, 6)
    for axis_at, shards_of in cuts:
        draws = jnp.exp(jax.random.uniform(jax.random.fold_in(own, axis_at), (shards_of,), jnp.float32, least / len(cuts), high / len(cuts)))
        level = level * jnp.repeat(draws, shape[axis_at] // shards_of).reshape([-1 if axis == axis_at else 1 for axis in range(len(shape))])
    return level


def scatter_about(own_key, shape, spread, most, cuts=(), kind=jnp.bfloat16):
    array = jax.random.normal(own_key, shape, jnp.float32) * spread
    if len(cuts) > 0:
        array = shard_levels(own_key, shape, cuts, -0.22, 0.18) * array
    return jnp.clip(array, min=-most, max=most).astype(kind)


def setup_inputs(seed: int = 0) -> dict:
    seeds = jax.random.split(jax.random.key(seed), 14)
    inputs = scatter_about(seeds[0], (BATCH, LENGTH, D), 1.0, 6.0, ((0, 16), (1, 4)))
    out_grad = scatter_about(seeds[1], (BATCH, LENGTH, D), 1.0, 6.0, ((0, 16), (1, 4)))
    norm_gain = jnp.clip(1.0 + 0.1 * jax.random.normal(seeds[2], (2, D), jnp.float32), 0.5, 1.5)
    in_gate_x = scatter_about(seeds[3], (2, D, 2, INNER), D ** -0.5, 0.1875, ((0, 2), (1, 16), (3, 4)))
    in_read_write = scatter_about(seeds[4], (2, D, 2 * STATE), D ** -0.5, 0.1875, ((0, 2), (1, 16)))
    in_step = scatter_about(seeds[5], (2, D, HEADS), D ** -0.5, 0.1875, ((0, 2), (1, 16), (2, 4)))
    conv_main = scatter_about(seeds[6], (2, CONV + 1, INNER), 0.5, 3.0, ((0, 2), (2, 4)), jnp.float32)
    conv_state = scatter_about(seeds[7], (2, CONV + 1, 2 * STATE), 0.5, 3.0, ((0, 2),), jnp.float32)
    step_bias = jnp.clip(-9.0 + 6.0 * jax.random.uniform(seeds[8], (2, HEADS), jnp.float32) ** shard_levels(seeds[8], (2, HEADS), ((0, 2), (1, 4)), -0.2, 0.2), -9.0, -3.0)
    log_rate = jnp.clip(2.77 * jax.random.uniform(seeds[9], (2, HEADS), jnp.float32) ** shard_levels(seeds[9], (2, HEADS), ((0, 2), (1, 4)), -0.2, 0.2), 0.0, 2.77)
    skip_gain = jnp.clip(1.0 + 0.1 * jax.random.normal(seeds[10], (2, HEADS), jnp.float32), 0.5, 1.5)
    gate_gain = jnp.clip(1.0 + 0.1 * jax.random.normal(seeds[11], (2, INNER), jnp.float32), 0.5, 1.5)
    out_weight = scatter_about(seeds[12], (2, D, INNER), INNER ** -0.5, 0.125, ((0, 2), (1, 16), (2, 4)))
    return {"inputs": inputs, "out_grad": out_grad, "norm_gain": norm_gain, "in_gate_x": in_gate_x, "in_read_write": in_read_write, "in_step": in_step, "conv_main": conv_main, "conv_state": conv_state, "step_bias": step_bias, "log_rate": log_rate, "skip_gain": skip_gain, "gate_gain": gate_gain, "out_weight": out_weight}


EPS = 1e-05
NEG_FILL = -1e+30
HIGH = lax.Precision.HIGHEST

@jax.custom_vjp
def low(v):
    return lax.optimization_barrier(v.astype(jnp.bfloat16)).astype(jnp.float32)

@jax.custom_vjp
def low_back(v):
    return v

def low_keep(v):
    return (low(v), None)

def low_pass(kept, grad):
    return (grad,)

def back_keep(v):
    return (v, None)

def back_low(kept, grad):
    return (low(grad),)
low.defvjp(low_keep, low_pass)
low_back.defvjp(back_keep, back_low)

def causal_conv(signal, taps):
    width = taps.shape[0] - 1
    padded = jnp.pad(signal, ((width - 1, 0), (0, 0)))
    total = taps[width][None, :] + jnp.zeros_like(signal)
    for index in range(width):
        total = total + taps[index][None, :] * padded[index:index + signal.shape[0]]
    return total

def ssd_block(decay, carry, block):
    block_x, block_b, block_c, block_dt = block
    width = block_dt.shape[0]
    log_decay = jnp.cumsum(block_dt * decay[None, :], axis=0)
    products = jnp.einsum('tn,sn->ts', block_c, block_b, precision=HIGH)
    spread_log = log_decay[:, None, :] - log_decay[None, :, :]
    causal = jnp.arange(width)[:, None] >= jnp.arange(width)[None, :]
    mixing = products[:, :, None] * jnp.exp(jnp.where(causal[:, :, None], spread_log, NEG_FILL)) * block_dt[None, :, :]
    within = jnp.einsum('tsh,shp->thp', mixing, block_x, precision=HIGH)
    carried = jnp.einsum('tn,hnp->thp', block_c, carry, precision=HIGH) * jnp.exp(log_decay)[:, :, None]
    to_end = jnp.exp(log_decay[-1][None, :] - log_decay) * block_dt
    carry = jnp.exp(log_decay[-1])[:, None, None] * carry + jnp.einsum('sn,shp->hnp', block_b, to_end[:, :, None] * block_x, precision=HIGH)
    return (carry, within + carried)

def scan_ssd(values, bmat, cmat, delta, decay, skip_gain):
    length, heads, head_width = values.shape
    count = length // BLOCK
    blocks = (values.reshape(count, BLOCK, heads, head_width), bmat.reshape(count, BLOCK, -1), cmat.reshape(count, BLOCK, -1), delta.reshape(count, BLOCK, heads))
    start = jnp.zeros((heads, bmat.shape[1], head_width), values.dtype)
    stepper = jax.checkpoint(partial(ssd_block, decay))
    final, outputs = lax.scan(stepper, start, blocks)
    return outputs.reshape(length, heads, head_width) + skip_gain[None, :, None] * values

def mixer(projected, taps, step_bias, log_rate, skip_gain, inner_width, state_width, head_count):
    gate = projected[:, :inner_width]
    convolved = jax.nn.silu(causal_conv(projected[:, inner_width:2 * inner_width + 2 * state_width], taps))
    values = convolved[:, :inner_width].reshape(-1, head_count, inner_width // head_count)
    bmat = convolved[:, inner_width:inner_width + state_width]
    cmat = convolved[:, inner_width + state_width:]
    delta = jax.nn.softplus(projected[:, 2 * inner_width + 2 * state_width:] + step_bias[None, :])
    outputs = scan_ssd(values, bmat, cmat, delta, -jnp.exp(log_rate), skip_gain)
    return outputs.reshape(projected.shape[0], inner_width) * jax.nn.silu(gate)

def rms_scale(value, gain):
    return value * lax.rsqrt(lax.optimization_barrier(jnp.mean(value * value, -1, keepdims=True)) + EPS) * gain

def layer(residual, params):
    norm_gain, in_gate_x, in_read_write, in_step, conv_main, conv_state, step_bias, log_rate, skip_gain, gate_gain, out_weight = params
    normed = low(rms_scale(residual, norm_gain))
    weight = jnp.concatenate([in_gate_x[:, 0], in_gate_x[:, 1], in_read_write, in_step], 1)
    projected = low_back(jnp.dot(normed, weight, precision=HIGH))
    taps = jnp.concatenate([conv_main, conv_state], 1)
    gated = mixer(projected, taps, step_bias, log_rate, skip_gain, HEADS * HEAD_DIM, STATE, HEADS)
    mixed = low(rms_scale(gated, gate_gain))
    branch = low_back(jnp.dot(mixed, out_weight.T, precision=HIGH))
    return residual + branch

def reference(inputs, out_grad, norm_gain, in_gate_x, in_read_write, in_step, conv_main, conv_state, step_bias, log_rate, skip_gain, gate_gain, out_weight):
    params = tuple((item.astype(jnp.float32) for item in (norm_gain, in_gate_x, in_read_write, in_step, conv_main, conv_state, step_bias, log_rate, skip_gain, gate_gain, out_weight)))

    def forward(weights, sequence, probe):
        first = layer(sequence, tuple((item[0] for item in weights))) + probe
        return (first, layer(first, tuple((item[1] for item in weights))))

    def one_sequence(totals, item):
        sequence, cotangent = item
        probe = jnp.zeros_like(sequence)
        (first, second), pullback = jax.vjp(forward, params, sequence, probe)
        grads, grad_seq, grad_probe = pullback((jnp.zeros_like(first), cotangent))
        totals = jax.tree.map(lambda left, right: left + right, totals, grads)
        return (totals, (first, second, grad_seq, grad_probe))
    start = jax.tree.map(jnp.zeros_like, params)
    grads, (first, second, grad_seq, grad_probe) = lax.scan(one_sequence, start, (inputs.astype(jnp.float32), out_grad.astype(jnp.float32)))
    activations = jnp.stack([first, second])
    input_grads = jnp.stack([grad_seq, grad_probe])
    return (activations, input_grads, grads[0], grads[1], grads[2], grads[3], grads[4], grads[5], grads[6], grads[7], grads[8], grads[9], grads[10])
```

```python
from functools import partial

import jax
import jax.numpy as jnp
import numpy as np
from jax import lax
from jax.experimental import pallas as pl
from jax.experimental.pallas import tpu as pltpu
from jax.sharding import PartitionSpec as P

F32, BF16 = jnp.float32, jnp.bfloat16
EPS = 1e-05
ROWS = 256
CHUNK = 128
LANES = 128
EXACT = lax.Precision.HIGHEST


def mm(left, right, contract=((1,), (0,))):
    return lax.dot_general(left, right, (contract, ((), ())), preferred_element_type=F32)


def mm_exact(left, right, contract=((1,), (0,))):
    return lax.dot_general(
        left, right, (contract, ((), ())), precision=EXACT, preferred_element_type=F32
    )


def spread(value, selector, heads):
    high = value.astype(BF16).astype(F32)
    both = high + pltpu.roll(value - high, heads, 1)
    return mm(both.astype(BF16), selector)


def per_head(value, collector):
    high = value.astype(BF16)
    low = (value - high.astype(F32)).astype(BF16)
    return mm(high, collector) + mm(low, collector)


def softplus(value):
    small = jnp.exp(-jnp.abs(value))
    series = small * (1.0 - small * (0.5 - small * (1.0 / 3.0 - small * 0.25)))
    return jnp.maximum(value, 0.0) + jnp.where(small < 0.01, series, jnp.log(1.0 + small))


def sigmoid(value):
    return 1.0 / (1.0 + jnp.exp(-value))


def iota(shape, axis):
    return lax.broadcasted_iota(jnp.int32, shape, axis)


def column_to_row(column):
    size = column.shape[0]
    same = iota((size, size), 0) == iota((size, size), 1)
    return jnp.sum(jnp.where(same, column, 0.0), 0, keepdims=True)


def row_to_column(row):
    size = row.shape[1]
    same = iota((size, size), 0) == iota((size, size), 1)
    return jnp.sum(jnp.where(same, row, 0.0), 1, keepdims=True)


def steps(raw, head, mask):
    delta = softplus(raw + head[0:1]) * mask
    tri = (iota((CHUNK, CHUNK), 0) >= iota((CHUNK, CHUNK), 1)).astype(F32)
    log_decay = mm_exact(tri, delta * head[1:2])
    return delta, log_decay


def forward_kernel(sizes, rows_ref, w_ref, taps_ref, head_ref, wide_ref, selector_ref,
                   part_ref, squares_ref, z_ref, p_ref, c_ref, raw_ref, y_ref, s_ref, state, pad):
    inner, pair, heads = sizes
    states = pair // 2
    split = inner + inner + pair
    conv = inner + pair

    @pl.when(pl.program_id(0) == 0)
    def _():
        state[...] = jnp.zeros_like(state)
        pad[0:8, :] = jnp.zeros((8, conv), F32)

    @pl.when(pl.program_id(0) > 0)
    def _():
        pad[0:8, :] = pad[ROWS : ROWS + 8, :]

    projected = mm(rows_ref[...], w_ref[:, : split + LANES])
    z_ref[...] = projected[:, :inner]
    p_ref[...] = projected[:, inner:split]
    pad[8 : ROWS + 8, :] = projected[:, inner:split]
    raw_ref[...] = projected[:, split:]
    selector = selector_ref[...]
    head = head_ref[...]
    mask = head[2:3]
    first = iota((CHUNK, LANES), 1) < LANES // 2
    causal = iota((CHUNK, CHUNK), 0) >= iota((CHUNK, CHUNK), 1)
    squares = []
    for chunk in range(ROWS // CHUNK):
        at = slice(chunk * CHUNK, (chunk + 1) * CHUNK)
        c = jnp.broadcast_to(taps_ref[4:5, :], (CHUNK, conv))
        for tap in range(4):
            begin = chunk * CHUNK + 5 + tap
            c = c + taps_ref[tap : tap + 1, :] * pad[begin : begin + CHUNK, :]
        c_ref[at, :] = c
        value = c * sigmoid(c)
        xs = value[:, :inner]
        b_low = value[:, inner : inner + states].astype(BF16)
        c_low = value[:, inner + states :].astype(BF16)
        delta, log_decay = steps(raw_ref[at, :], head, mask)
        turned = log_decay.T
        final = log_decay[CHUNK - 1 : CHUNK, :]
        scaled = spread(delta, selector, heads) * xs
        scaled_low = scaled.astype(BF16)
        products = jnp.where(causal, mm(c_low, b_low, ((1,), (1,))), 0.0)
        within = []
        for two in range(heads // 2):
            lanes = slice(two * LANES, (two + 1) * LANES)
            parts = []
            for h in (2 * two, 2 * two + 1):
                gap = jnp.minimum(log_decay[:, h : h + 1] - turned[h : h + 1, :], 0.0)
                parts.append(mm((products * jnp.exp(gap)).astype(BF16), scaled_low[:, lanes]))
            within.append(jnp.where(first, parts[0], parts[1]))
        old = state[...]
        s_ref[chunk] = old
        carried = mm(c_low, old.astype(BF16)) * spread(jnp.exp(log_decay) * mask, selector, heads)
        y = jnp.concatenate(within, 1) + carried + wide_ref[1:2, :] * xs
        y_ref[at, :] = y
        ends = (spread(jnp.exp(final - log_decay) * mask, selector, heads) * scaled).astype(BF16)
        keep = spread(jnp.broadcast_to(jnp.exp(final) * mask, (8, LANES)), selector, heads)[0:1]
        state[...] = keep * old + mm(b_low, ends, ((0,), (0,)))
        z = z_ref[at, :]
        gated = y * (z * sigmoid(z))
        squares.append(jnp.sum(gated * gated, 1, keepdims=True))
        mixed = (gated * wide_ref[0:1, :]).astype(BF16)
        part_ref[at, :] = mm(mixed, w_ref[:, split + LANES :], ((1,), (1,))).astype(part_ref.dtype)
    row = column_to_row(jnp.concatenate(squares, 0))
    squares_ref[0] = jnp.broadcast_to(row, (8, ROWS))


def backward_kernel(sizes, e_ref, scales_ref, w_ref, taps_ref, head_ref, wide_ref, selector_ref,
                    collector_ref, z_ref, p_ref, c_ref, raw_ref, y_ref, s_ref,
                    part_ref, grad_ref, mixed_ref, taps_out, wide_out, head_out, state, later, pad):
    inner, pair, heads = sizes
    states = pair // 2
    split = inner + inner + pair
    conv = inner + pair

    @pl.when(pl.program_id(0) == 0)
    def _():
        state[...] = jnp.zeros_like(state)
        later[...] = jnp.zeros_like(later)
        pad[ROWS : ROWS + 8, :] = jnp.zeros((8, conv), F32)
        taps_out[...] = jnp.zeros_like(taps_out)
        wide_out[...] = jnp.zeros_like(wide_out)
        head_out[...] = jnp.zeros_like(head_out)

    @pl.when(pl.program_id(0) > 0)
    def _():
        pad[ROWS : ROWS + 8, :] = pad[0:8, :]

    selector = selector_ref[...]
    collector = collector_ref[...]
    head = head_ref[...]
    mask = head[2:3]
    first = iota((CHUNK, LANES), 1) < LANES // 2
    later_in = iota((CHUNK, CHUNK), 1) >= iota((CHUNK, CHUNK), 0)
    last = iota((CHUNK, LANES), 0) == CHUNK - 1
    inverse = row_to_column(scales_ref[0, 0:1, :])
    inner_dot = row_to_column(scales_ref[0, 1:2, :])
    mixed_grad = mm(e_ref[...], w_ref[:, split + LANES :])
    for chunk in reversed(range(ROWS // CHUNK)):
        at = slice(chunk * CHUNK, (chunk + 1) * CHUNK)
        z = z_ref[at, :]
        y = y_ref[at, :]
        sig = sigmoid(z)
        act = z * sig
        g = y * act * inverse[at]
        gain = wide_ref[0:1, :]
        mixed_ref[at, :] = (g * gain).astype(BF16)
        mixed_here = mixed_grad[at]
        gated_grad = inverse[at] * (mixed_here * gain - g * inner_dot[at])
        dy = gated_grad * act
        grad_ref[at, :inner] = (gated_grad * y * (sig * (1.0 + z - act))).astype(BF16)
        c = c_ref[at, :]
        csig = sigmoid(c)
        value = c * csig
        slope = csig * (1.0 + c - value)
        xs = value[:, :inner]
        b_low = value[:, inner : inner + states].astype(BF16)
        c_low = value[:, inner + states :].astype(BF16)
        raw = raw_ref[at, :]
        delta, log_decay = steps(raw, head, mask)
        turned = log_decay.T
        final = log_decay[CHUNK - 1 : CHUNK, :]
        wide_delta = spread(delta, selector, heads)
        scaled = wide_delta * xs
        scaled_low = scaled.astype(BF16)
        dy_low = dy.astype(BF16)
        products = jnp.where(later_in, mm(b_low, c_low, ((1,), (1,))), 0.0)
        dproducts = jnp.zeros((CHUNK, CHUNK), F32)
        within = []
        for two in range(heads // 2):
            lanes = slice(two * LANES, (two + 1) * LANES)
            parts = []
            for odd in range(2):
                h = 2 * two + odd
                mine = first if odd == 0 else ~first
                decay = jnp.exp(jnp.minimum(turned[h : h + 1, :] - log_decay[:, h : h + 1], 0.0))
                parts.append(mm((products * decay).astype(BF16), dy_low[:, lanes]))
                own = jnp.where(mine, scaled_low[:, lanes], jnp.zeros((), BF16))
                dproducts = dproducts + decay * mm(own, dy_low[:, lanes], ((1,), (1,)))
            within.append(jnp.where(first, parts[0], parts[1]))
        dproducts = jnp.where(later_in, dproducts, 0.0).astype(BF16)
        old = s_ref[chunk]
        old_low = old.astype(BF16)
        dstate = state[...]
        dstate_low = dstate.astype(BF16)
        to_end = spread(jnp.exp(final - log_decay) * mask, selector, heads)
        from_start = (spread(jnp.exp(log_decay) * mask, selector, heads) * dy).astype(BF16)
        dscaled = jnp.concatenate(within, 1) + to_end * mm(b_low, dstate_low)
        dc_state = mm(from_start, old_low, ((1,), (1,))) + mm(dproducts, b_low, ((0,), (0,)))
        db_state = mm((to_end * scaled).astype(BF16), dstate_low, ((1,), (1,))) + mm(dproducts, c_low)
        carry = jnp.broadcast_to(jnp.sum(later[...] * dstate, 0, keepdims=True), (8, inner))
        carry = per_head(carry, collector)[0:1]
        keep = spread(jnp.broadcast_to(jnp.exp(final) * mask, (8, LANES)), selector, heads)[0:1]
        state[...] = keep * dstate + mm(c_low, from_start, ((0,), (0,)))
        later[...] = old
        skip = wide_ref[1:2, :]
        flow = dy_low.astype(F32) * (y - skip * xs) - scaled_low.astype(F32) * dscaled
        dlog = per_head(flow, collector) + jnp.where(last, carry, 0.0)
        tri = (iota((CHUNK, CHUNK), 1) >= iota((CHUNK, CHUNK), 0)).astype(F32)
        dstep = mm_exact(tri, dlog)
        ddelta = per_head(xs * dscaled, collector) + head[1:2] * dstep
        draw = ddelta * sigmoid(raw + head[0:1]) * mask
        head_out[0:1, :] += jnp.sum(draw, 0, keepdims=True)
        head_out[1:2, :] += jnp.sum(delta * dstep, 0, keepdims=True)
        wide_out[0:1, :] += jnp.sum(mixed_here * g, 0, keepdims=True)
        wide_out[1:2, :] += jnp.sum(dy * xs, 0, keepdims=True)
        dxs = wide_delta * dscaled + skip * dy
        pad[at, :] = jnp.concatenate([dxs, db_state, dc_state], 1) * slope
        grad_ref[at, split:] = draw.astype(BF16)
    for chunk in range(ROWS // CHUNK):
        at = slice(chunk * CHUNK, (chunk + 1) * CHUNK)
        p = p_ref[at, :]
        total = jnp.zeros((CHUNK, conv), F32)
        for tap in range(4):
            begin = chunk * CHUNK + 3 - tap
            shifted = pad[begin : begin + CHUNK, :]
            total = total + taps_ref[tap : tap + 1, :] * shifted
            taps_out[tap : tap + 1, :] += jnp.sum(p * shifted, 0, keepdims=True)
        taps_out[4:5, :] += jnp.sum(pad[at, :], 0, keepdims=True)
        grad_ref[at, inner:split] = total.astype(BF16)
    part_ref[...] = mm(grad_ref[...], w_ref[:, : split + LANES], ((1,), (1,))).astype(part_ref.dtype)


def constants(inner, heads):
    width = inner // heads
    lane = np.arange(LANES)[:, None]
    channel = np.arange(inner)[None, :] // width
    selector = ((lane % heads == channel) & (lane < 2 * heads)).astype(np.float32)
    collector = (lane == channel).astype(np.float32).T
    return jnp.asarray(selector, BF16), jnp.asarray(collector, BF16)


def forward_call(rows, w, taps, head, wide, inner, pair, heads):
    length, width = rows.shape
    count = length // ROWS
    conv = inner + pair
    states = pair // 2
    selector, _ = constants(inner, heads)
    whole = lambda array: pl.BlockSpec(array.shape, lambda i: (0,) * array.ndim)
    by_rows = lambda columns: pl.BlockSpec((ROWS, columns), lambda i: (i, 0))
    chunks = ROWS // CHUNK
    out = lambda columns, kind=F32: jax.ShapeDtypeStruct((length, columns), kind)
    return pl.pallas_call(
        partial(forward_kernel, (inner, pair, heads)),
        grid=(count,),
        in_specs=[by_rows(width), whole(w), whole(taps), whole(head), whole(wide), whole(selector)],
        out_specs=[
            by_rows(width),
            pl.BlockSpec((1, 8, ROWS), lambda i: (i, 0, 0)),
            by_rows(inner),
            by_rows(conv),
            by_rows(conv),
            by_rows(LANES),
            by_rows(inner),
            pl.BlockSpec((chunks, states, inner), lambda i: (i, 0, 0)),
        ],
        out_shape=[
            out(width, BF16),
            jax.ShapeDtypeStruct((count, 8, ROWS), F32),
            out(inner),
            out(conv),
            out(conv),
            out(LANES),
            out(inner),
            jax.ShapeDtypeStruct((count * chunks, states, inner), F32),
        ],
        scratch_shapes=[pltpu.VMEM((states, inner), F32), pltpu.VMEM((ROWS + 8, conv), F32)],
        compiler_params=pltpu.CompilerParams(vmem_limit_bytes=56 * 2**20),
        name="layer_forward",
    )(rows, w, taps, head, wide, selector)


def backward_call(e, scales, w, taps, head, wide, saved, inner, pair, heads):
    length, width = e.shape
    count = length // ROWS
    conv = inner + pair
    states = pair // 2
    split = inner + conv
    z, p, c, raw, y, s = saved
    selector, collector = constants(inner, heads)
    whole = lambda array: pl.BlockSpec(array.shape, lambda i: (0,) * array.ndim)
    by_rows = lambda columns: pl.BlockSpec((ROWS, columns), lambda i: (count - 1 - i, 0))
    fixed = lambda columns: pl.BlockSpec((8, columns), lambda i: (0, 0))
    chunks = ROWS // CHUNK
    by_block = lambda lead, rows, columns: pl.BlockSpec(
        (lead, rows, columns), lambda i: (count - 1 - i, 0, 0)
    )
    out = lambda columns, kind=F32: jax.ShapeDtypeStruct((length, columns), kind)
    few = lambda columns: jax.ShapeDtypeStruct((8, columns), F32)
    return pl.pallas_call(
        partial(backward_kernel, (inner, pair, heads)),
        grid=(count,),
        in_specs=[
            by_rows(width),
            by_block(1, 8, ROWS),
            whole(w),
            whole(taps),
            whole(head),
            whole(wide),
            whole(selector),
            whole(collector),
            by_rows(inner),
            by_rows(conv),
            by_rows(conv),
            by_rows(LANES),
            by_rows(inner),
            by_block(chunks, states, inner),
        ],
        out_specs=[
            by_rows(width),
            by_rows(split + LANES),
            by_rows(inner),
            fixed(conv),
            fixed(inner),
            fixed(LANES),
        ],
        out_shape=[
            out(width, BF16),
            out(split + LANES, BF16),
            out(inner, BF16),
            few(conv),
            few(inner),
            few(LANES),
        ],
        scratch_shapes=[
            pltpu.VMEM((states, inner), F32),
            pltpu.VMEM((states, inner), F32),
            pltpu.VMEM((ROWS + 8, conv), F32),
        ],
        compiler_params=pltpu.CompilerParams(vmem_limit_bytes=56 * 2**20),
        name="layer_backward",
    )(e, scales, w, taps, head, wide, selector, collector, z, p, c, raw, y, s)


def swap(value):
    return lax.ppermute(value, "pipe", [(0, 1), (1, 0)])


def both_layers(value, first):
    other = swap(value)
    return jnp.where(first, value, other), jnp.where(first, other, value)


def by_layer(values, first):
    mine = jnp.where(first, values[0], values[1])
    theirs = swap(jnp.where(first, values[1], values[0]).astype(BF16)).astype(F32)
    return jnp.where(first, jnp.stack([mine, theirs]), jnp.stack([theirs, mine]))


def body(inputs, out_grad, norm_gain, in_gate_x, in_read_write, in_step, conv_main, conv_state,
         step_bias, log_rate, skip_gain, gate_gain, out_weight):
    _, part, width = inputs.shape
    inner = out_weight.shape[2]
    pair = in_read_write.shape[2]
    heads = step_bias.shape[1]
    whole_inner = inner * lax.axis_size("tensor")
    split = 2 * inner + pair
    blocks = lax.axis_size("tensor")
    pipe = lax.axis_index("pipe")
    first = pipe == 0
    shard = jnp.concatenate(
        [
            in_gate_x[0, :, 0],
            in_gate_x[0, :, 1],
            in_read_write[0],
            jnp.pad(in_step[0], ((0, 0), (0, LANES - heads))),
            out_weight[0],
        ],
        1,
    )
    taps = jnp.pad(jnp.concatenate([conv_main[0], conv_state[0]], 1), ((0, 3), (0, 0)))
    rate = -jnp.exp(log_rate[0])
    head = jnp.stack([step_bias[0], rate, jnp.ones_like(rate)])
    head = jnp.pad(head, ((0, 5), (0, LANES - heads)))
    wide = jnp.stack([gate_gain[0], jnp.repeat(skip_gain[0], inner // heads)])
    wide = jnp.pad(wide, ((0, 6), (0, 0)))
    shards = both_layers(shard, first)
    weights = [lax.all_gather(item, "dp", axis=0, tiled=True) for item in shards]
    gains, taps, head, wide = (
        both_layers(item, first) for item in (norm_gain, taps, head, wide)
    )
    residual = lax.dynamic_index_in_dim(inputs, pipe, 0, False).astype(F32)
    kept = []
    activations = []
    for layer in range(2):
        scale = lax.rsqrt(jnp.mean(residual * residual, -1, keepdims=True) + EPS)
        normed = (residual * scale * gains[layer]).astype(BF16)
        rows = lax.all_gather(normed, "tensor", axis=0, tiled=True)
        partial_rows, squares, *saved = forward_call(
            rows, weights[layer], taps[layer], head[layer], wide[layer], inner, pair, heads
        )
        squares = lax.psum_scatter(squares, "tensor", scatter_dimension=0, tiled=True)[0, 0]
        summed = lax.psum_scatter(partial_rows, "tensor", scatter_dimension=0, tiled=True)
        inverse = lax.rsqrt(squares / whole_inner + EPS)
        branch = inverse[:, None] * summed.astype(F32)
        kept.append((residual, scale, rows, inverse, branch, saved))
        residual = residual + branch
        activations.append(residual)
    activations = by_layer(activations, first)
    error = lax.dynamic_index_in_dim(out_grad, pipe, 0, False).astype(F32)
    input_grads = [None, None]
    large = [None, None]
    small = [None, None]
    for layer in (1, 0):
        before, scale, rows, inverse, branch, saved = kept[layer]
        sent = error.astype(BF16)
        dots = jnp.sum(sent.astype(F32) * branch, -1) / whole_inner
        scales = jnp.pad(jnp.stack([inverse, dots]), ((0, 6), (0, 0)))[None]
        scales = lax.all_gather(scales, "tensor", axis=0, tiled=True)
        errors = lax.all_gather(sent, "tensor", axis=0, tiled=True)
        partial_rows, grad, mixed, taps_out, wide_out, head_out = backward_call(
            errors, scales, weights[layer], taps[layer], head[layer], wide[layer], saved,
            inner, pair, heads,
        )
        summed = lax.psum_scatter(partial_rows, "tensor", scatter_dimension=0, tiled=True)
        summed = summed.astype(F32)
        unit = before * scale
        scaled = summed * gains[layer]
        mean = jnp.mean(scaled * unit, -1, keepdims=True)
        error = error + scale * (scaled - unit * mean)
        input_grads[layer] = error
        grad_in = jnp.einsum("td,tc->dc", rows, grad, preferred_element_type=F32)
        grad_out = jnp.einsum("td,tc->dc", errors, mixed, preferred_element_type=F32)
        large[layer] = jnp.concatenate([grad_in, grad_out], 1).astype(BF16)
        small[layer] = (
            taps_out[:5, :inner],
            wide_out[0],
            wide_out[1].reshape(heads, -1).sum(1),
            head_out[0, :heads],
            head_out[1, :heads] * head[layer][1, :heads],
            taps_out[:5, inner:],
            jnp.sum(summed * unit, 0),
        )
    input_grads = by_layer(input_grads, first)
    reduced = [lax.psum_scatter(item, "dp", scatter_dimension=0, tiled=True) for item in large]
    mine = jnp.where(first, reduced[0], reduced[1]).astype(F32)
    theirs = swap(jnp.where(first, reduced[1], reduced[0])).astype(F32)
    large = mine + theirs
    state_grad = lax.psum_scatter(
        large[:, 2 * inner : split], "tensor", scatter_dimension=0, tiled=True
    )
    few = [jnp.concatenate([item.reshape(-1) for item in one]) for one in small]
    few = lax.psum(jnp.stack(few), ("pipe", "dp"))
    few = jnp.where(first, few[0], few[1])
    shared = lax.psum(few[-(5 * pair + width) :], "tensor")
    sizes = np.cumsum([5 * inner, inner, heads, heads, heads])
    main, gate, skip, bias, rates = jnp.split(few[: sizes[-1]], sizes[:-1])
    return (
        activations[None],
        input_grads[None],
        shared[None, 5 * pair :],
        large[:, : 2 * inner].reshape(1, -1, 2, inner),
        state_grad[None],
        large[None, :, split : split + heads],
        main.reshape(1, 5, inner),
        shared[: 5 * pair].reshape(1, 5, pair),
        bias[None],
        rates[None],
        skip[None],
        gate[None],
        large[None, :, split + LANES :],
    )


def solution(mesh):
    in_specs = (
        P("dp", "tensor", None),
        P("dp", "tensor", None),
        P("pipe", None),
        P("pipe", "dp", None, "tensor"),
        P("pipe", "dp", None),
        P("pipe", "dp", "tensor"),
        P("pipe", None, "tensor"),
        P("pipe", None, None),
        P("pipe", "tensor"),
        P("pipe", "tensor"),
        P("pipe", "tensor"),
        P("pipe", "tensor"),
        P("pipe", "dp", "tensor"),
    )
    out_specs = (
        P("pipe", "dp", "tensor", None),
        P("pipe", "dp", "tensor", None),
        P("pipe", None),
        P("pipe", "dp", None, "tensor"),
        P("pipe", ("dp", "tensor"), None),
        P("pipe", "dp", "tensor"),
        P("pipe", None, "tensor"),
        P("pipe", None, None),
        P("pipe", "tensor"),
        P("pipe", "tensor"),
        P("pipe", "tensor"),
        P("pipe", "tensor"),
        P("pipe", "dp", "tensor"),
    )
    return jax.shard_map(body, mesh=mesh, in_specs=in_specs, out_specs=out_specs, check_vma=False)
```

```python
from functools import partial

import jax
import jax.numpy as jnp
import numpy as np
from jax import lax
from jax.experimental import pallas as pl
from jax.experimental.pallas import tpu as pltpu
from jax.sharding import PartitionSpec as P

F32, BF16 = jnp.float32, jnp.bfloat16
EPS = 1e-05
ROWS = 256
CHUNK = 128
LANES = 128
EXACT = lax.Precision.HIGHEST


def mm(left, right, contract=((1,), (0,))):
    return lax.dot_general(left, right, (contract, ((), ())), preferred_element_type=F32)


def mm_exact(left, right, contract=((1,), (0,))):
    return lax.dot_general(
        left, right, (contract, ((), ())), precision=EXACT, preferred_element_type=F32
    )


def spread(value, selector, heads):
    high = value.astype(BF16).astype(F32)
    both = high + pltpu.roll(value - high, heads, 1)
    return mm(both.astype(BF16), selector)


def per_head(value, collector):
    high = value.astype(BF16)
    low = (value - high.astype(F32)).astype(BF16)
    return mm(high, collector) + mm(low, collector)


def softplus(value):
    small = jnp.exp(-jnp.abs(value))
    series = small * (1.0 - small * (0.5 - small * (1.0 / 3.0 - small * 0.25)))
    return jnp.maximum(value, 0.0) + jnp.where(small < 0.01, series, jnp.log(1.0 + small))


def sigmoid(value):
    return 1.0 / (1.0 + jnp.exp(-value))


def iota(shape, axis):
    return lax.broadcasted_iota(jnp.int32, shape, axis)


def column_to_row(column):
    size = column.shape[0]
    same = iota((size, size), 0) == iota((size, size), 1)
    return jnp.sum(jnp.where(same, column, 0.0), 0, keepdims=True)


def row_to_column(row):
    size = row.shape[1]
    same = iota((size, size), 0) == iota((size, size), 1)
    return jnp.sum(jnp.where(same, row, 0.0), 1, keepdims=True)


def steps(raw, bias, rate, mask):
    delta = softplus(raw + bias) * mask
    tri = (iota((CHUNK, CHUNK), 0) >= iota((CHUNK, CHUNK), 1)).astype(F32)
    log_decay = mm_exact(tri, delta * rate)
    return delta, log_decay


def forward_kernel(sizes, rows_ref, w_ref, few_ref, selector_ref,
                   part_ref, squares_ref, z_ref, p_ref, c_ref, raw_ref, y_ref, s_ref, state, pad):
    inner, pair, heads = sizes
    states = pair // 2
    split = inner + inner + pair
    conv = inner + pair

    @pl.when(pl.program_id(0) == 0)
    def _():
        state[...] = jnp.zeros_like(state)
        pad[0:8, :] = jnp.zeros((8, conv), F32)

    @pl.when(pl.program_id(0) > 0)
    def _():
        pad[0:8, :] = pad[ROWS : ROWS + 8, :]

    projected = mm(rows_ref[...], w_ref[:, : split + LANES])
    z_ref[...] = projected[:, :inner]
    p_ref[...] = projected[:, inner:split]
    pad[8 : ROWS + 8, :] = projected[:, inner:split]
    raw_ref[...] = projected[:, split:]
    selector = selector_ref[...]
    bias = few_ref[0, 5:6, inner : inner + LANES]
    rate = few_ref[0, 5:6, inner + LANES : inner + 2 * LANES]
    gain = few_ref[0, 5:6, :inner]
    skip = few_ref[0, 6:7, :inner]
    mask = (iota((1, LANES), 1) < heads).astype(F32)
    first = iota((CHUNK, LANES), 1) < LANES // 2
    causal = iota((CHUNK, CHUNK), 0) >= iota((CHUNK, CHUNK), 1)
    squares = []
    for chunk in range(ROWS // CHUNK):
        at = slice(chunk * CHUNK, (chunk + 1) * CHUNK)
        c = jnp.broadcast_to(few_ref[0, 4:5, :], (CHUNK, conv))
        for tap in range(4):
            begin = chunk * CHUNK + 5 + tap
            c = c + few_ref[0, tap : tap + 1, :] * pad[begin : begin + CHUNK, :]
        c_ref[at, :] = c
        value = c * sigmoid(c)
        xs = value[:, :inner]
        b_low = value[:, inner : inner + states].astype(BF16)
        c_low = value[:, inner + states :].astype(BF16)
        delta, log_decay = steps(raw_ref[at, :], bias, rate, mask)
        turned = log_decay.T
        final = log_decay[CHUNK - 1 : CHUNK, :]
        scaled = spread(delta, selector, heads) * xs
        scaled_low = scaled.astype(BF16)
        products = jnp.where(causal, mm(c_low, b_low, ((1,), (1,))), 0.0)
        within = []
        for two in range(heads // 2):
            lanes = slice(two * LANES, (two + 1) * LANES)
            parts = []
            for h in (2 * two, 2 * two + 1):
                gap = jnp.minimum(log_decay[:, h : h + 1] - turned[h : h + 1, :], 0.0)
                parts.append(mm((products * jnp.exp(gap)).astype(BF16), scaled_low[:, lanes]))
            within.append(jnp.where(first, parts[0], parts[1]))
        old = state[...]
        s_ref[chunk] = old
        carried = mm(c_low, old.astype(BF16)) * spread(jnp.exp(log_decay) * mask, selector, heads)
        y = jnp.concatenate(within, 1) + carried + skip * xs
        y_ref[at, :] = y
        ends = (spread(jnp.exp(final - log_decay) * mask, selector, heads) * scaled).astype(BF16)
        keep = spread(jnp.broadcast_to(jnp.exp(final) * mask, (8, LANES)), selector, heads)[0:1]
        state[...] = keep * old + mm(b_low, ends, ((0,), (0,)))
        z = z_ref[at, :]
        gated = y * (z * sigmoid(z))
        squares.append(jnp.sum(gated * gated, 1, keepdims=True))
        mixed = (gated * gain).astype(BF16)
        part_ref[at, :] = mm(mixed, w_ref[:, split + LANES :], ((1,), (1,))).astype(part_ref.dtype)
    row = column_to_row(jnp.concatenate(squares, 0))
    squares_ref[0] = jnp.broadcast_to(row, (8, ROWS))


def backward_kernel(sizes, e_ref, scales_ref, w_ref, few_ref, selector_ref,
                    collector_ref, z_ref, p_ref, c_ref, raw_ref, y_ref, s_ref,
                    part_ref, grad_ref, mixed_ref, few_out, state, later, pad):
    inner, pair, heads = sizes
    states = pair // 2
    split = inner + inner + pair
    conv = inner + pair

    @pl.when(pl.program_id(0) == 0)
    def _():
        state[...] = jnp.zeros_like(state)
        later[...] = jnp.zeros_like(later)
        pad[ROWS : ROWS + 8, :] = jnp.zeros((8, conv), F32)
        few_out[...] = jnp.zeros_like(few_out)

    @pl.when(pl.program_id(0) > 0)
    def _():
        pad[ROWS : ROWS + 8, :] = pad[0:8, :]

    selector = selector_ref[...]
    collector = collector_ref[...]
    bias = few_ref[0, 5:6, inner : inner + LANES]
    rate = few_ref[0, 5:6, inner + LANES : inner + 2 * LANES]
    gain = few_ref[0, 5:6, :inner]
    skip = few_ref[0, 6:7, :inner]
    mask = (iota((1, LANES), 1) < heads).astype(F32)
    first = iota((CHUNK, LANES), 1) < LANES // 2
    later_in = iota((CHUNK, CHUNK), 1) >= iota((CHUNK, CHUNK), 0)
    last = iota((CHUNK, LANES), 0) == CHUNK - 1
    inverse = row_to_column(scales_ref[0, 0:1, :])
    inner_dot = row_to_column(scales_ref[0, 1:2, :])
    mixed_grad = mm(e_ref[...], w_ref[:, split + LANES :])
    for chunk in reversed(range(ROWS // CHUNK)):
        at = slice(chunk * CHUNK, (chunk + 1) * CHUNK)
        z = z_ref[at, :]
        y = y_ref[at, :]
        sig = sigmoid(z)
        act = z * sig
        g = y * act * inverse[at]
        mixed_ref[at, :] = (g * gain).astype(BF16)
        mixed_here = mixed_grad[at]
        gated_grad = inverse[at] * (mixed_here * gain - g * inner_dot[at])
        dy = gated_grad * act
        grad_ref[at, :inner] = (gated_grad * y * (sig * (1.0 + z - act))).astype(BF16)
        c = c_ref[at, :]
        csig = sigmoid(c)
        value = c * csig
        slope = csig * (1.0 + c - value)
        xs = value[:, :inner]
        b_low = value[:, inner : inner + states].astype(BF16)
        c_low = value[:, inner + states :].astype(BF16)
        raw = raw_ref[at, :]
        delta, log_decay = steps(raw, bias, rate, mask)
        turned = log_decay.T
        final = log_decay[CHUNK - 1 : CHUNK, :]
        wide_delta = spread(delta, selector, heads)
        scaled = wide_delta * xs
        scaled_low = scaled.astype(BF16)
        dy_low = dy.astype(BF16)
        products = jnp.where(later_in, mm(b_low, c_low, ((1,), (1,))), 0.0)
        dproducts = jnp.zeros((CHUNK, CHUNK), F32)
        within = []
        for two in range(heads // 2):
            lanes = slice(two * LANES, (two + 1) * LANES)
            parts = []
            for odd in range(2):
                h = 2 * two + odd
                mine = first if odd == 0 else ~first
                decay = jnp.exp(jnp.minimum(turned[h : h + 1, :] - log_decay[:, h : h + 1], 0.0))
                parts.append(mm((products * decay).astype(BF16), dy_low[:, lanes]))
                own = jnp.where(mine, scaled_low[:, lanes], jnp.zeros((), BF16))
                dproducts = dproducts + decay * mm(own, dy_low[:, lanes], ((1,), (1,)))
            within.append(jnp.where(first, parts[0], parts[1]))
        dproducts = jnp.where(later_in, dproducts, 0.0).astype(BF16)
        old = s_ref[chunk]
        old_low = old.astype(BF16)
        dstate = state[...]
        dstate_low = dstate.astype(BF16)
        to_end = spread(jnp.exp(final - log_decay) * mask, selector, heads)
        from_start = (spread(jnp.exp(log_decay) * mask, selector, heads) * dy).astype(BF16)
        dscaled = jnp.concatenate(within, 1) + to_end * mm(b_low, dstate_low)
        dc_state = mm(from_start, old_low, ((1,), (1,))) + mm(dproducts, b_low, ((0,), (0,)))
        db_state = mm((to_end * scaled).astype(BF16), dstate_low, ((1,), (1,))) + mm(dproducts, c_low)
        carry = jnp.broadcast_to(jnp.sum(later[...] * dstate, 0, keepdims=True), (8, inner))
        carry = per_head(carry, collector)[0:1]
        keep = spread(jnp.broadcast_to(jnp.exp(final) * mask, (8, LANES)), selector, heads)[0:1]
        state[...] = keep * dstate + mm(c_low, from_start, ((0,), (0,)))
        later[...] = old
        flow = dy_low.astype(F32) * (y - skip * xs) - scaled_low.astype(F32) * dscaled
        dlog = per_head(flow, collector) + jnp.where(last, carry, 0.0)
        tri = (iota((CHUNK, CHUNK), 1) >= iota((CHUNK, CHUNK), 0)).astype(F32)
        dstep = mm_exact(tri, dlog)
        ddelta = per_head(xs * dscaled, collector) + rate * dstep
        draw = ddelta * sigmoid(raw + bias) * mask
        few_out[5:6, inner : inner + LANES] += jnp.sum(draw, 0, keepdims=True)
        few_out[5:6, inner + LANES : inner + 2 * LANES] += jnp.sum(delta * dstep, 0, keepdims=True)
        few_out[5:6, :inner] += jnp.sum(mixed_here * g, 0, keepdims=True)
        few_out[6:7, :inner] += jnp.sum(dy * xs, 0, keepdims=True)
        dxs = wide_delta * dscaled + skip * dy
        pad[at, :] = jnp.concatenate([dxs, db_state, dc_state], 1) * slope
        grad_ref[at, split:] = draw.astype(BF16)
    for chunk in range(ROWS // CHUNK):
        at = slice(chunk * CHUNK, (chunk + 1) * CHUNK)
        p = p_ref[at, :]
        total = jnp.zeros((CHUNK, conv), F32)
        for tap in range(4):
            begin = chunk * CHUNK + 3 - tap
            shifted = pad[begin : begin + CHUNK, :]
            total = total + few_ref[0, tap : tap + 1, :] * shifted
            few_out[tap : tap + 1, :] += jnp.sum(p * shifted, 0, keepdims=True)
        few_out[4:5, :] += jnp.sum(pad[at, :], 0, keepdims=True)
        grad_ref[at, inner:split] = total.astype(BF16)
    part_ref[...] = mm(grad_ref[...], w_ref[:, : split + LANES], ((1,), (1,))).astype(part_ref.dtype)


def constants(inner, heads):
    width = inner // heads
    lane = np.arange(LANES)[:, None]
    channel = np.arange(inner)[None, :] // width
    selector = ((lane % heads == channel) & (lane < 2 * heads)).astype(np.float32)
    collector = (lane == channel).astype(np.float32).T
    return jnp.asarray(selector, BF16), jnp.asarray(collector, BF16)


def whole(array):
    return pl.BlockSpec(array.shape, lambda i: (0,) * array.ndim)


def forward_call(layer, rows, w, few, inner, pair, heads):
    length, width = rows.shape
    count = length // ROWS
    conv = inner + pair
    states = pair // 2
    selector, _ = constants(inner, heads)
    by_rows = lambda columns: pl.BlockSpec((ROWS, columns), lambda i: (i, 0))
    chunks = ROWS // CHUNK
    out = lambda columns, kind=F32: jax.ShapeDtypeStruct((length, columns), kind)
    return pl.pallas_call(
        partial(forward_kernel, (inner, pair, heads)),
        grid=(count,),
        in_specs=[
            by_rows(width),
            whole(w),
            pl.BlockSpec((1, 8, conv), lambda i: (layer, 0, 0)),
            whole(selector),
        ],
        out_specs=[
            by_rows(width),
            pl.BlockSpec((1, 8, ROWS), lambda i: (i, 0, 0)),
            by_rows(inner),
            by_rows(conv),
            by_rows(conv),
            by_rows(LANES),
            by_rows(inner),
            pl.BlockSpec((chunks, states, inner), lambda i: (i, 0, 0)),
        ],
        out_shape=[
            out(width, BF16),
            jax.ShapeDtypeStruct((count, 8, ROWS), F32),
            out(inner),
            out(conv),
            out(conv),
            out(LANES),
            out(inner),
            jax.ShapeDtypeStruct((count * chunks, states, inner), F32),
        ],
        scratch_shapes=[pltpu.VMEM((states, inner), F32), pltpu.VMEM((ROWS + 8, conv), F32)],
        compiler_params=pltpu.CompilerParams(vmem_limit_bytes=56 * 2**20),
        name="layer_forward",
    )(rows, w, few, selector)


def backward_call(layer, e, scales, w, few, saved, inner, pair, heads):
    length, width = e.shape
    count = length // ROWS
    conv = inner + pair
    states = pair // 2
    split = inner + conv
    z, p, c, raw, y, s = saved
    selector, collector = constants(inner, heads)
    by_rows = lambda columns: pl.BlockSpec((ROWS, columns), lambda i: (count - 1 - i, 0))
    chunks = ROWS // CHUNK
    by_block = lambda lead, rows, columns: pl.BlockSpec(
        (lead, rows, columns), lambda i: (count - 1 - i, 0, 0)
    )
    out = lambda columns, kind=F32: jax.ShapeDtypeStruct((length, columns), kind)
    return pl.pallas_call(
        partial(backward_kernel, (inner, pair, heads)),
        grid=(count,),
        in_specs=[
            by_rows(width),
            by_block(1, 8, ROWS),
            whole(w),
            pl.BlockSpec((1, 8, conv), lambda i: (layer, 0, 0)),
            whole(selector),
            whole(collector),
            by_rows(inner),
            by_rows(conv),
            by_rows(conv),
            by_rows(LANES),
            by_rows(inner),
            by_block(chunks, states, inner),
        ],
        out_specs=[
            by_rows(width),
            by_rows(split + LANES),
            by_rows(inner),
            pl.BlockSpec((8, conv), lambda i: (0, 0)),
        ],
        out_shape=[
            out(width, BF16),
            out(split + LANES, BF16),
            out(inner, BF16),
            jax.ShapeDtypeStruct((8, conv), F32),
        ],
        scratch_shapes=[
            pltpu.VMEM((states, inner), F32),
            pltpu.VMEM((states, inner), F32),
            pltpu.VMEM((ROWS + 8, conv), F32),
        ],
        compiler_params=pltpu.CompilerParams(vmem_limit_bytes=56 * 2**20),
        name="layer_backward",
    )(e, scales, w, few, selector, collector, z, p, c, raw, y, s)


def weight_kernel(rows_ref, grad_ref, errors_ref, mixed_ref, out_ref):
    columns = grad_ref.shape[1]
    turn = ((0,), (0,))
    out_ref[:, :columns] = mm(rows_ref[...], grad_ref[...], turn).astype(out_ref.dtype)
    out_ref[:, columns:] = mm(errors_ref[...], mixed_ref[...], turn).astype(out_ref.dtype)


def weight_call(rows, grad, errors, mixed):
    length, width = rows.shape
    columns = grad.shape[1] + mixed.shape[1]
    by_columns = pl.BlockSpec((length, ROWS), lambda i: (0, i))
    return pl.pallas_call(
        weight_kernel,
        grid=(width // ROWS,),
        in_specs=[by_columns, whole(grad), by_columns, whole(mixed)],
        out_specs=pl.BlockSpec((ROWS, columns), lambda i: (i, 0)),
        out_shape=jax.ShapeDtypeStruct((width, columns), BF16),
        compiler_params=pltpu.CompilerParams(vmem_limit_bytes=56 * 2**20),
        name="weight_gradients",
    )(rows, grad, errors, mixed)


MESH = pl.DeviceIdType.MESH
ANY = pl.BlockSpec(memory_space=pl.ANY)
VMEM = pl.BlockSpec(memory_space=pltpu.VMEM)


def place():
    pipe, dp, x = lax.axis_index("pipe"), lax.axis_index("dp"), lax.axis_index("tensor")
    return (dp // 8) * 2 + pipe, (dp // 2) % 4, dp % 2, x


def at_z(z):
    _, y, core, _ = place()
    return {"pipe": z % 2, "dp": ((z // 2) * 4 + y) * 2 + core}


def at_y(y):
    z, _, core, _ = place()
    return {"dp": ((z // 2) * 4 + y) * 2 + core}


def at_core(core):
    z, y, _, _ = place()
    return {"dp": ((z // 2) * 4 + y) * 2 + core}


def at_x(x):
    return {"tensor": x}


def at_pipe(pipe):
    return {"pipe": pipe}


def greet(*devices):
    barrier = pltpu.get_barrier_semaphore()
    for device in devices:
        pl.semaphore_signal(barrier, inc=1, device_id=device, device_id_type=MESH)
    pl.semaphore_wait(barrier, len(devices))


def around(me, device, steps=(1, 3)):
    return [device((me + step) % 4) for step in steps]


def remote(source, target, sems, index, device):
    return pltpu.make_async_remote_copy(
        src_ref=source,
        dst_ref=target,
        send_sem=sems[0].at[index],
        recv_sem=sems[1].at[index],
        device_id=device,
        device_id_type=MESH,
    )


class RingGather:
    def __init__(self, me, device, own, slot, sems):
        right, left, across = (me + 1) % 4, (me + 3) % 4, (me + 2) % 4
        to_right, to_left = device(right), device(left)
        self.copies = [
            remote(own(0), slot(me, 0), sems, 0, to_right),
            remote(own(1), slot(me, 1), sems, 1, to_left),
            remote(own(1), slot(me, 1), sems, 2, to_right),
            remote(own(0), slot(me, 0), sems, 3, to_left),
            remote(slot(left, 0), slot(left, 0), sems, 4, to_right),
            remote(slot(right, 1), slot(right, 1), sems, 5, to_left),
        ]
        self.origins = [(left, 0), (right, 1), (left, 1), (right, 0), (across, 0), (across, 1)]
        self.local = [
            pltpu.make_async_copy(own(half), slot(me, half), sems[2].at[half]) for half in range(2)
        ]

    def start(self):
        for copy in self.copies[:4]:
            copy.start()
        for copy in self.local:
            copy.start()

    def relay(self):
        for index in range(2):
            self.copies[index].wait_recv()
            self.copies[4 + index].start()

    def wait(self, *indices):
        for index in indices:
            self.copies[index].wait_recv()

    def finish(self):
        for copy in self.local:
            copy.wait()
        for copy in self.copies:
            copy.wait_send()


class RingScatter:
    def __init__(self, me, device, blocks, buffers, sems):
        self.me, self.right, self.left = me, (me + 1) % 4, (me + 3) % 4
        across = (me + 2) % 4
        self.blocks, self.buffers = blocks, buffers
        relays, sums, arrived = buffers
        to_right, to_left = device(self.right), device(self.left)
        self.copies = [
            remote(blocks.at[across, 0], relays.at[0], sems, 0, to_right),
            remote(blocks.at[across, 1], relays.at[1], sems, 1, to_left),
            remote(blocks.at[self.right, 1], arrived.at[0, 1], sems, 2, to_right),
            remote(blocks.at[self.left, 0], arrived.at[1, 0], sems, 3, to_left),
            remote(sums.at[0], arrived.at[0, 0], sems, 4, to_right),
            remote(sums.at[1], arrived.at[1, 1], sems, 5, to_left),
        ]

    def start(self):
        for copy in self.copies[:4]:
            copy.start()

    def relay(self):
        relays, sums, _ = self.buffers
        for half, block in ((0, self.right), (1, self.left)):
            self.copies[half].wait_recv()
            total = relays[half].astype(F32) + self.blocks[block, half].astype(F32)
            sums[half] = total.astype(sums.dtype)
            self.copies[4 + half].start()

    def wait(self):
        for index in range(2, 6):
            self.copies[index].wait_recv()

    def result(self, half):
        arrived = self.buffers[2]
        mine = self.blocks[self.me, half].astype(F32)
        return mine + arrived[0, half].astype(F32) + arrived[1, half].astype(F32)

    def finish(self):
        for copy in self.copies:
            copy.wait_send()


class Everyone:
    def __init__(self, me, device, source, target, sems):
        self.copies = [
            remote(source((me + step) % 4), target(me), sems, step - 1, device((me + step) % 4))
            for step in (1, 2, 3)
        ]

    def start(self):
        for copy in self.copies:
            copy.start()

    def wait(self):
        for copy in self.copies:
            copy.wait()


def dma(count):
    return [pltpu.SemaphoreType.DMA((count,)), pltpu.SemaphoreType.DMA((count,))]


def gather_sems():
    return dma(6) + [pltpu.SemaphoreType.DMA((2,))]


def scatter_buffers(rows, columns):
    return [
        pltpu.VMEM((2, rows // 2, columns), BF16),
        pltpu.VMEM((2, rows // 2, columns), BF16),
        pltpu.VMEM((2, 2, rows // 2, columns), BF16),
    ]


def norm_scale(value):
    return lax.rsqrt(jnp.mean(value * value, -1, keepdims=True) + EPS)


def norm_gain_of(few, layer, lead):
    return jnp.concatenate([few[layer, 6:7, lead:], few[layer, 7:8, :]], 1)


class WeightGather:
    def __init__(self, source, target, sems, core_sems):
        _, y, core, _ = place()
        self.core_sems, self.device = core_sems, at_core(1 - core)
        self.slot = lambda origin, half: target.at[half, origin, core]
        self.ring = RingGather(y, at_y, source, self.slot, sems)
        self.hand = [remote(source(half), self.slot(y, half), core_sems, 6 + half, self.device) for half in range(2)]

    def start(self):
        self.ring.start()
        for copy in self.hand:
            copy.start()

    def pass_on(self, index):
        piece = self.slot(*self.ring.origins[index])
        copy = remote(piece, piece, self.core_sems, index, self.device)
        copy.start()
        self.hand.append(copy)

    def relay(self):
        self.ring.relay()
        for index in range(2):
            self.pass_on(index)

    def finish(self):
        for index in range(2, 6):
            self.ring.wait(index)
            self.pass_on(index)
        self.ring.finish()
        for copy in self.hand:
            copy.wait()


def open_kernel(lead, inputs, shard, few_in, rows, spread_weights, weights, few, raw, normed, few_both,
                xs, xr, xl, zs, zr, zl, ys, yr, yl, cs, cr, fs, fr, load):
    z, y, core, x = place()
    pipe = z % 2
    read = pltpu.make_async_copy(inputs.at[pipe], raw, load.at[0])
    read.start()
    few_both[pipe] = few_in[...]
    greet(*around(x, at_x), *around(y, at_y), *around(z, at_z), at_core(1 - core), at_pipe(1 - pipe))
    swap = remote(few_both.at[pipe], few_both.at[pipe], (fs, fr), 0, at_pipe(1 - pipe))
    swap.start()
    z_slot = lambda origin, half: spread_weights.at[(origin % 2) * 2 + origin // 2, half]
    z_ring = RingGather(z, at_z, lambda half: shard.at[half], z_slot, (zs, zr, zl))
    z_ring.start()
    read.wait()
    swap.wait()
    few[...] = few_both[...]
    gain = norm_gain_of(few_both, 0, lead)
    for half in range(2):
        value = raw[half].astype(F32)
        normed[half] = (value * norm_scale(value) * gain).astype(BF16)
    x_ring = RingGather(x, at_x, lambda half: normed.at[half], lambda origin, half: rows.at[origin, half], (xs, xr, xl))
    x_ring.start()
    z_ring.relay()
    z_ring.wait(2, 3, 4, 5)
    z_ring.finish()
    y_ring = WeightGather(lambda half: spread_weights.at[half], weights, (ys, yr, yl), (cs, cr))
    y_ring.start()
    x_ring.relay()
    y_ring.relay()
    y_ring.finish()
    x_ring.wait(2, 3, 4, 5)
    x_ring.finish()


def remote_params(collective_id):
    return pltpu.CompilerParams(
        collective_id=collective_id, has_side_effects=True, vmem_limit_bytes=56 * 2**20
    )


def open_call(inputs, shard, few):
    _, part, width = inputs.shape
    rows, columns = shard.shape
    lead = few.shape[1] - (width - few.shape[1])
    inputs = inputs.reshape(2, 2, part // 2, width)
    got, spread_weights, weights, few = pl.pallas_call(
        partial(open_kernel, lead),
        out_shape=[
            jax.ShapeDtypeStruct((4, 2, part // 2, width), BF16),
            jax.ShapeDtypeStruct((4, 2, rows // 2, columns), BF16),
            jax.ShapeDtypeStruct((2, 4, 2, 2, rows // 2, columns), BF16),
            jax.ShapeDtypeStruct((2,) + few.shape, F32),
        ],
        in_specs=[ANY, ANY, VMEM],
        out_specs=[ANY, ANY, ANY, VMEM],
        scratch_shapes=[
            pltpu.VMEM((2, part // 2, width), BF16),
            pltpu.VMEM((2, part // 2, width), BF16),
            pltpu.VMEM((2,) + few.shape, F32),
        ]
        + gather_sems() * 3 + dma(8) + dma(1) + [pltpu.SemaphoreType.DMA((1,))],
        compiler_params=remote_params(0),
        name="gather_first",
    )(inputs, shard.reshape(2, rows // 2, columns), few)
    return got.reshape(4 * part, width), spread_weights, weights.reshape(16 * rows, columns), few


def scale_rows(squares, arrived, me, inner):
    total = squares[me, 0:1, :]
    for step in (1, 2, 3):
        total = total + arrived[(me + step) % 4, 0:1, :]
    return lax.rsqrt(total / inner + EPS)


def middle_kernel(inner, lead, part, squares, inputs, few, spread_weights, rows, weights, residual, branch,
                  scales, swapped, raw, normed, low, others, b0, b1, b2, xs, xr, gs, gr, gl,
                  ys, yr, yl, cs, cr, qs, qr, ps, pr, load):
    z, y, core, x = place()
    pipe = z % 2
    read = pltpu.make_async_copy(inputs.at[pipe], raw, load.at[0])
    read.start()
    greet(*around(x, at_x, (1, 2, 3)), *around(y, at_y), at_core(1 - core), at_pipe(1 - pipe))
    sums = RingScatter(x, at_x, part, (b0, b1, b2), (xs, xr))
    sums.start()
    share = Everyone(x, at_x, lambda to: squares.at[to], lambda me: others.at[me], (qs, qr))
    share.start()
    y_ring = WeightGather(lambda half: spread_weights.at[2 + half], weights, (ys, yr, yl), (cs, cr))
    y_ring.start()
    share.wait()
    inverse = scale_rows(squares, others, x, inner)
    scales[...] = jnp.broadcast_to(inverse, scales.shape)
    column = row_to_column(inverse)
    read.wait()
    gain = norm_gain_of(few, 1, lead)
    sums.relay()
    y_ring.relay()
    sums.wait()
    half_rows = part.shape[2]
    for half in range(2):
        here = column[half * half_rows : (half + 1) * half_rows] * sums.result(half)
        branch[half] = here
        value = raw[half].astype(F32) + here
        residual[half] = value
        low[half] = value.astype(BF16)
        normed[half] = (value * norm_scale(value) * gain).astype(BF16)
    x_ring = RingGather(x, at_x, lambda half: normed.at[half], lambda origin, half: rows.at[origin, half], (gs, gr, gl))
    x_ring.start()
    swap = remote(low, swapped, (ps, pr), 0, at_pipe(1 - pipe))
    swap.start()
    y_ring.finish()
    x_ring.relay()
    swap.wait()
    x_ring.wait(2, 3, 4, 5)
    x_ring.finish()
    sums.finish()


def middle_call(part, squares, inputs, few, spread_weights, inner):
    _, rows, width = inputs.shape
    piece, columns = spread_weights.shape[2:]
    lead = few.shape[2] - (width - few.shape[2])
    half = (2, rows // 2, width)
    got, weights, residual, branch, scales, swapped = pl.pallas_call(
        partial(middle_kernel, inner, lead),
        out_shape=[
            jax.ShapeDtypeStruct((4,) + half, BF16),
            jax.ShapeDtypeStruct((2, 4, 2, 2, piece, columns), BF16),
            jax.ShapeDtypeStruct(half, F32),
            jax.ShapeDtypeStruct(half, F32),
            jax.ShapeDtypeStruct((8, rows), F32),
            jax.ShapeDtypeStruct(half, BF16),
        ],
        in_specs=[VMEM, VMEM, ANY, VMEM, ANY],
        out_specs=[ANY, ANY, VMEM, VMEM, VMEM, ANY],
        scratch_shapes=[pltpu.VMEM(half, BF16), pltpu.VMEM(half, BF16), pltpu.VMEM(half, BF16),
                        pltpu.VMEM((4, 8, rows), F32)]
        + scatter_buffers(rows, width)
        + dma(6) + gather_sems() + gather_sems() + dma(8) + dma(3) + dma(1)
        + [pltpu.SemaphoreType.DMA((1,))],
        compiler_params=remote_params(1),
        name="between_layers",
    )(part.reshape((4,) + half), squares, inputs.reshape((2,) + half), few, spread_weights)
    return (got.reshape(4 * rows, width), weights.reshape(-1, columns),
            residual, branch, scales, swapped)


def last_kernel(inner, part, squares, residual, out_grad, output, scales, own, raw, others,
                b0, b1, b2, xs, xr, qs, qr, ds, dr, load):
    z, y, core, x = place()
    pipe = z % 2
    read = pltpu.make_async_copy(out_grad.at[pipe], raw, load.at[0])
    read.start()
    greet(*around(x, at_x, (1, 2, 3)))
    sums = RingScatter(x, at_x, part, (b0, b1, b2), (xs, xr))
    sums.start()
    share = Everyone(x, at_x, lambda to: squares.at[to], lambda me: others.at[me], (qs, qr))
    share.start()
    share.wait()
    inverse = scale_rows(squares, others, x, inner)
    column = row_to_column(inverse)
    read.wait()
    sums.relay()
    sums.wait()
    half_rows = part.shape[2]
    dots = []
    for half in range(2):
        here = column[half * half_rows : (half + 1) * half_rows] * sums.result(half)
        output[half] = residual[half] + here
        dots.append(jnp.sum(raw[half].astype(F32) * here, -1, keepdims=True))
    dots = column_to_row(jnp.concatenate(dots, 0)) / inner
    own[...] = jnp.zeros_like(own)
    own[0:1, :] = inverse
    own[1:2, :] = dots
    tell = Everyone(x, at_x, lambda to: own, lambda me: scales.at[me], (ds, dr))
    tell.start()
    keep = pltpu.make_async_copy(own, scales.at[x], load.at[1])
    keep.start()
    keep.wait()
    tell.wait()
    sums.finish()


def last_call(part, squares, residual, out_grad, inner):
    half = residual.shape
    rows = half[0] * half[1]
    return pl.pallas_call(
        partial(last_kernel, inner),
        out_shape=[jax.ShapeDtypeStruct(half, F32), jax.ShapeDtypeStruct((4, 8, rows), F32)],
        in_specs=[VMEM, VMEM, VMEM, ANY],
        out_specs=[VMEM, ANY],
        scratch_shapes=[pltpu.VMEM((8, rows), F32), pltpu.VMEM(half, BF16), pltpu.VMEM((4, 8, rows), F32)]
        + scatter_buffers(rows, half[2])
        + dma(6) + dma(3) + dma(3) + [pltpu.SemaphoreType.DMA((2,))],
        compiler_params=remote_params(2),
        name="last_output",
    )(part.reshape((4,) + half), squares, residual, out_grad.reshape((2,) + half))


class CoreSum:
    def __init__(self, grads, kept, arrived, total, sems, load):
        _, _, core, _ = place()
        self.kept, self.arrived, self.total = kept, arrived, total
        self.pieces = [(y, half) for y in range(4) for half in range(2)]
        self.copies, self.reads = [], []
        for index, (y, half) in enumerate(self.pieces):
            target = arrived.at[y, half]
            self.copies.append(remote(grads.at[half, y, 1 - core], target, sems, index, at_core(1 - core)))
            self.reads.append(pltpu.make_async_copy(grads.at[half, y, core], kept.at[y, half], load.at[index]))

    def start(self):
        for copy, read in zip(self.copies, self.reads):
            copy.start()
            read.start()

    def finish(self):
        for copy, read, (y, half) in zip(self.copies, self.reads, self.pieces):
            read.wait()
            copy.wait_recv()
            value = self.kept[y, half].astype(F32) + self.arrived[y, half].astype(F32)
            self.total[y, half] = value.astype(BF16)
        for copy in self.copies:
            copy.wait_send()


def core_buffers(rows, columns):
    return [pltpu.VMEM((4, 2, rows, columns), BF16)] * 3


def back_through_norm(value, grad_out, summed, gain):
    scale = norm_scale(value)
    unit = value * scale
    scaled = summed * gain
    mean = jnp.mean(scaled * unit, -1, keepdims=True)
    return grad_out + scale * (scaled - unit * mean), jnp.sum(summed * unit, 0, keepdims=True)


def add_norm_grad(target, source, gain_grad, lead):
    wide = target.shape[1]
    first = wide - lead
    target[...] = source[...]
    target[6:7, lead:] = gain_grad[:, :first]
    target[7:8, :] = gain_grad[:, first:]


def turn_kernel(inner, lead, part, residual, few, out_grad, branch, inverse, output, grads, few_grad,
                errors, scales, input_grad, few_total, swapped_out, swapped_grad, middle,
                raw, own, sent, low_out, low_grad, b0, b1, b2, kept, arrived, total, d0, d1, d2,
                xs, xr, gs, gr, gl, ts, tr, ps, pr, cs, cr, ys, yr, load):
    z, y, core, x = place()
    pipe = z % 2
    read = pltpu.make_async_copy(out_grad.at[pipe], raw, load.at[8])
    read.start()
    low_out[...] = output[...].astype(BF16)
    greet(*around(x, at_x, (1, 2, 3)), *around(y, at_y), at_core(1 - core), at_pipe(1 - pipe))
    sums = RingScatter(x, at_x, part, (b0, b1, b2), (xs, xr))
    sums.start()
    swap_out = remote(low_out, swapped_out, (ps, pr), 0, at_pipe(1 - pipe))
    swap_out.start()
    cores = CoreSum(grads, kept, arrived, total, (cs, cr), load)
    cores.start()
    cores.finish()
    y_sums = RingScatter(y, at_y, total, (d0, d1, d2), (ys, yr))
    y_sums.start()
    read.wait()
    gain = norm_gain_of(few, 1, lead)
    sums.relay()
    y_sums.relay()
    sums.wait()
    gain_grad = jnp.zeros_like(gain)
    dots = []
    for half in range(2):
        value, gain_part = back_through_norm(residual[half], raw[half].astype(F32), sums.result(half), gain)
        gain_grad = gain_grad + gain_part
        input_grad[half] = value
        low = value.astype(BF16)
        sent[half] = low
        dots.append(jnp.sum(low.astype(F32) * branch[half], -1, keepdims=True))
    x_ring = RingGather(x, at_x, lambda half: sent.at[half], lambda origin, half: errors.at[origin, half], (gs, gr, gl))
    x_ring.start()
    swap_grad = remote(sent, swapped_grad, (ps, pr), 1, at_pipe(1 - pipe))
    swap_grad.start()
    own[...] = jnp.zeros_like(own)
    own[0:1, :] = inverse[0:1, :]
    own[1:2, :] = column_to_row(jnp.concatenate(dots, 0)) / inner
    tell = Everyone(x, at_x, lambda to: own, lambda me: scales.at[me], (ts, tr))
    tell.start()
    keep = pltpu.make_async_copy(own, scales.at[x], load.at[9])
    keep.start()
    add_norm_grad(few_total, few_grad, gain_grad, lead)
    y_sums.wait()
    for half in range(2):
        middle[half] = y_sums.result(half).astype(BF16)
    y_sums.finish()
    x_ring.relay()
    swap_out.wait()
    swap_grad.wait()
    keep.wait()
    tell.wait()
    x_ring.wait(2, 3, 4, 5)
    x_ring.finish()
    sums.finish()


def turn_call(part, residual, few, out_grad, branch, inverse, output, grads, few_grad, inner):
    half = residual.shape
    rows, width = half[0] * half[1], half[2]
    lead = few.shape[2] - (width - few.shape[2])
    columns = grads.shape[1]
    piece = grads.shape[0] // 16
    return pl.pallas_call(
        partial(turn_kernel, inner, lead),
        out_shape=[
            jax.ShapeDtypeStruct((4,) + half, BF16),
            jax.ShapeDtypeStruct((4, 8, rows), F32),
            jax.ShapeDtypeStruct(half, F32),
            jax.ShapeDtypeStruct(few_grad.shape, F32),
            jax.ShapeDtypeStruct(half, BF16),
            jax.ShapeDtypeStruct(half, BF16),
            jax.ShapeDtypeStruct((2, piece, columns), BF16),
        ],
        in_specs=[VMEM, VMEM, VMEM, ANY, VMEM, VMEM, VMEM, ANY, VMEM],
        out_specs=[ANY, ANY, VMEM, VMEM, ANY, ANY, VMEM],
        scratch_shapes=[
            pltpu.VMEM(half, BF16),
            pltpu.VMEM((8, rows), F32),
            pltpu.VMEM(half, BF16),
            pltpu.VMEM(half, BF16),
            pltpu.VMEM((8, LANES), BF16),
        ]
        + scatter_buffers(rows, width)
        + core_buffers(piece, columns)
        + scatter_buffers(2 * piece, columns)
        + dma(6) + gather_sems() + dma(3) + dma(2) + dma(8) + dma(6)
        + [pltpu.SemaphoreType.DMA((10,))],
        compiler_params=remote_params(3),
        name="between_gradients",
    )(part.reshape((4,) + half), residual, few, out_grad.reshape((2,) + half), branch, inverse, output,
      grads.reshape(2, 4, 2, piece, columns), few_grad)


def final_kernel(sizes, part, inputs, few, error, grads, middle, few_grad, few_later,
                 input_grad, swapped, large, few_sum, few_shared, state_grad,
                 raw, low, b0, b1, b2, kept, arrived, total, d0, d1, d2, e0, e1, e2, z_blocks,
                 mine, pair, y_few, z_few, x_few, state_parts,
                 xs, xr, ps, pr, cs, cr, ys, yr, zs, zr, fs, fr, hs, hr, js, jr, ks, kr, ws, wr, load):
    lead, state_at, state_columns = sizes
    z, y, core, x = place()
    pipe = z % 2
    every = (1, 2, 3)
    read = pltpu.make_async_copy(inputs.at[pipe], raw, load.at[8])
    read.start()
    greet(*around(x, at_x, every), *around(y, at_y, every), *around(z, at_z, every), at_core(1 - core),
          at_pipe(1 - pipe))
    sums = RingScatter(x, at_x, part, (b0, b1, b2), (xs, xr))
    sums.start()
    cores = CoreSum(grads, kept, arrived, total, (cs, cr), load)
    cores.start()
    cores.finish()
    y_sums = RingScatter(y, at_y, total, (d0, d1, d2), (ys, yr))
    y_sums.start()
    read.wait()
    gain = norm_gain_of(few, 0, lead)
    sums.relay()
    y_sums.relay()
    sums.wait()
    gain_grad = jnp.zeros_like(gain)
    for half in range(2):
        value, gain_part = back_through_norm(raw[half].astype(F32), error[half], sums.result(half), gain)
        gain_grad = gain_grad + gain_part
        input_grad[half] = value
        low[half] = value.astype(BF16)
    swap = remote(low, swapped, (ps, pr), 0, at_pipe(1 - pipe))
    swap.start()
    mine[1] = few_later[...]
    add_norm_grad(mine.at[0], few_grad, gain_grad, lead)
    few_core = remote(mine, pair, (fs, fr), 0, at_core(1 - core))
    few_core.start()
    few_core.wait()
    mine[...] = mine[...] + pair[...]
    few_y = Everyone(y, at_y, lambda to: mine, lambda me: y_few.at[me], (hs, hr))
    few_y.start()
    y_sums.wait()
    rows = z_blocks.shape[2]
    for z_hi in range(2):
        first = y_sums.result(z_hi).astype(BF16)
        second = middle[z_hi]
        for half in range(2):
            z_blocks[2 * z_hi, half] = first[half * rows : (half + 1) * rows]
            z_blocks[2 * z_hi + 1, half] = second[half * rows : (half + 1) * rows]
    y_sums.finish()
    z_sums = RingScatter(z, at_z, z_blocks, (e0, e1, e2), (zs, zr))
    z_sums.start()
    few_y.wait()
    y_few[y] = mine[...]
    mine[...] = (y_few[0] + y_few[1]) + (y_few[2] + y_few[3])
    few_z = Everyone(z, at_z, lambda to: mine.at[to % 2], lambda me: z_few.at[me], (js, jr))
    few_z.start()
    z_sums.relay()
    few_z.wait()
    z_few[z] = mine[pipe]
    few_sum[...] = (z_few[0] + z_few[1]) + (z_few[2] + z_few[3])
    x_few[x] = few_sum[...]
    few_x = Everyone(x, at_x, lambda to: few_sum, lambda me: x_few.at[me], (ks, kr))
    few_x.start()
    z_sums.wait()
    for half in range(2):
        large[half * rows : (half + 1) * rows, :] = z_sums.result(half)
    z_sums.finish()
    quarter = 2 * rows // 4
    columns = pl.ds(state_at, state_columns)
    for block in range(4):
        state_parts[0, block] = large[block * quarter : (block + 1) * quarter, state_at : state_at + state_columns]
    state_x = Everyone(x, at_x, lambda to: state_parts.at[0, to], lambda me: state_parts.at[1, me], (ws, wr))
    state_x.start()
    few_x.wait()
    few_shared[...] = (x_few[0] + x_few[1]) + (x_few[2] + x_few[3])
    state_x.wait()
    total_state = state_parts[0, x]
    for step in every:
        total_state = total_state + state_parts[1, (x + step) % 4]
    state_grad[...] = total_state
    swap.wait()
    sums.finish()


def final_call(part, inputs, few, error, grads, middle, few_grad, few_later, sizes):
    half = error.shape
    rows, width = half[0] * half[1], half[2]
    wide = few.shape[2]
    lead = wide - (width - wide)
    columns = grads.shape[1]
    piece = grads.shape[0] // 16
    state_at, state_columns = sizes
    both = (2,) + few_grad.shape
    return pl.pallas_call(
        partial(final_kernel, (lead, state_at, state_columns)),
        out_shape=[
            jax.ShapeDtypeStruct(half, F32),
            jax.ShapeDtypeStruct(half, BF16),
            jax.ShapeDtypeStruct((piece, columns), F32),
            jax.ShapeDtypeStruct(few_grad.shape, F32),
            jax.ShapeDtypeStruct(few_grad.shape, F32),
            jax.ShapeDtypeStruct((piece // 4, state_columns), F32),
        ],
        in_specs=[VMEM, ANY, VMEM, VMEM, ANY, VMEM, VMEM, VMEM],
        out_specs=[VMEM, ANY, VMEM, VMEM, VMEM, VMEM],
        scratch_shapes=[pltpu.VMEM(half, BF16), pltpu.VMEM(half, BF16)]
        + scatter_buffers(rows, width)
        + core_buffers(piece, columns)
        + scatter_buffers(2 * piece, columns)
        + scatter_buffers(piece, columns)
        + [
            pltpu.VMEM((4, 2, piece // 2, columns), BF16),
            pltpu.VMEM(both, F32),
            pltpu.VMEM(both, F32),
            pltpu.VMEM((4,) + both, F32),
            pltpu.VMEM((4,) + few_grad.shape, F32),
            pltpu.VMEM((4,) + few_grad.shape, F32),
            pltpu.VMEM((2, 4, piece // 4, state_columns), F32),
        ]
        + dma(6) + dma(1) + dma(8) + dma(6) + dma(6) + dma(1) + dma(3) + dma(3) + dma(3) + dma(3)
        + [pltpu.SemaphoreType.DMA((9,))],
        compiler_params=remote_params(4),
        name="final_sums",
    )(part.reshape((4,) + half), inputs.reshape((2,) + half), few, error,
      grads.reshape(2, 4, 2, piece, columns), middle, few_grad, few_later)


def body(inputs, out_grad, norm_gain, in_gate_x, in_read_write, in_step, conv_main, conv_state,
         step_bias, log_rate, skip_gain, gate_gain, out_weight):
    _, part, width = inputs.shape
    inner = out_weight.shape[2]
    pair = in_read_write.shape[2]
    heads = step_bias.shape[1]
    whole_inner = inner * lax.axis_size("tensor")
    split = 2 * inner + pair
    wide = inner + pair
    pipe = lax.axis_index("pipe")
    first = pipe == 0
    shard = jnp.concatenate(
        [
            in_gate_x[0, :, 0],
            in_gate_x[0, :, 1],
            in_read_write[0],
            jnp.pad(in_step[0], ((0, 0), (0, LANES - heads))),
            out_weight[0],
        ],
        1,
    )
    rate = -jnp.exp(log_rate[0])
    pad = ((0, 0), (0, LANES - heads))
    skip = jnp.broadcast_to(skip_gain[0][:, None], (heads, inner // heads)).reshape(1, inner)
    few = jnp.concatenate(
        [
            jnp.concatenate([conv_main[0], conv_state[0]], 1),
            jnp.concatenate([gate_gain, jnp.pad(step_bias, pad), jnp.pad(rate[None], pad)], 1),
            jnp.concatenate([skip, norm_gain], 1).reshape(2, wide),
        ],
        0,
    )
    rows0, spread_weights, w0, few = open_call(inputs, shard, few)
    mine = lax.dynamic_index_in_dim(out_grad, pipe, 0, False)
    mine, w0 = lax.optimization_barrier((mine, w0))
    errors1 = lax.all_gather(mine, "tensor", axis=0, tiled=True)
    part0, squares0, *saved0 = forward_call(0, rows0, w0, few, inner, pair, heads)
    rows1, w1, residual, branch0, inverse0, swapped0 = middle_call(
        part0, squares0, inputs, few, spread_weights, whole_inner
    )
    part1, squares1, *saved1 = forward_call(1, rows1, w1, few, inner, pair, heads)
    output, scales1 = last_call(part1, squares1, residual, out_grad, whole_inner)
    part1, grad1, mixed1, few_grad1 = backward_call(
        1, errors1, scales1, w1, few, saved1, inner, pair, heads
    )
    large1 = weight_call(rows1, grad1, errors1, mixed1)
    errors0, scales0, input_grad1, few_grad1, swapped1, swapped_grad1, middle = turn_call(
        part1, residual, few, out_grad, branch0, inverse0, output, large1, few_grad1, whole_inner
    )
    errors0 = errors0.reshape(4 * part, width)
    part0, grad0, mixed0, few_grad0 = backward_call(
        0, errors0, scales0, w0, few, saved0, inner, pair, heads
    )
    large0 = weight_call(rows0, grad0, errors0, mixed0)
    input_grad0, swapped_grad0, large, few_sum, few_shared, state_grad = final_call(
        part0, inputs, few, input_grad1, large0, middle, few_grad0, few_grad1, (2 * inner, pair)
    )

    def by_layer(zero, one, from_zero, from_one):
        own = jnp.where(first, zero, one).reshape(part, width)
        other = jnp.where(first, from_zero, from_one).reshape(part, width).astype(F32)
        return jnp.where(first, jnp.stack([own, other]), jnp.stack([other, own]))[None]

    activations = by_layer(residual, output, swapped0, swapped1)
    input_grads = by_layer(input_grad0, input_grad1, swapped_grad0, swapped_grad1)
    rates = few_sum[5, inner + LANES : inner + LANES + heads] * rate
    return (
        activations,
        input_grads,
        few_shared[6:].reshape(1, 2 * wide)[:, inner:],
        large[:, : 2 * inner].reshape(1, -1, 2, inner),
        state_grad[None],
        large[None, :, split : split + heads],
        few_sum[None, :5, :inner],
        few_shared[None, :5, inner:],
        few_sum[5:6, inner : inner + heads],
        rates[None],
        few_sum[6, :inner].reshape(1, heads, -1).sum(2),
        few_sum[5:6, :inner],
        large[None, :, split + LANES :],
    )


def solution(mesh):
    in_specs = (
        P("dp", "tensor", None),
        P("dp", "tensor", None),
        P("pipe", None),
        P("pipe", "dp", None, "tensor"),
        P("pipe", "dp", None),
        P("pipe", "dp", "tensor"),
        P("pipe", None, "tensor"),
        P("pipe", None, None),
        P("pipe", "tensor"),
        P("pipe", "tensor"),
        P("pipe", "tensor"),
        P("pipe", "tensor"),
        P("pipe", "dp", "tensor"),
    )
    out_specs = (
        P("pipe", "dp", "tensor", None),
        P("pipe", "dp", "tensor", None),
        P("pipe", None),
        P("pipe", "dp", None, "tensor"),
        P("pipe", ("dp", "tensor"), None),
        P("pipe", "dp", "tensor"),
        P("pipe", None, "tensor"),
        P("pipe", None, None),
        P("pipe", "tensor"),
        P("pipe", "tensor"),
        P("pipe", "tensor"),
        P("pipe", "tensor"),
        P("pipe", "dp", "tensor"),
    )
    return jax.shard_map(body, mesh=mesh, in_specs=in_specs, out_specs=out_specs, check_vma=False)
```

```python
from functools import partial

import jax
import jax.numpy as jnp
import numpy as np
from jax import lax
from jax.experimental import pallas as pl
from jax.experimental.pallas import tpu as pltpu
from jax.sharding import PartitionSpec as P

F32, BF16 = jnp.float32, jnp.bfloat16
EPS = 1e-05
ROWS = 256
CHUNK = 128
LANES = 128
EXACT = lax.Precision.HIGHEST


def mm(left, right, contract=((1,), (0,))):
    return lax.dot_general(left, right, (contract, ((), ())), preferred_element_type=F32)


def mm_exact(left, right, contract=((1,), (0,))):
    return lax.dot_general(
        left, right, (contract, ((), ())), precision=EXACT, preferred_element_type=F32
    )


def spread(value, selector, heads):
    high = value.astype(BF16).astype(F32)
    both = high + pltpu.roll(value - high, heads, 1)
    return mm(both.astype(BF16), selector)


def per_head(value, collector):
    high = value.astype(BF16)
    low = (value - high.astype(F32)).astype(BF16)
    return mm(high, collector) + mm(low, collector)


def softplus(value):
    small = jnp.exp(-jnp.abs(value))
    series = small * (1.0 - small * (0.5 - small * (1.0 / 3.0 - small * 0.25)))
    return jnp.maximum(value, 0.0) + jnp.where(small < 0.01, series, jnp.log(1.0 + small))


def sigmoid(value):
    return 1.0 / (1.0 + jnp.exp(-value))


def iota(shape, axis):
    return lax.broadcasted_iota(jnp.int32, shape, axis)


def column_to_row(column):
    size = column.shape[0]
    same = iota((size, size), 0) == iota((size, size), 1)
    return jnp.sum(jnp.where(same, column, 0.0), 0, keepdims=True)


def row_to_column(row):
    size = row.shape[1]
    same = iota((size, size), 0) == iota((size, size), 1)
    return jnp.sum(jnp.where(same, row, 0.0), 1, keepdims=True)


def steps(raw, bias, rate, mask):
    delta = softplus(raw + bias) * mask
    tri = (iota((CHUNK, CHUNK), 0) >= iota((CHUNK, CHUNK), 1)).astype(F32)
    log_decay = mm_exact(tri, delta * rate)
    return delta, log_decay


def backward_kernel(sizes, e_ref, scales_ref, w_ref, few_ref, selector_ref,
                    collector_ref, saved_ref, s_ref,
                    part_ref, grad_ref, mixed_ref, few_out, state, later, pad):
    inner, pair, heads = sizes
    states = pair // 2
    split = inner + inner + pair
    conv = inner + pair
    (z_at, p_at, c_at, raw_at, y_at), _ = columns_of(inner, conv)

    @pl.when(pl.program_id(0) == 0)
    def _():
        state[...] = jnp.zeros_like(state)
        later[...] = jnp.zeros_like(later)
        pad[ROWS : ROWS + 8, :] = jnp.zeros((8, conv), F32)
        few_out[...] = jnp.zeros_like(few_out)

    @pl.when(pl.program_id(0) > 0)
    def _():
        pad[ROWS : ROWS + 8, :] = pad[0:8, :]

    selector = selector_ref[...]
    collector = collector_ref[...]
    bias = few_ref[0, 5:6, inner : inner + LANES]
    rate = few_ref[0, 5:6, inner + LANES : inner + 2 * LANES]
    gain = few_ref[0, 5:6, :inner]
    skip = few_ref[0, 6:7, :inner]
    mask = (iota((1, LANES), 1) < heads).astype(F32)
    first = iota((CHUNK, LANES), 1) < LANES // 2
    later_in = iota((CHUNK, CHUNK), 1) >= iota((CHUNK, CHUNK), 0)
    last = iota((CHUNK, LANES), 0) == CHUNK - 1
    quarter = ROWS // 4
    column = lambda row: jnp.concatenate(
        [row_to_column(scales_ref[0, owner, row : row + 1, :])[:quarter] for owner in range(4)], 0
    )
    inverse = column(0)
    inner_dot = column(1)
    mixed_grad = mm(e_ref[...], w_ref[0, :, split + LANES :])
    for chunk in reversed(range(ROWS // CHUNK)):
        at = slice(chunk * CHUNK, (chunk + 1) * CHUNK)
        z = saved_ref[0, at, z_at]
        y = saved_ref[0, at, y_at]
        sig = sigmoid(z)
        act = z * sig
        g = y * act * inverse[at]
        mixed_ref[at, :] = (g * gain).astype(BF16)
        mixed_here = mixed_grad[at]
        gated_grad = inverse[at] * (mixed_here * gain - g * inner_dot[at])
        dy = gated_grad * act
        grad_ref[at, :inner] = (gated_grad * y * (sig * (1.0 + z - act))).astype(BF16)
        c = saved_ref[0, at, c_at]
        csig = sigmoid(c)
        value = c * csig
        slope = csig * (1.0 + c - value)
        xs = value[:, :inner]
        b_low = value[:, inner : inner + states].astype(BF16)
        c_low = value[:, inner + states :].astype(BF16)
        raw = saved_ref[0, at, raw_at]
        delta, log_decay = steps(raw, bias, rate, mask)
        turned = log_decay.T
        final = log_decay[CHUNK - 1 : CHUNK, :]
        wide_delta = spread(delta, selector, heads)
        scaled = wide_delta * xs
        scaled_low = scaled.astype(BF16)
        dy_low = dy.astype(BF16)
        products = jnp.where(later_in, mm(b_low, c_low, ((1,), (1,))), 0.0)
        dproducts = jnp.zeros((CHUNK, CHUNK), F32)
        within = []
        for two in range(heads // 2):
            lanes = slice(two * LANES, (two + 1) * LANES)
            parts = []
            for odd in range(2):
                h = 2 * two + odd
                mine = first if odd == 0 else ~first
                decay = jnp.exp(jnp.minimum(turned[h : h + 1, :] - log_decay[:, h : h + 1], 0.0))
                parts.append(mm((products * decay).astype(BF16), dy_low[:, lanes]))
                own = jnp.where(mine, scaled_low[:, lanes], jnp.zeros((), BF16))
                dproducts = dproducts + decay * mm(own, dy_low[:, lanes], ((1,), (1,)))
            within.append(jnp.where(first, parts[0], parts[1]))
        dproducts = jnp.where(later_in, dproducts, 0.0).astype(BF16)
        old = s_ref[0, chunk]
        old_low = old.astype(BF16)
        dstate = state[...]
        dstate_low = dstate.astype(BF16)
        to_end = spread(jnp.exp(final - log_decay) * mask, selector, heads)
        from_start = (spread(jnp.exp(log_decay) * mask, selector, heads) * dy).astype(BF16)
        dscaled = jnp.concatenate(within, 1) + to_end * mm(b_low, dstate_low)
        dc_state = mm(from_start, old_low, ((1,), (1,))) + mm(dproducts, b_low, ((0,), (0,)))
        db_state = mm((to_end * scaled).astype(BF16), dstate_low, ((1,), (1,))) + mm(dproducts, c_low)
        carry = jnp.broadcast_to(jnp.sum(later[...] * dstate, 0, keepdims=True), (8, inner))
        carry = per_head(carry, collector)[0:1]
        keep = spread(jnp.broadcast_to(jnp.exp(final) * mask, (8, LANES)), selector, heads)[0:1]
        state[...] = keep * dstate + mm(c_low, from_start, ((0,), (0,)))
        later[...] = old
        flow = dy_low.astype(F32) * (y - skip * xs) - scaled_low.astype(F32) * dscaled
        dlog = per_head(flow, collector) + jnp.where(last, carry, 0.0)
        tri = (iota((CHUNK, CHUNK), 1) >= iota((CHUNK, CHUNK), 0)).astype(F32)
        dstep = mm_exact(tri, dlog)
        ddelta = per_head(xs * dscaled, collector) + rate * dstep
        draw = ddelta * sigmoid(raw + bias) * mask
        few_out[5:6, inner : inner + LANES] += jnp.sum(draw, 0, keepdims=True)
        few_out[5:6, inner + LANES : inner + 2 * LANES] += jnp.sum(delta * dstep, 0, keepdims=True)
        few_out[5:6, :inner] += jnp.sum(mixed_here * g, 0, keepdims=True)
        few_out[6:7, :inner] += jnp.sum(dy * xs, 0, keepdims=True)
        dxs = wide_delta * dscaled + skip * dy
        pad[at, :] = jnp.concatenate([dxs, db_state, dc_state], 1) * slope
        grad_ref[at, split:] = draw.astype(BF16)
    for chunk in range(ROWS // CHUNK):
        at = slice(chunk * CHUNK, (chunk + 1) * CHUNK)
        p = saved_ref[0, at, p_at]
        total = jnp.zeros((CHUNK, conv), F32)
        for tap in range(4):
            begin = chunk * CHUNK + 3 - tap
            shifted = pad[begin : begin + CHUNK, :]
            total = total + few_ref[0, tap : tap + 1, :] * shifted
            few_out[tap : tap + 1, :] += jnp.sum(p * shifted, 0, keepdims=True)
        few_out[4:5, :] += jnp.sum(pad[at, :], 0, keepdims=True)
        grad_ref[at, inner:split] = total.astype(BF16)
    part_ref[...] = mm(grad_ref[...], w_ref[0, :, : split + LANES], ((1,), (1,))).astype(part_ref.dtype)


def constants(inner, heads):
    width = inner // heads
    lane = np.arange(LANES)[:, None]
    channel = np.arange(inner)[None, :] // width
    selector = ((lane % heads == channel) & (lane < 2 * heads)).astype(np.float32)
    collector = (lane == channel).astype(np.float32).T
    return jnp.asarray(selector, BF16), jnp.asarray(collector, BF16)


def whole(array):
    return pl.BlockSpec(array.shape, lambda i: (0,) * array.ndim)


def backward_call(layer, e, scales, w, few, saved, states, inner, pair, heads):
    length, width = e.shape
    count = length // ROWS
    conv = inner + pair
    split = inner + conv
    selector, collector = constants(inner, heads)
    by_rows = lambda columns: pl.BlockSpec((ROWS, columns), lambda i: (count - 1 - i, 0))
    of_layer = lambda array: pl.BlockSpec((1,) + array.shape[1:], lambda i: (layer, 0, 0))
    chunks = ROWS // CHUNK
    out = lambda columns, kind=F32: jax.ShapeDtypeStruct((length, columns), kind)
    return pl.pallas_call(
        partial(backward_kernel, (inner, pair, heads)),
        grid=(count,),
        in_specs=[
            by_rows(width),
            pl.BlockSpec((1,) + scales.shape[1:], lambda i: (count - 1 - i, 0, 0, 0)),
            of_layer(w),
            of_layer(few),
            whole(selector),
            whole(collector),
            pl.BlockSpec((1, ROWS, saved.shape[2]), lambda i: (layer, count - 1 - i, 0)),
            pl.BlockSpec((1, chunks) + states.shape[2:], lambda i: (layer, count - 1 - i, 0, 0)),
        ],
        out_specs=[
            by_rows(width),
            by_rows(split + LANES),
            by_rows(inner),
            pl.BlockSpec((8, conv), lambda i: (0, 0)),
        ],
        out_shape=[
            out(width, BF16),
            out(split + LANES, BF16),
            out(inner, BF16),
            jax.ShapeDtypeStruct((8, conv), F32),
        ],
        scratch_shapes=[
            pltpu.VMEM((pair // 2, inner), F32),
            pltpu.VMEM((pair // 2, inner), F32),
            pltpu.VMEM((ROWS + 8, conv), F32),
        ],
        compiler_params=pltpu.CompilerParams(vmem_limit_bytes=56 * 2**20),
        name="layer_backward",
    )(e, scales, w, few, selector, collector, saved, states)


def weight_kernel(rows_ref, grad_ref, errors_ref, mixed_ref, out_ref):
    columns = grad_ref.shape[1]
    turn = ((0,), (0,))
    out_ref[:, :columns] = mm(rows_ref[0], grad_ref[...], turn).astype(out_ref.dtype)
    out_ref[:, columns:] = mm(errors_ref[...], mixed_ref[...], turn).astype(out_ref.dtype)


def weight_call(layer, normed, grad, errors, mixed):
    length, width = errors.shape
    columns = grad.shape[1] + mixed.shape[1]
    return pl.pallas_call(
        weight_kernel,
        grid=(width // ROWS,),
        in_specs=[
            pl.BlockSpec((1, length, ROWS), lambda i: (layer, 0, i)),
            whole(grad),
            pl.BlockSpec((length, ROWS), lambda i: (0, i)),
            whole(mixed),
        ],
        out_specs=pl.BlockSpec((ROWS, columns), lambda i: (i, 0)),
        out_shape=jax.ShapeDtypeStruct((width, columns), BF16),
        compiler_params=pltpu.CompilerParams(vmem_limit_bytes=56 * 2**20),
        name="weight_gradients",
    )(normed, grad, errors, mixed)


MESH = pl.DeviceIdType.MESH
ANY = pl.BlockSpec(memory_space=pl.ANY)
VMEM = pl.BlockSpec(memory_space=pltpu.VMEM)


def place():
    pipe, dp, x = lax.axis_index("pipe"), lax.axis_index("dp"), lax.axis_index("tensor")
    return (dp // 8) * 2 + pipe, (dp // 2) % 4, dp % 2, x


def at_z(z):
    _, y, core, _ = place()
    return {"pipe": z % 2, "dp": ((z // 2) * 4 + y) * 2 + core}


def at_y(y):
    z, _, core, _ = place()
    return {"dp": ((z // 2) * 4 + y) * 2 + core}


def at_core(core):
    z, y, _, _ = place()
    return {"dp": ((z // 2) * 4 + y) * 2 + core}


def at_x(x):
    return {"tensor": x}


def at_pipe(pipe):
    return {"pipe": pipe}


def greet(*devices):
    barrier = pltpu.get_barrier_semaphore()
    for device in devices:
        pl.semaphore_signal(barrier, inc=1, device_id=device, device_id_type=MESH)
    pl.semaphore_wait(barrier, len(devices))


def around(me, device, steps=(1, 3)):
    return [device((me + step) % 4) for step in steps]


def remote(source, target, sems, index, device):
    return pltpu.make_async_remote_copy(
        src_ref=source,
        dst_ref=target,
        send_sem=sems[0].at[index],
        recv_sem=sems[1].at[index],
        device_id=device,
        device_id_type=MESH,
    )


class RingGather:
    def __init__(self, me, device, own, slot, sems, local=True):
        right, left, across = (me + 1) % 4, (me + 3) % 4, (me + 2) % 4
        to_right, to_left = device(right), device(left)
        self.copies = [
            remote(own(0), slot(me, 0), sems, 0, to_right),
            remote(own(1), slot(me, 1), sems, 1, to_left),
            remote(own(1), slot(me, 1), sems, 2, to_right),
            remote(own(0), slot(me, 0), sems, 3, to_left),
            remote(slot(left, 0), slot(left, 0), sems, 4, to_right),
            remote(slot(right, 1), slot(right, 1), sems, 5, to_left),
        ]
        self.origins = [(left, 0), (right, 1), (left, 1), (right, 0), (across, 0), (across, 1)]
        self.local = [
            pltpu.make_async_copy(own(half), slot(me, half), sems[2].at[half]) for half in range(2 * local)
        ]

    def start(self):
        for copy in self.copies[:4]:
            copy.start()
        for copy in self.local:
            copy.start()

    def relay(self):
        for index in range(2):
            self.copies[index].wait_recv()
            self.copies[4 + index].start()

    def wait(self, *indices):
        for index in indices:
            self.copies[index].wait_recv()

    def finish(self):
        for copy in self.local:
            copy.wait()
        for copy in self.copies:
            copy.wait_send()


class RingScatter:
    def __init__(self, me, device, piece, buffers, sems):
        self.me, self.right, self.left = me, (me + 1) % 4, (me + 3) % 4
        across = (me + 2) % 4
        self.piece, self.buffers = piece, buffers
        relays, sums, arrived = buffers
        to_right, to_left = device(self.right), device(self.left)
        self.copies = [
            remote(piece(across, 0), relays.at[0], sems, 0, to_right),
            remote(piece(across, 1), relays.at[1], sems, 1, to_left),
            remote(piece(self.right, 1), arrived.at[0, 1], sems, 2, to_right),
            remote(piece(self.left, 0), arrived.at[1, 0], sems, 3, to_left),
            remote(sums.at[0], arrived.at[0, 0], sems, 4, to_right),
            remote(sums.at[1], arrived.at[1, 1], sems, 5, to_left),
        ]

    def start(self):
        for copy in self.copies[:4]:
            copy.start()

    def relay(self):
        relays, sums, _ = self.buffers
        for half, block in ((0, self.right), (1, self.left)):
            self.copies[half].wait_recv()
            total = relays[half].astype(F32) + self.piece(block, half)[...].astype(F32)
            sums[half] = total.astype(sums.dtype)
            self.copies[4 + half].start()

    def wait(self):
        for index in range(2, 6):
            self.copies[index].wait_recv()

    def result(self, half):
        arrived = self.buffers[2]
        mine = self.piece(self.me, half)[...].astype(F32)
        return mine + arrived[0, half].astype(F32) + arrived[1, half].astype(F32)

    def finish(self):
        for copy in self.copies:
            copy.wait_send()


class Everyone:
    def __init__(self, me, device, source, target, sems):
        self.copies = [
            remote(source((me + step) % 4), target(me), sems, step - 1, device((me + step) % 4))
            for step in (1, 2, 3)
        ]

    def start(self):
        for copy in self.copies:
            copy.start()

    def wait(self):
        for copy in self.copies:
            copy.wait()


def dma(count):
    return [pltpu.SemaphoreType.DMA((count,)), pltpu.SemaphoreType.DMA((count,))]


def gather_sems():
    return dma(6) + [pltpu.SemaphoreType.DMA((2,))]


def scatter_buffers(*half):
    return [pltpu.VMEM((2,) + half, BF16), pltpu.VMEM((2,) + half, BF16), pltpu.VMEM((2, 2) + half, BF16)]


def norm_scale(value):
    return lax.rsqrt(jnp.mean(value * value, -1, keepdims=True) + EPS)


def norm_gain_of(few, layer, lead):
    return jnp.concatenate([few[layer, 6:7, lead:], few[layer, 7:8, :]], 1)


def remote_params(collective_id):
    return pltpu.CompilerParams(
        collective_id=collective_id, has_side_effects=True, vmem_limit_bytes=56 * 2**20
    )


class CoreSum:
    def __init__(self, grads, kept, arrived, total, sems, load):
        _, _, core, _ = place()
        self.kept, self.arrived, self.total = kept, arrived, total
        self.pieces = [(y, half) for y in range(4) for half in range(2)]
        self.copies, self.reads = [], []
        for index, (y, half) in enumerate(self.pieces):
            target = arrived.at[y, half]
            self.copies.append(remote(grads.at[half, y, 1 - core], target, sems, index, at_core(1 - core)))
            self.reads.append(pltpu.make_async_copy(grads.at[half, y, core], kept.at[y, half], load.at[index]))

    def start(self):
        for copy, read in zip(self.copies, self.reads):
            copy.start()
            read.start()

    def finish(self):
        for copy, read, (y, half) in zip(self.copies, self.reads, self.pieces):
            read.wait()
            copy.wait_recv()
            value = self.kept[y, half].astype(F32) + self.arrived[y, half].astype(F32)
            self.total[y, half] = value.astype(BF16)
        for copy in self.copies:
            copy.wait_send()


def core_buffers(rows, columns):
    return [pltpu.VMEM((4, 2, rows, columns), BF16)] * 3


def back_through_norm(value, grad_out, summed, gain):
    scale = norm_scale(value)
    unit = value * scale
    scaled = summed * gain
    mean = jnp.mean(scaled * unit, -1, keepdims=True)
    return grad_out + scale * (scaled - unit * mean), jnp.sum(summed * unit, 0, keepdims=True)


def add_norm_grad(target, source, gain_grad, lead):
    wide = target.shape[1]
    first = wide - lead
    target[...] = source[...]
    target[6:7, lead:] = gain_grad[:, :first]
    target[7:8, :] = gain_grad[:, first:]


def owned(block, x, rows):
    return pl.ds(pl.multiple_of(block * ROWS + x * rows, rows), rows)


class BlockSums:
    def __init__(self, x, piece, relays, sums, arrived, sems, op):
        self.right, self.left, self.me = (x + 1) % 4, (x + 3) % 4, x
        across = (x + 2) % 4
        self.piece, self.relays, self.sums, self.arrived = piece, relays, sums, arrived
        at_op = [sem.at[op] for sem in sems]
        to_right, to_left = at_x(self.right), at_x(self.left)
        self.copies = [
            remote(piece(across, 0), relays.at[op, 0], at_op, 0, to_right),
            remote(piece(across, 1), relays.at[op, 1], at_op, 1, to_left),
            remote(piece(self.right, 1), arrived.at[op, 0, 1], at_op, 2, to_right),
            remote(piece(self.left, 0), arrived.at[op, 1, 0], at_op, 3, to_left),
            remote(sums.at[op, 0], arrived.at[op, 0, 0], at_op, 4, to_right),
            remote(sums.at[op, 1], arrived.at[op, 1, 1], at_op, 5, to_left),
        ]
        self.op = op

    def start(self):
        for copy in self.copies[:4]:
            copy.start()

    def relay(self):
        for half, block in ((0, self.right), (1, self.left)):
            self.copies[half].wait_recv()
            total = self.relays[self.op, half].astype(F32) + self.piece(block, half)[...].astype(F32)
            self.sums[self.op, half] = total.astype(BF16)
            self.copies[4 + half].start()

    def wait(self):
        for index in range(2, 6):
            self.copies[index].wait_recv()

    def result(self):
        return jnp.concatenate(
            [
                self.piece(self.me, half)[...].astype(F32)
                + self.arrived[self.op, 0, half].astype(F32)
                + self.arrived[self.op, 1, half].astype(F32)
                for half in range(2)
            ],
            0,
        )

    def finish(self):
        for copy in self.copies:
            copy.wait_send()


def to_everyone(me, device, source, target, sems, op):
    at_op = [sem.at[op] for sem in sems]
    return Everyone(me, device, source, target, at_op)


def columns_of(inner, conv):
    ends = np.cumsum([0, inner, conv, conv, LANES, inner])
    return [slice(int(begin), int(end)) for begin, end in zip(ends[:-1], ends[1:])], int(ends[-1])


def forward_block(sizes, first_block, rows, w, few, selector, save, states, part, squares, state, pad):
    inner, pair, heads = sizes
    states_count = pair // 2
    split = inner + inner + pair
    conv = inner + pair
    (z_at, p_at, c_at, raw_at, y_at), _ = columns_of(inner, conv)

    @pl.when(first_block)
    def _():
        state[...] = jnp.zeros_like(state)
        pad[0:8, :] = jnp.zeros((8, conv), F32)

    @pl.when(jnp.logical_not(first_block))
    def _():
        pad[0:8, :] = pad[ROWS : ROWS + 8, :]

    projected = mm(rows, w[:, : split + LANES])
    save[:, z_at] = projected[:, :inner]
    save[:, p_at] = projected[:, inner:split]
    pad[8 : ROWS + 8, :] = projected[:, inner:split]
    save[:, raw_at] = projected[:, split:]
    bias = few[5:6, inner : inner + LANES]
    rate = few[5:6, inner + LANES : inner + 2 * LANES]
    gain = few[5:6, :inner]
    skip = few[6:7, :inner]
    mask = (iota((1, LANES), 1) < heads).astype(F32)
    first = iota((CHUNK, LANES), 1) < LANES // 2
    causal = iota((CHUNK, CHUNK), 0) >= iota((CHUNK, CHUNK), 1)
    owner_rows = ROWS // 4
    for chunk in range(ROWS // CHUNK):
        at = slice(chunk * CHUNK, (chunk + 1) * CHUNK)
        c = jnp.broadcast_to(few[4:5, :], (CHUNK, conv))
        for tap in range(4):
            begin = chunk * CHUNK + 5 + tap
            c = c + few[tap : tap + 1, :] * pad[begin : begin + CHUNK, :]
        save[at, c_at] = c
        value = c * sigmoid(c)
        xs = value[:, :inner]
        b_low = value[:, inner : inner + states_count].astype(BF16)
        c_low = value[:, inner + states_count :].astype(BF16)
        delta, log_decay = steps(save[at, raw_at], bias, rate, mask)
        turned = log_decay.T
        final = log_decay[CHUNK - 1 : CHUNK, :]
        scaled = spread(delta, selector, heads) * xs
        scaled_low = scaled.astype(BF16)
        products = jnp.where(causal, mm(c_low, b_low, ((1,), (1,))), 0.0)
        within = []
        for two in range(heads // 2):
            lanes = slice(two * LANES, (two + 1) * LANES)
            parts = []
            for h in (2 * two, 2 * two + 1):
                gap = jnp.minimum(log_decay[:, h : h + 1] - turned[h : h + 1, :], 0.0)
                parts.append(mm((products * jnp.exp(gap)).astype(BF16), scaled_low[:, lanes]))
            within.append(jnp.where(first, parts[0], parts[1]))
        old = state[...]
        states[chunk] = old
        carried = mm(c_low, old.astype(BF16)) * spread(jnp.exp(log_decay) * mask, selector, heads)
        y = jnp.concatenate(within, 1) + carried + skip * xs
        save[at, y_at] = y
        ends = (spread(jnp.exp(final - log_decay) * mask, selector, heads) * scaled).astype(BF16)
        keep = spread(jnp.broadcast_to(jnp.exp(final) * mask, (8, LANES)), selector, heads)[0:1]
        state[...] = keep * old + mm(b_low, ends, ((0,), (0,)))
        z = save[at, z_at]
        gated = y * (z * sigmoid(z))
        total = jnp.sum(gated * gated, 1, keepdims=True)
        for piece in range(CHUNK // owner_rows):
            row = column_to_row(total[piece * owner_rows : (piece + 1) * owner_rows])
            squares[chunk * (CHUNK // owner_rows) + piece, 0:1, 0:owner_rows] = row
        mixed = (gated * gain).astype(BF16)
        part[at, :] = mm(mixed, w[:, split + LANES :], ((1,), (1,))).astype(BF16)


def forward_all_kernel(sizes, inputs, out_grad, shard, few_in, selector,
                       few_both, weights, errors, normed, saved, states, res, inverses, scales, firsts,
                       hidden, w_held, part, relays, sums, arrived, squares, others, stage, state_stage, norm_stage,
                       error_rows, own_scales, state, pad, spread_weights, few,
                       xs, xr, xl, es, er, el, zs, zr, zl, ys, yr, yl, cs, cr, y1s, y1r, y1l, c1s, c1r,
                       fs, fr, rs, rr, gs, gr, gl, qs, qr, ss, sr, ps, pr, outs, load):
    inner, pair, heads, lead, whole_inner = sizes
    layer_sizes = (inner, pair, heads)
    z, y, core, x = place()
    pipe = z % 2
    quarter = ROWS // 4
    few[pipe] = few_in[...]
    squares[...] = jnp.zeros_like(squares)
    greet(*around(x, at_x, (1, 2, 3)), *around(y, at_y), *around(z, at_z), at_core(1 - core), at_pipe(1 - pipe))
    few_swap = remote(few.at[pipe], few.at[pipe], (fs, fr), 0, at_pipe(1 - pipe))
    few_swap.start()
    piece = spread_weights.shape[1]
    shard_rows = lambda half: pl.ds(half * (piece // 2), piece // 2)
    z_slot = lambda origin, half: spread_weights.at[(origin % 2) * 2 + origin // 2, shard_rows(half)]
    z_ring = RingGather(z, at_z, lambda half: shard.at[shard_rows(half)], z_slot, (zs, zr, zl))
    z_ring.start()
    block_rows = lambda origin, half: pl.ds(pl.multiple_of(origin * ROWS + half * (ROWS // 2), ROWS // 2), ROWS // 2)
    x_ring = RingGather(x, at_x, lambda half: inputs.at[pipe, half],
                        lambda origin, half: hidden.at[0, block_rows(origin, half)], (xs, xr, xl))
    x_ring.start()
    e_ring = RingGather(x, at_x, lambda half: out_grad.at[pipe, half],
                        lambda origin, half: errors.at[block_rows(origin, half)], (es, er, el))
    weight_rings = []
    for layer, sems, core_sems in ((0, (ys, yr, yl), (cs, cr)), (1, (y1s, y1r, y1l), (c1s, c1r))):
        weight_rings.append(
            WeightRows(
                lambda half, layer=layer: spread_weights.at[2 * layer + half],
                lambda origin, half, core, layer=layer: weights.at[layer, (half * 4 + origin) * 2 + core],
                sems,
                core_sems,
            )
        )
    z_ring.relay()
    z_ring.wait(2, 3, 4, 5)
    z_ring.finish()
    weight_rings[0].start()
    x_ring.relay()
    e_ring.start()
    weight_rings[0].relay()
    few_swap.wait()
    few_both[...] = few[...]
    x_ring.wait(2, 3, 4, 5)
    x_ring.finish()
    for block in range(4):
        res[0, block] = hidden[0, owned(block, x, quarter)].astype(F32)
    weight_rings[0].finish()
    weight_rings[1].start()
    w_loads = [
        [
            pltpu.make_async_copy(
                weights.at[layer, index],
                w_held.at[layer, pl.ds(index * piece, piece)],
                load.at[layer * 16 + index],
            )
            for index in range(16)
        ]
        for layer in range(2)
    ]
    for copy in w_loads[0]:
        copy.start()
    for copy in w_loads[0]:
        copy.wait()

    def sums_of(op):
        rows = lambda owner, half: part.at[op, pl.ds(pl.multiple_of(owner * quarter + half * (quarter // 2), quarter // 2), quarter // 2)]
        return BlockSums(x, rows, relays, sums, arrived, (rs, rr), op)

    def squares_of(op):
        return to_everyone(x, at_x, lambda to: squares.at[op, to], lambda me: others.at[op, me], (qs, qr), op)

    def gather_of(block):
        place_of = lambda origin, half: hidden.at[
            1, pl.ds(pl.multiple_of(block * ROWS + origin * quarter + half * (quarter // 2), quarter // 2), quarter // 2)
        ]
        return RingGather(x, at_x, lambda half: place_of(x, half), place_of, (gs.at[block], gr.at[block], gl), local=False)

    def scales_of(block):
        return to_everyone(x, at_x, lambda to: own_scales.at[block], lambda me: scales.at[block, me], (ss, sr), block)

    def outs_of(op):
        layer, block = op // 4, op % 4
        slot = op % 2
        at = pl.ds(pl.multiple_of(block * ROWS, ROWS), ROWS)
        count = ROWS // CHUNK
        return [
            pltpu.make_async_copy(stage.at[slot], saved.at[layer, at], outs.at[0, slot]),
            pltpu.make_async_copy(state_stage.at[slot], states.at[layer, pl.ds(block * count, count)], outs.at[1, slot]),
            pltpu.make_async_copy(norm_stage.at[slot], normed.at[layer, at], outs.at[2, slot]),
        ]

    def finish_sums(op):
        layer, block = op // 4, op % 4
        job = sums_of(op)
        squares_of(op).wait()
        total = squares[op, x, 0:1, :]
        for step in (1, 2, 3):
            total = total + others[op, (x + step) % 4, 0:1, :]
        inverse = lax.rsqrt(total / whole_inner + EPS)
        inverses[layer, block] = jnp.broadcast_to(inverse, (8, LANES))
        column = row_to_column(inverse)[:quarter]
        job.wait()
        branch = column * job.result()
        value = res[layer, block] + branch
        res[layer + 1, block] = value
        job.finish()

        @pl.when(layer == 0)
        def _():
            hidden[1, owned(block, x, quarter)] = value.astype(BF16)
            gather_of(block).start()

        @pl.when(layer == 1)
        def _():
            dots = jnp.sum(error_rows[block].astype(F32) * branch, -1, keepdims=True) / whole_inner
            own_scales[block] = jnp.zeros((8, LANES), F32)
            own_scales[block, 0:1, :] = inverse
            own_scales[block, 1:2, 0:quarter] = column_to_row(dots)
            scales_of(block).start()

    error_loads = [
        pltpu.make_async_copy(errors.at[owned(block, x, quarter)], error_rows.at[block], load.at[32 + block])
        for block in range(4)
    ]
    own_block = hidden.at[1, pl.ds(pl.multiple_of(x * ROWS, ROWS), ROWS)]
    first_copy = pltpu.make_async_copy(own_block, firsts.at[pipe], load.at[36])
    swap = remote(own_block, firsts.at[pipe], (ps, pr), 0, at_pipe(1 - pipe))

    def step(op, carry):
        layer, block = op // 4, op % 4

        @pl.when(op < 8)
        def _():
            @pl.when(layer == 1)
            def _():
                job = gather_of(block)
                job.wait(2, 3, 4, 5)
                job.finish()

            @pl.when(op == 7)
            def _():
                first_copy.start()
                swap.start()

            @pl.when(op >= 2)
            def _():
                for copy in outs_of(op - 2):
                    copy.wait()

            slot = op % 2
            at = pl.ds(pl.multiple_of(block * ROWS, ROWS), ROWS)
            value = hidden[layer, at].astype(F32)
            gain = jnp.concatenate([few[layer, 6:7, lead:], few[layer, 7:8, :]], 1)
            norm_stage[slot] = (value * norm_scale(value) * gain).astype(BF16)
            forward_block(layer_sizes, block == 0, norm_stage[slot], w_held.at[layer], few.at[layer], selector[...],
                          stage.at[slot], state_stage.at[slot], part.at[op], squares.at[op], state, pad)
            for copy in outs_of(op):
                copy.start()

        @pl.when(op == 0)
        def _():
            e_ring.relay()

        @pl.when(op == 1)
        def _():
            weight_rings[1].relay()

        @pl.when(op == 2)
        def _():
            e_ring.wait(2, 3, 4, 5)
            e_ring.finish()
            for copy in error_loads:
                copy.start()

        @pl.when(op == 3)
        def _():
            weight_rings[1].finish()
            for copy in w_loads[1]:
                copy.start()
            for copy in error_loads:
                copy.wait()

        @pl.when((op >= 3) & (op < 7))
        def _():
            gather_of(op - 3).relay()

        @pl.when(op >= 2)
        def _():
            finish_sums(op - 2)

        @pl.when((op >= 1) & (op < 9))
        def _():
            sums_of(op - 1).relay()

        @pl.when(op < 8)
        def _():
            sums_of(op).start()
            squares_of(op).start()

        @pl.when(op == 3)
        def _():
            for copy in w_loads[1]:
                copy.wait()

        return carry

    lax.fori_loop(0, 10, step, 0)
    for op in (6, 7):
        for copy in outs_of(op):
            copy.wait()
    keep = [pltpu.make_async_copy(own_scales.at[block], scales.at[block, x], load.at[37 + block]) for block in range(4)]
    for copy in keep:
        copy.start()
    for block in range(4):
        scales_of(block).wait()
    for copy in keep:
        copy.wait()
    first_copy.wait()
    swap.wait()


class WeightRows:
    def __init__(self, source, slot, sems, core_sems):
        _, y, core, _ = place()
        self.core_sems, self.device = core_sems, at_core(1 - core)
        self.slot = lambda origin, half: slot(origin, half, core)
        self.ring = RingGather(y, at_y, source, self.slot, sems)
        self.hand = [remote(source(half), self.slot(y, half), core_sems, 6 + half, self.device) for half in range(2)]
        for index in range(6):
            held = self.slot(*self.ring.origins[index])
            self.hand.append(remote(held, held, core_sems, index, self.device))

    def start(self):
        self.ring.start()
        for copy in self.hand[:2]:
            copy.start()

    def relay(self):
        self.ring.relay()
        for index in range(2):
            self.hand[2 + index].start()

    def finish(self):
        for index in range(2, 6):
            self.ring.wait(index)
            self.hand[2 + index].start()
        self.ring.finish()
        for copy in self.hand:
            copy.wait()


def forward_all(inputs, out_grad, shard, few, inner, pair, heads, whole_inner):
    _, part, width = inputs.shape
    rows, columns = shard.shape
    conv = inner + pair
    lead = conv - (width - conv)
    length = 4 * part
    _, saved_columns = columns_of(inner, conv)
    quarter = ROWS // 4
    chunks = ROWS // CHUNK
    selector, _ = constants(inner, heads)
    half = (2, 2, part // 2, width)
    shape = jax.ShapeDtypeStruct
    return pl.pallas_call(
        partial(forward_all_kernel, (inner, pair, heads, lead, whole_inner)),
        out_shape=[
            shape((2,) + few.shape, F32),
            shape((2, 16, rows, columns), BF16),
            shape((length, width), BF16),
            shape((2, length, width), BF16),
            shape((2, length, saved_columns), F32),
            shape((2, length // CHUNK, pair // 2, inner), F32),
            shape((3, 4, quarter, width), F32),
            shape((2, 4, 8, LANES), F32),
            shape((4, 4, 8, LANES), F32),
            shape((2, part, width), BF16),
        ],
        in_specs=[ANY, ANY, ANY, VMEM, VMEM],
        out_specs=[VMEM, ANY, ANY, ANY, ANY, ANY, VMEM, VMEM, ANY, ANY],
        scratch_shapes=[
            pltpu.VMEM((2, length, width), BF16),
            pltpu.VMEM((2, 16 * rows, columns), BF16),
            pltpu.VMEM((8, ROWS, width), BF16),
            pltpu.VMEM((8, 2, quarter // 2, width), BF16),
            pltpu.VMEM((8, 2, quarter // 2, width), BF16),
            pltpu.VMEM((8, 2, 2, quarter // 2, width), BF16),
            pltpu.VMEM((8, 4, 8, LANES), F32),
            pltpu.VMEM((8, 4, 8, LANES), F32),
            pltpu.VMEM((2, ROWS, saved_columns), F32),
            pltpu.VMEM((2, chunks, pair // 2, inner), F32),
            pltpu.VMEM((2, ROWS, width), BF16),
            pltpu.VMEM((4, quarter, width), BF16),
            pltpu.VMEM((4, 8, LANES), F32),
            pltpu.VMEM((pair // 2, inner), F32),
            pltpu.VMEM((ROWS + 8, conv), F32),
            pltpu.VMEM((4, rows, columns), BF16),
            pltpu.VMEM((2,) + few.shape, F32),
        ]
        + gather_sems() * 3
        + (gather_sems() + dma(8)) * 2
        + dma(1)
        + [pltpu.SemaphoreType.DMA((8, 6))] * 2
        + [pltpu.SemaphoreType.DMA((4, 6))] * 2
        + [pltpu.SemaphoreType.DMA((2,))]
        + [pltpu.SemaphoreType.DMA((8, 3))] * 2
        + [pltpu.SemaphoreType.DMA((4, 3))] * 2
        + dma(1)
        + [pltpu.SemaphoreType.DMA((3, 2)), pltpu.SemaphoreType.DMA((41,))],
        compiler_params=remote_params(0),
        name="forward_layers",
    )(inputs.reshape(half), out_grad.reshape(half), shard, few, selector)


class Deliver:
    def __init__(self, layer, source, target, sends, recvs, local):
        z, _, _, x = place()
        self.pipe = z % 2
        self.here = self.pipe == layer
        self.copies = [
            pltpu.make_async_remote_copy(
                src_ref=source.at[(x + step) % 4],
                dst_ref=target.at[self.pipe, x],
                send_sem=sends.at[step],
                recv_sem=recvs.at[self.pipe * 4 + step],
                device_id={"pipe": layer, "tensor": (x + step) % 4},
                device_id_type=MESH,
            )
            for step in range(4)
        ]
        self.arrivals = [
            pltpu.make_async_remote_copy(
                src_ref=source.at[x],
                dst_ref=target.at[1 - self.pipe, x],
                send_sem=sends.at[step],
                recv_sem=recvs.at[(1 - self.pipe) * 4 + step],
                device_id={"pipe": 1 - self.pipe, "tensor": x},
                device_id_type=MESH,
            )
            for step in range(4)
        ]
        self.local = pltpu.make_async_copy(source.at[x], target.at[self.pipe, x], local)

    def start(self):
        for copy in self.copies[1:]:
            copy.start()

        @pl.when(self.here)
        def _():
            self.local.start()

        @pl.when(jnp.logical_not(self.here))
        def _():
            self.copies[0].start()

    def wait(self):
        for copy in self.copies[1:]:
            copy.wait_send()

        @pl.when(self.here)
        def _():
            self.local.wait()
            for copy in self.copies[1:] + self.arrivals:
                copy.wait_recv()

        @pl.when(jnp.logical_not(self.here))
        def _():
            self.copies[0].wait_send()


def both_pipes(x, pipe):
    return [{"pipe": 1 - pipe, "tensor": (x + step) % 4} for step in range(4)]


def turn_kernel(inner, lead, part, res, few, errors_later, inverses, grads, few_grad,
                errors, scales, input_grad, few_total, middle,
                raw, own, sent, b0, b1, b2, kept, arrived, total, d0, d1, d2,
                xs, xr, gs, gr, gl, ts, tr, cs, cr, ys, yr, load):
    z, y, core, x = place()
    quarter = ROWS // 4
    reads = [
        pltpu.make_async_copy(errors_later.at[owned(block, x, quarter)], raw.at[block], load.at[8 + block])
        for block in range(4)
    ]
    for read in reads:
        read.start()
    greet(*around(x, at_x, (1, 2, 3)), *around(y, at_y), at_core(1 - core))
    two = lambda half: pl.ds(2 * half, 2)
    sums = RingScatter(x, at_x, lambda owner, half: part.at[two(half), owner], (b0, b1, b2), (xs, xr))
    sums.start()
    cores = CoreSum(grads, kept, arrived, total, (cs, cr), load)
    cores.start()
    cores.finish()
    y_sums = RingScatter(y, at_y, lambda owner, half: total.at[owner, half], (d0, d1, d2), (ys, yr))
    y_sums.start()
    for read in reads:
        read.wait()
    gain = norm_gain_of(few, 1, lead)
    sums.relay()
    y_sums.relay()
    sums.wait()
    gain_grad = jnp.zeros_like(gain)
    own[...] = jnp.zeros_like(own)
    for half in range(2):
        result = sums.result(half)
        for index in range(2):
            block = 2 * half + index
            value, gain_part = back_through_norm(res[1, block], raw[block].astype(F32), result[index], gain)
            gain_grad = gain_grad + gain_part
            input_grad[block] = value
            low = value.astype(BF16)
            sent[block] = low
            branch = res[1, block] - res[0, block]
            dots = jnp.sum(low.astype(F32) * branch, -1, keepdims=True) / inner
            own[block, 0:1, :] = inverses[0, block, 0:1, :]
            own[block, 1:2, 0:quarter] = column_to_row(dots)
    x_ring = RingGather(x, at_x, lambda half: sent.at[two(half)], lambda origin, half: errors.at[two(half), origin], (gs, gr, gl))
    x_ring.start()
    tell = Everyone(x, at_x, lambda to: own, lambda me: scales.at[pl.ds(0, 4), me], (ts, tr))
    tell.start()
    keep = pltpu.make_async_copy(own, scales.at[pl.ds(0, 4), x], load.at[12])
    keep.start()
    add_norm_grad(few_total, few_grad, gain_grad, lead)
    y_sums.wait()
    for half in range(2):
        middle[half] = y_sums.result(half).astype(BF16)
    y_sums.finish()
    x_ring.relay()
    keep.wait()
    tell.wait()
    x_ring.wait(2, 3, 4, 5)
    x_ring.finish()
    sums.finish()


def turn_call(part, res, few, errors, inverses, grads, few_grad, inner):
    _, blocks, quarter, width = res.shape
    lead = few.shape[2] - (width - few.shape[2])
    columns = grads.shape[1]
    piece = grads.shape[0] // 16
    owned_rows = (blocks, quarter, width)
    shape = jax.ShapeDtypeStruct
    return pl.pallas_call(
        partial(turn_kernel, inner, lead),
        out_shape=[
            shape((blocks, 4, quarter, width), BF16),
            shape((blocks, 4, 8, LANES), F32),
            shape(owned_rows, F32),
            shape(few_grad.shape, F32),
            shape((2, piece, columns), BF16),
        ],
        in_specs=[VMEM, VMEM, VMEM, ANY, VMEM, ANY, VMEM],
        out_specs=[ANY, ANY, VMEM, VMEM, VMEM],
        scratch_shapes=[
            pltpu.VMEM(owned_rows, BF16),
            pltpu.VMEM((blocks, 8, LANES), F32),
            pltpu.VMEM(owned_rows, BF16),
        ]
        + scatter_buffers(2, quarter, width)
        + core_buffers(piece, columns)
        + scatter_buffers(piece, columns)
        + dma(6) + gather_sems() + dma(3) + dma(8) + dma(6)
        + [pltpu.SemaphoreType.DMA((13,))],
        compiler_params=remote_params(3),
        name="between_gradients",
    )(part.reshape(blocks, 4, quarter, width), res, few, errors, inverses,
      grads.reshape(2, 4, 2, piece, columns), few_grad)


def final_kernel(sizes, part, res, few, error, errors, grads, middle, few_grad, few_later,
                 last_out, first_grad, second_grad, large, few_sum, few_shared, state_grad,
                 low_out, low_grad, b0, b1, b2, kept, arrived, total, d0, d1, d2, e0, e1, e2, z_blocks,
                 mine, pair, y_few, z_few, x_few, state_parts,
                 xs, xr, ps, pr, cs, cr, ys, yr, zs, zr, fs, fr, hs, hr, js, jr, ks, kr, ws, wr,
                 os, og, is_, ig, load):
    lead, state_at, state_columns = sizes
    z, y, core, x = place()
    pipe = z % 2
    every = (1, 2, 3)
    for block in range(4):
        low_out[block] = res[2, block].astype(BF16)
    greet(*around(x, at_x, every), *around(y, at_y, every), *around(z, at_z, every), at_core(1 - core),
          *both_pipes(x, pipe))
    two = lambda half: pl.ds(2 * half, 2)
    sums = RingScatter(x, at_x, lambda owner, half: part.at[two(half), owner], (b0, b1, b2), (xs, xr))
    sums.start()
    cores = CoreSum(grads, kept, arrived, total, (cs, cr), load)
    cores.start()
    own_block = errors.at[x]
    keep = pltpu.make_async_copy(own_block, second_grad.at[pipe], load.at[8])
    keep.start()
    swap = remote(own_block, second_grad.at[pipe], (ps, pr), 0, at_pipe(1 - pipe))
    swap.start()
    output = Deliver(1, low_out, last_out, os, og, load.at[9])
    cores.finish()
    y_sums = RingScatter(y, at_y, lambda owner, half: total.at[owner, half], (d0, d1, d2), (ys, yr))
    y_sums.start()
    gain = norm_gain_of(few, 0, lead)
    sums.relay()
    output.start()
    y_sums.relay()
    sums.wait()
    gain_grad = jnp.zeros_like(gain)
    for half in range(2):
        result = sums.result(half)
        for index in range(2):
            block = 2 * half + index
            value, gain_part = back_through_norm(res[0, block], error[block], result[index], gain)
            gain_grad = gain_grad + gain_part
            low_grad[block] = value.astype(BF16)
    gradient = Deliver(0, low_grad, first_grad, is_, ig, load.at[10])
    gradient.start()
    mine[1] = few_later[...]
    add_norm_grad(mine.at[0], few_grad, gain_grad, lead)
    few_core = remote(mine, pair, (fs, fr), 0, at_core(1 - core))
    few_core.start()
    few_core.wait()
    mine[...] = mine[...] + pair[...]
    few_y = Everyone(y, at_y, lambda to: mine, lambda me: y_few.at[me], (hs, hr))
    few_y.start()
    y_sums.wait()
    rows = z_blocks.shape[2]
    for z_hi in range(2):
        first = y_sums.result(z_hi).astype(BF16)
        second = middle[z_hi]
        for half in range(2):
            z_blocks[2 * z_hi, half] = first[half * rows : (half + 1) * rows]
            z_blocks[2 * z_hi + 1, half] = second[half * rows : (half + 1) * rows]
    y_sums.finish()
    z_sums = RingScatter(z, at_z, lambda owner, half: z_blocks.at[owner, half], (e0, e1, e2), (zs, zr))
    z_sums.start()
    few_y.wait()
    y_few[y] = mine[...]
    mine[...] = (y_few[0] + y_few[1]) + (y_few[2] + y_few[3])
    few_z = Everyone(z, at_z, lambda to: mine.at[to % 2], lambda me: z_few.at[me], (js, jr))
    few_z.start()
    z_sums.relay()
    few_z.wait()
    z_few[z] = mine[pipe]
    few_sum[...] = (z_few[0] + z_few[1]) + (z_few[2] + z_few[3])
    x_few[x] = few_sum[...]
    few_x = Everyone(x, at_x, lambda to: few_sum, lambda me: x_few.at[me], (ks, kr))
    few_x.start()
    z_sums.wait()
    for half in range(2):
        large[half * rows : (half + 1) * rows, :] = z_sums.result(half)
    z_sums.finish()
    quarter = 2 * rows // 4
    for block in range(4):
        state_parts[0, block] = large[block * quarter : (block + 1) * quarter, state_at : state_at + state_columns]
    state_x = Everyone(x, at_x, lambda to: state_parts.at[0, to], lambda me: state_parts.at[1, me], (ws, wr))
    state_x.start()
    few_x.wait()
    few_shared[...] = (x_few[0] + x_few[1]) + (x_few[2] + x_few[3])
    state_x.wait()
    total_state = state_parts[0, x]
    for step in every:
        total_state = total_state + state_parts[1, (x + step) % 4]
    state_grad[...] = total_state
    keep.wait()
    swap.wait()
    output.wait()
    gradient.wait()
    sums.finish()


def final_call(part, res, few, error, errors, grads, middle, few_grad, few_later, sizes):
    blocks, quarter, width = error.shape
    wide = few.shape[2]
    lead = wide - (width - wide)
    columns = grads.shape[1]
    piece = grads.shape[0] // 16
    state_at, state_columns = sizes
    both = (2,) + few_grad.shape
    delivered = jax.ShapeDtypeStruct((2, blocks, quarter, width), BF16)
    return pl.pallas_call(
        partial(final_kernel, (lead, state_at, state_columns)),
        out_shape=[
            delivered,
            delivered,
            delivered,
            jax.ShapeDtypeStruct((piece, columns), F32),
            jax.ShapeDtypeStruct(few_grad.shape, F32),
            jax.ShapeDtypeStruct(few_grad.shape, F32),
            jax.ShapeDtypeStruct((piece // 4, state_columns), F32),
        ],
        in_specs=[VMEM, VMEM, VMEM, VMEM, ANY, ANY, VMEM, VMEM, VMEM],
        out_specs=[ANY, ANY, ANY, VMEM, VMEM, VMEM, VMEM],
        scratch_shapes=[pltpu.VMEM(error.shape, BF16), pltpu.VMEM(error.shape, BF16)]
        + scatter_buffers(2, quarter, width)
        + core_buffers(piece, columns)
        + scatter_buffers(piece, columns)
        + scatter_buffers(piece // 2, columns)
        + [
            pltpu.VMEM((4, 2, piece // 2, columns), BF16),
            pltpu.VMEM(both, F32),
            pltpu.VMEM(both, F32),
            pltpu.VMEM((4,) + both, F32),
            pltpu.VMEM((4,) + few_grad.shape, F32),
            pltpu.VMEM((4,) + few_grad.shape, F32),
            pltpu.VMEM((2, 4, piece // 4, state_columns), F32),
        ]
        + dma(6) + dma(1) + dma(8) + dma(6) + dma(6) + dma(1) + dma(3) + dma(3) + dma(3) + dma(3)
        + [pltpu.SemaphoreType.DMA((4,)), pltpu.SemaphoreType.DMA((8,))] * 2
        + [pltpu.SemaphoreType.DMA((11,))],
        compiler_params=remote_params(4),
        name="final_sums",
    )(part.reshape(blocks, 4, quarter, width), res, few, error, errors,
      grads.reshape(2, 4, 2, piece, columns), middle, few_grad, few_later)


def body(inputs, out_grad, norm_gain, in_gate_x, in_read_write, in_step, conv_main, conv_state,
         step_bias, log_rate, skip_gain, gate_gain, out_weight):
    _, part, width = inputs.shape
    inner = out_weight.shape[2]
    pair = in_read_write.shape[2]
    heads = step_bias.shape[1]
    whole_inner = inner * lax.axis_size("tensor")
    split = 2 * inner + pair
    wide = inner + pair
    first = lax.axis_index("pipe") == 0
    shard = jnp.concatenate(
        [
            in_gate_x[0, :, 0],
            in_gate_x[0, :, 1],
            in_read_write[0],
            jnp.pad(in_step[0], ((0, 0), (0, LANES - heads))),
            out_weight[0],
        ],
        1,
    )
    rate = -jnp.exp(log_rate[0])
    pad = ((0, 0), (0, LANES - heads))
    skip = jnp.broadcast_to(skip_gain[0][:, None], (heads, inner // heads)).reshape(1, inner)
    few = jnp.concatenate(
        [
            jnp.concatenate([conv_main[0], conv_state[0]], 1),
            jnp.concatenate([gate_gain, jnp.pad(step_bias, pad), jnp.pad(rate[None], pad)], 1),
            jnp.concatenate([skip, norm_gain], 1).reshape(2, wide),
        ],
        0,
    )
    few, weights, errors1, normed, saved, states, res, inverses, scales1, firsts = forward_all(
        inputs, out_grad, shard, few, inner, pair, heads, whole_inner
    )
    weights = weights.reshape(2, width, -1)
    part1, grad1, mixed1, few_grad1 = backward_call(
        1, errors1, scales1, weights, few, saved, states, inner, pair, heads
    )
    large1 = weight_call(1, normed, grad1, errors1, mixed1)
    errors0, scales0, input_grad1, few_grad1, middle = turn_call(
        part1, res, few, errors1, inverses, large1, few_grad1, whole_inner
    )
    rows0 = errors0.reshape(4 * part, width)
    part0, grad0, mixed0, few_grad0 = backward_call(
        0, rows0, scales0, weights, few, saved, states, inner, pair, heads
    )
    large0 = weight_call(0, normed, grad0, rows0, mixed0)
    last_out, first_grad, second_grad, large, few_sum, few_shared, state_grad = final_call(
        part0, res, few, input_grad1, errors0, large0, middle, few_grad0, few_grad1, (2 * inner, pair)
    )
    by_layer = lambda zero, one: jnp.where(
        first, zero.reshape(1, 2, part, width), one.reshape(1, 2, part, width)
    ).astype(F32)
    rates = few_sum[5, inner + LANES : inner + LANES + heads] * rate
    return (
        by_layer(firsts, last_out),
        by_layer(first_grad, second_grad),
        few_shared[6:].reshape(1, 2 * wide)[:, inner:],
        large[:, : 2 * inner].reshape(1, -1, 2, inner),
        state_grad[None],
        large[None, :, split : split + heads],
        few_sum[None, :5, :inner],
        few_shared[None, :5, inner:],
        few_sum[5:6, inner : inner + heads],
        rates[None],
        few_sum[6, :inner].reshape(1, heads, -1).sum(2),
        few_sum[5:6, :inner],
        large[None, :, split + LANES :],
    )


def solution(mesh):
    in_specs = (
        P("dp", "tensor", None),
        P("dp", "tensor", None),
        P("pipe", None),
        P("pipe", "dp", None, "tensor"),
        P("pipe", "dp", None),
        P("pipe", "dp", "tensor"),
        P("pipe", None, "tensor"),
        P("pipe", None, None),
        P("pipe", "tensor"),
        P("pipe", "tensor"),
        P("pipe", "tensor"),
        P("pipe", "tensor"),
        P("pipe", "dp", "tensor"),
    )
    out_specs = (
        P("pipe", "dp", "tensor", None),
        P("pipe", "dp", "tensor", None),
        P("pipe", None),
        P("pipe", "dp", None, "tensor"),
        P("pipe", ("dp", "tensor"), None),
        P("pipe", "dp", "tensor"),
        P("pipe", None, "tensor"),
        P("pipe", None, None),
        P("pipe", "tensor"),
        P("pipe", "tensor"),
        P("pipe", "tensor"),
        P("pipe", "tensor"),
        P("pipe", "dp", "tensor"),
    )
    return jax.shard_map(body, mesh=mesh, in_specs=in_specs, out_specs=out_specs, check_vma=False)
```

```python
from functools import partial

import jax
import jax.numpy as jnp
import numpy as np
from jax import lax
from jax.experimental import pallas as pl
from jax.experimental.pallas import tpu as pltpu
from jax.sharding import PartitionSpec as P

F32, BF16 = jnp.float32, jnp.bfloat16
EPS = 1e-05
ROWS = 256
CHUNK = 128
LANES = 128
EXACT = lax.Precision.HIGHEST


def mm(left, right, contract=((1,), (0,))):
    return lax.dot_general(left, right, (contract, ((), ())), preferred_element_type=F32)


def mm_exact(left, right, contract=((1,), (0,))):
    return lax.dot_general(
        left, right, (contract, ((), ())), precision=EXACT, preferred_element_type=F32
    )


def spread(value, selector, heads):
    high = value.astype(BF16).astype(F32)
    both = high + pltpu.roll(value - high, heads, 1)
    return mm(both.astype(BF16), selector)


def per_head(value, collector):
    high = value.astype(BF16)
    low = (value - high.astype(F32)).astype(BF16)
    return mm(high, collector) + mm(low, collector)


def softplus(value):
    small = jnp.exp(-jnp.abs(value))
    series = small * (1.0 - small * (0.5 - small * (1.0 / 3.0 - small * 0.25)))
    return jnp.maximum(value, 0.0) + jnp.where(small < 0.01, series, jnp.log(1.0 + small))


def sigmoid(value):
    return 1.0 / (1.0 + jnp.exp(-value))


def iota(shape, axis):
    return lax.broadcasted_iota(jnp.int32, shape, axis)


def column_to_row(column):
    size = column.shape[0]
    same = iota((size, size), 0) == iota((size, size), 1)
    return jnp.sum(jnp.where(same, column, 0.0), 0, keepdims=True)


def row_to_column(row):
    size = row.shape[1]
    same = iota((size, size), 0) == iota((size, size), 1)
    return jnp.sum(jnp.where(same, row, 0.0), 1, keepdims=True)


def steps(raw, bias, rate, mask):
    delta = softplus(raw + bias) * mask
    tri = (iota((CHUNK, CHUNK), 0) >= iota((CHUNK, CHUNK), 1)).astype(F32)
    log_decay = mm_exact(tri, delta * rate)
    return delta, log_decay


def constants(inner, heads):
    width = inner // heads
    lane = np.arange(LANES)[:, None]
    channel = np.arange(inner)[None, :] // width
    selector = ((lane % heads == channel) & (lane < 2 * heads)).astype(np.float32)
    collector = (lane == channel).astype(np.float32).T
    return jnp.asarray(selector, BF16), jnp.asarray(collector, BF16)


MESH = pl.DeviceIdType.MESH
ANY = pl.BlockSpec(memory_space=pl.ANY)
VMEM = pl.BlockSpec(memory_space=pltpu.VMEM)


def place():
    pipe, dp, x = lax.axis_index("pipe"), lax.axis_index("dp"), lax.axis_index("tensor")
    return (dp // 8) * 2 + pipe, (dp // 2) % 4, dp % 2, x


def at_z(z):
    _, y, core, _ = place()
    return {"pipe": z % 2, "dp": ((z // 2) * 4 + y) * 2 + core}


def at_y(y):
    z, _, core, _ = place()
    return {"dp": ((z // 2) * 4 + y) * 2 + core}


def at_core(core):
    z, y, _, _ = place()
    return {"dp": ((z // 2) * 4 + y) * 2 + core}


def at_x(x):
    return {"tensor": x}


def at_pipe(pipe):
    return {"pipe": pipe}


def greet(*devices):
    barrier = pltpu.get_barrier_semaphore()
    for device in devices:
        pl.semaphore_signal(barrier, inc=1, device_id=device, device_id_type=MESH)
    pl.semaphore_wait(barrier, len(devices))


def around(me, device, steps=(1, 3)):
    return [device((me + step) % 4) for step in steps]


def remote(source, target, sems, index, device):
    return pltpu.make_async_remote_copy(
        src_ref=source,
        dst_ref=target,
        send_sem=sems[0].at[index],
        recv_sem=sems[1].at[index],
        device_id=device,
        device_id_type=MESH,
    )


class RingGather:
    def __init__(self, me, device, own, slot, sems, local=True):
        right, left, across = (me + 1) % 4, (me + 3) % 4, (me + 2) % 4
        to_right, to_left = device(right), device(left)
        self.copies = [
            remote(own(0), slot(me, 0), sems, 0, to_right),
            remote(own(1), slot(me, 1), sems, 1, to_left),
            remote(own(1), slot(me, 1), sems, 2, to_right),
            remote(own(0), slot(me, 0), sems, 3, to_left),
            remote(slot(left, 0), slot(left, 0), sems, 4, to_right),
            remote(slot(right, 1), slot(right, 1), sems, 5, to_left),
        ]
        self.origins = [(left, 0), (right, 1), (left, 1), (right, 0), (across, 0), (across, 1)]
        self.local = [
            pltpu.make_async_copy(own(half), slot(me, half), sems[2].at[half]) for half in range(2 * local)
        ]

    def start(self):
        for copy in self.copies[:4]:
            copy.start()
        for copy in self.local:
            copy.start()

    def relay(self):
        for index in range(2):
            self.copies[index].wait_recv()
            self.copies[4 + index].start()

    def wait(self, *indices):
        for index in indices:
            self.copies[index].wait_recv()

    def finish(self):
        for copy in self.local:
            copy.wait()
        for copy in self.copies:
            copy.wait_send()


class RingScatter:
    def __init__(self, me, device, piece, buffers, sems):
        self.me, self.right, self.left = me, (me + 1) % 4, (me + 3) % 4
        across = (me + 2) % 4
        self.piece, self.buffers = piece, buffers
        relays, sums, arrived = buffers
        to_right, to_left = device(self.right), device(self.left)
        self.copies = [
            remote(piece(across, 0), relays.at[0], sems, 0, to_right),
            remote(piece(across, 1), relays.at[1], sems, 1, to_left),
            remote(piece(self.right, 1), arrived.at[0, 1], sems, 2, to_right),
            remote(piece(self.left, 0), arrived.at[1, 0], sems, 3, to_left),
            remote(sums.at[0], arrived.at[0, 0], sems, 4, to_right),
            remote(sums.at[1], arrived.at[1, 1], sems, 5, to_left),
        ]

    def start(self):
        for copy in self.copies[:4]:
            copy.start()

    def relay(self):
        relays, sums, _ = self.buffers
        for half, block in ((0, self.right), (1, self.left)):
            self.copies[half].wait_recv()
            total = relays[half].astype(F32) + self.piece(block, half)[...].astype(F32)
            sums[half] = total.astype(sums.dtype)
            self.copies[4 + half].start()

    def wait(self):
        for index in range(2, 6):
            self.copies[index].wait_recv()

    def result(self, half):
        arrived = self.buffers[2]
        mine = self.piece(self.me, half)[...].astype(F32)
        return mine + arrived[0, half].astype(F32) + arrived[1, half].astype(F32)

    def finish(self):
        for copy in self.copies:
            copy.wait_send()


class Everyone:
    def __init__(self, me, device, source, target, sems):
        self.copies = [
            remote(source((me + step) % 4), target(me), sems, step - 1, device((me + step) % 4))
            for step in (1, 2, 3)
        ]

    def start(self):
        for copy in self.copies:
            copy.start()

    def wait(self):
        for copy in self.copies:
            copy.wait()


def dma(count):
    return [pltpu.SemaphoreType.DMA((count,)), pltpu.SemaphoreType.DMA((count,))]


def gather_sems():
    return dma(6) + [pltpu.SemaphoreType.DMA((2,))]


def scatter_buffers(*half):
    return [pltpu.VMEM((2,) + half, BF16), pltpu.VMEM((2,) + half, BF16), pltpu.VMEM((2, 2) + half, BF16)]


def norm_scale(value):
    return lax.rsqrt(jnp.mean(value * value, -1, keepdims=True) + EPS)


def norm_gain_of(few, layer, lead):
    return jnp.concatenate([few[layer, 6:7, lead:], few[layer, 7:8, :]], 1)


def remote_params(collective_id):
    return pltpu.CompilerParams(
        collective_id=collective_id, has_side_effects=True, vmem_limit_bytes=56 * 2**20
    )


def owned(block, x, rows):
    return pl.ds(pl.multiple_of(block * ROWS + x * rows, rows), rows)


class BlockSums:
    def __init__(self, x, piece, relays, sums, arrived, sems, op):
        self.right, self.left, self.me = (x + 1) % 4, (x + 3) % 4, x
        across = (x + 2) % 4
        self.piece, self.relays, self.sums, self.arrived = piece, relays, sums, arrived
        at_op = [sem.at[op] for sem in sems]
        to_right, to_left = at_x(self.right), at_x(self.left)
        self.copies = [
            remote(piece(across, 0), relays.at[op, 0], at_op, 0, to_right),
            remote(piece(across, 1), relays.at[op, 1], at_op, 1, to_left),
            remote(piece(self.right, 1), arrived.at[op, 0, 1], at_op, 2, to_right),
            remote(piece(self.left, 0), arrived.at[op, 1, 0], at_op, 3, to_left),
            remote(sums.at[op, 0], arrived.at[op, 0, 0], at_op, 4, to_right),
            remote(sums.at[op, 1], arrived.at[op, 1, 1], at_op, 5, to_left),
        ]
        self.op = op

    def start(self):
        for copy in self.copies[:4]:
            copy.start()

    def relay(self):
        for half, block in ((0, self.right), (1, self.left)):
            self.copies[half].wait_recv()
            total = self.relays[self.op, half].astype(F32) + self.piece(block, half)[...].astype(F32)
            self.sums[self.op, half] = total.astype(BF16)
            self.copies[4 + half].start()

    def wait(self):
        for index in range(2, 6):
            self.copies[index].wait_recv()

    def result(self):
        return jnp.concatenate(
            [
                self.piece(self.me, half)[...].astype(F32)
                + self.arrived[self.op, 0, half].astype(F32)
                + self.arrived[self.op, 1, half].astype(F32)
                for half in range(2)
            ],
            0,
        )

    def finish(self):
        for copy in self.copies:
            copy.wait_send()


def to_everyone(me, device, source, target, sems, op):
    at_op = [sem.at[op] for sem in sems]
    return Everyone(me, device, source, target, at_op)


def columns_of(inner, conv):
    ends = np.cumsum([0, inner, conv, conv, LANES, inner])
    return [slice(int(begin), int(end)) for begin, end in zip(ends[:-1], ends[1:])], int(ends[-1])


def forward_block(sizes, first_block, rows, w, few, selector, save, states, part, squares, state, pad):
    inner, pair, heads = sizes
    states_count = pair // 2
    split = inner + inner + pair
    conv = inner + pair
    (z_at, p_at, c_at, raw_at, y_at), _ = columns_of(inner, conv)

    @pl.when(first_block)
    def _():
        state[...] = jnp.zeros_like(state)
        pad[0:8, :] = jnp.zeros((8, conv), F32)

    @pl.when(jnp.logical_not(first_block))
    def _():
        pad[0:8, :] = pad[ROWS : ROWS + 8, :]

    projected = mm(rows, w[:, : split + LANES])
    save[:, z_at] = projected[:, :inner]
    save[:, p_at] = projected[:, inner:split]
    pad[8 : ROWS + 8, :] = projected[:, inner:split]
    save[:, raw_at] = projected[:, split:]
    bias = few[5:6, inner : inner + LANES]
    rate = few[5:6, inner + LANES : inner + 2 * LANES]
    gain = few[5:6, :inner]
    skip = few[6:7, :inner]
    mask = (iota((1, LANES), 1) < heads).astype(F32)
    first = iota((CHUNK, LANES), 1) < LANES // 2
    causal = iota((CHUNK, CHUNK), 0) >= iota((CHUNK, CHUNK), 1)
    owner_rows = ROWS // 4
    for chunk in range(ROWS // CHUNK):
        at = slice(chunk * CHUNK, (chunk + 1) * CHUNK)
        c = jnp.broadcast_to(few[4:5, :], (CHUNK, conv))
        for tap in range(4):
            begin = chunk * CHUNK + 5 + tap
            c = c + few[tap : tap + 1, :] * pad[begin : begin + CHUNK, :]
        save[at, c_at] = c
        value = c * sigmoid(c)
        xs = value[:, :inner]
        b_low = value[:, inner : inner + states_count].astype(BF16)
        c_low = value[:, inner + states_count :].astype(BF16)
        delta, log_decay = steps(save[at, raw_at], bias, rate, mask)
        turned = log_decay.T
        final = log_decay[CHUNK - 1 : CHUNK, :]
        scaled = spread(delta, selector, heads) * xs
        scaled_low = scaled.astype(BF16)
        products = jnp.where(causal, mm(c_low, b_low, ((1,), (1,))), 0.0)
        within = []
        for two in range(heads // 2):
            lanes = slice(two * LANES, (two + 1) * LANES)
            parts = []
            for h in (2 * two, 2 * two + 1):
                gap = jnp.minimum(log_decay[:, h : h + 1] - turned[h : h + 1, :], 0.0)
                parts.append(mm((products * jnp.exp(gap)).astype(BF16), scaled_low[:, lanes]))
            within.append(jnp.where(first, parts[0], parts[1]))
        old = state[...]
        states[chunk] = old
        carried = mm(c_low, old.astype(BF16)) * spread(jnp.exp(log_decay) * mask, selector, heads)
        y = jnp.concatenate(within, 1) + carried + skip * xs
        save[at, y_at] = y
        ends = (spread(jnp.exp(final - log_decay) * mask, selector, heads) * scaled).astype(BF16)
        keep = spread(jnp.broadcast_to(jnp.exp(final) * mask, (8, LANES)), selector, heads)[0:1]
        state[...] = keep * old + mm(b_low, ends, ((0,), (0,)))
        z = save[at, z_at]
        gated = y * (z * sigmoid(z))
        total = jnp.sum(gated * gated, 1, keepdims=True)
        for piece in range(CHUNK // owner_rows):
            row = column_to_row(total[piece * owner_rows : (piece + 1) * owner_rows])
            squares[chunk * (CHUNK // owner_rows) + piece, 0:1, 0:owner_rows] = row
        mixed = (gated * gain).astype(BF16)
        part[at, :] = mm(mixed, w[:, split + LANES :], ((1,), (1,))).astype(BF16)


def forward_all_kernel(sizes, inputs, out_grad, shard, few_in, selector,
                       few_both, weights, errors, normed, saved, states, res, inverses, scales, firsts, last_low,
                       hidden, w_held, part, relays, sums, arrived, squares, others, stage, state_stage, norm_stage,
                       error_rows, own_scales, state, pad, spread_weights, few,
                       xs, xr, xl, es, er, el, zs, zr, zl, ys, yr, yl, cs, cr, y1s, y1r, y1l, c1s, c1r,
                       fs, fr, rs, rr, gs, gr, gl, qs, qr, ss, sr, ps, pr, outs, load):
    inner, pair, heads, lead, whole_inner = sizes
    layer_sizes = (inner, pair, heads)
    z, y, core, x = place()
    pipe = z % 2
    quarter = ROWS // 4
    few[pipe] = few_in[...]
    squares[...] = jnp.zeros_like(squares)
    greet(*around(x, at_x, (1, 2, 3)), *around(y, at_y), *around(z, at_z), at_core(1 - core), at_pipe(1 - pipe))
    few_swap = remote(few.at[pipe], few.at[pipe], (fs, fr), 0, at_pipe(1 - pipe))
    few_swap.start()
    piece = spread_weights.shape[1]
    shard_rows = lambda half: pl.ds(half * (piece // 2), piece // 2)
    z_slot = lambda origin, half: spread_weights.at[(origin % 2) * 2 + origin // 2, shard_rows(half)]
    z_ring = RingGather(z, at_z, lambda half: shard.at[shard_rows(half)], z_slot, (zs, zr, zl))
    z_ring.start()
    block_rows = lambda origin, half: pl.ds(pl.multiple_of(origin * ROWS + half * (ROWS // 2), ROWS // 2), ROWS // 2)
    x_ring = RingGather(x, at_x, lambda half: inputs.at[pipe, half],
                        lambda origin, half: hidden.at[0, block_rows(origin, half)], (xs, xr, xl))
    x_ring.start()
    e_ring = RingGather(x, at_x, lambda half: out_grad.at[pipe, half],
                        lambda origin, half: errors.at[block_rows(origin, half)], (es, er, el))
    weight_rings = []
    for layer, sems, core_sems in ((0, (ys, yr, yl), (cs, cr)), (1, (y1s, y1r, y1l), (c1s, c1r))):
        weight_rings.append(
            WeightRows(
                lambda half, layer=layer: spread_weights.at[2 * layer + half],
                lambda origin, half, core, layer=layer: weights.at[layer, (half * 4 + origin) * 2 + core],
                sems,
                core_sems,
            )
        )
    z_ring.relay()
    z_ring.wait(2, 3, 4, 5)
    z_ring.finish()
    weight_rings[0].start()
    x_ring.relay()
    e_ring.start()
    weight_rings[0].relay()
    few_swap.wait()
    few_both[...] = few[...]
    x_ring.wait(2, 3, 4, 5)
    x_ring.finish()
    for block in range(4):
        res[0, block] = hidden[0, owned(block, x, quarter)].astype(F32)
    weight_rings[0].finish()
    weight_rings[1].start()
    w_loads = [
        [
            pltpu.make_async_copy(
                weights.at[layer, index],
                w_held.at[layer, pl.ds(index * piece, piece)],
                load.at[layer * 16 + index],
            )
            for index in range(16)
        ]
        for layer in range(2)
    ]
    for copy in w_loads[0]:
        copy.start()
    for copy in w_loads[0]:
        copy.wait()

    def sums_of(op):
        rows = lambda owner, half: part.at[op, pl.ds(pl.multiple_of(owner * quarter + half * (quarter // 2), quarter // 2), quarter // 2)]
        return BlockSums(x, rows, relays, sums, arrived, (rs, rr), op)

    def squares_of(op):
        return to_everyone(x, at_x, lambda to: squares.at[op, to], lambda me: others.at[op, me], (qs, qr), op)

    def gather_of(block):
        place_of = lambda origin, half: hidden.at[
            1, pl.ds(pl.multiple_of(block * ROWS + origin * quarter + half * (quarter // 2), quarter // 2), quarter // 2)
        ]
        return RingGather(x, at_x, lambda half: place_of(x, half), place_of, (gs.at[block], gr.at[block], gl), local=False)

    def scales_of(block):
        return to_everyone(x, at_x, lambda to: own_scales.at[block], lambda me: scales.at[block, me], (ss, sr), block)

    def outs_of(op):
        layer, block = op // 4, op % 4
        slot = op % 2
        at = pl.ds(pl.multiple_of(block * ROWS, ROWS), ROWS)
        count = ROWS // CHUNK
        return [
            pltpu.make_async_copy(stage.at[slot], saved.at[layer, at], outs.at[0, slot]),
            pltpu.make_async_copy(state_stage.at[slot], states.at[layer, pl.ds(block * count, count)], outs.at[1, slot]),
            pltpu.make_async_copy(norm_stage.at[slot], normed.at[layer, at], outs.at[2, slot]),
        ]

    def finish_sums(op):
        layer, block = op // 4, op % 4
        job = sums_of(op)
        squares_of(op).wait()
        total = squares[op, x, 0:1, :]
        for step in (1, 2, 3):
            total = total + others[op, (x + step) % 4, 0:1, :]
        inverse = lax.rsqrt(total / whole_inner + EPS)
        inverses[layer, block] = jnp.broadcast_to(inverse, (8, LANES))
        column = row_to_column(inverse)[:quarter]
        job.wait()
        branch = column * job.result()
        value = res[layer, block] + branch
        job.finish()

        @pl.when(layer == 0)
        def _():
            res[1, block] = value
            hidden[1, owned(block, x, quarter)] = value.astype(BF16)
            gather_of(block).start()

        @pl.when(layer == 1)
        def _():
            last_low[block] = value.astype(BF16)
            dots = jnp.sum(error_rows[block].astype(F32) * branch, -1, keepdims=True) / whole_inner
            own_scales[block] = jnp.zeros((8, LANES), F32)
            own_scales[block, 0:1, :] = inverse
            own_scales[block, 1:2, 0:quarter] = column_to_row(dots)
            scales_of(block).start()

    error_loads = [
        pltpu.make_async_copy(errors.at[owned(block, x, quarter)], error_rows.at[block], load.at[32 + block])
        for block in range(4)
    ]
    own_block = hidden.at[1, pl.ds(pl.multiple_of(x * ROWS, ROWS), ROWS)]
    first_copy = pltpu.make_async_copy(own_block, firsts.at[pipe], load.at[36])
    swap = remote(own_block, firsts.at[pipe], (ps, pr), 0, at_pipe(1 - pipe))

    def step(op, carry):
        layer, block = op // 4, op % 4

        @pl.when(op < 8)
        def _():
            @pl.when(layer == 1)
            def _():
                job = gather_of(block)
                job.wait(2, 3, 4, 5)
                job.finish()

            @pl.when(op == 7)
            def _():
                first_copy.start()
                swap.start()

            @pl.when(op >= 2)
            def _():
                for copy in outs_of(op - 2):
                    copy.wait()

            slot = op % 2
            at = pl.ds(pl.multiple_of(block * ROWS, ROWS), ROWS)
            value = hidden[layer, at].astype(F32)
            gain = jnp.concatenate([few[layer, 6:7, lead:], few[layer, 7:8, :]], 1)
            norm_stage[slot] = (value * norm_scale(value) * gain).astype(BF16)
            forward_block(layer_sizes, block == 0, norm_stage[slot], w_held.at[layer], few.at[layer], selector[...],
                          stage.at[slot], state_stage.at[slot], part.at[op], squares.at[op], state, pad)
            for copy in outs_of(op):
                copy.start()

        @pl.when(op == 0)
        def _():
            e_ring.relay()

        @pl.when(op == 1)
        def _():
            weight_rings[1].relay()

        @pl.when(op == 2)
        def _():
            e_ring.wait(2, 3, 4, 5)
            e_ring.finish()
            for copy in error_loads:
                copy.start()

        @pl.when(op == 3)
        def _():
            weight_rings[1].finish()
            for copy in w_loads[1]:
                copy.start()
            for copy in error_loads:
                copy.wait()

        @pl.when((op >= 3) & (op < 7))
        def _():
            gather_of(op - 3).relay()

        @pl.when(op >= 2)
        def _():
            finish_sums(op - 2)

        @pl.when((op >= 1) & (op < 9))
        def _():
            sums_of(op - 1).relay()

        @pl.when(op < 8)
        def _():
            sums_of(op).start()
            squares_of(op).start()

        @pl.when(op == 3)
        def _():
            for copy in w_loads[1]:
                copy.wait()

        return carry

    lax.fori_loop(0, 10, step, 0)
    for op in (6, 7):
        for copy in outs_of(op):
            copy.wait()
    keep = [pltpu.make_async_copy(own_scales.at[block], scales.at[block, x], load.at[37 + block]) for block in range(4)]
    for copy in keep:
        copy.start()
    for block in range(4):
        scales_of(block).wait()
    for copy in keep:
        copy.wait()
    first_copy.wait()
    swap.wait()


class WeightRows:
    def __init__(self, source, slot, sems, core_sems):
        _, y, core, _ = place()
        self.core_sems, self.device = core_sems, at_core(1 - core)
        self.slot = lambda origin, half: slot(origin, half, core)
        self.ring = RingGather(y, at_y, source, self.slot, sems)
        self.hand = [remote(source(half), self.slot(y, half), core_sems, 6 + half, self.device) for half in range(2)]
        for index in range(6):
            held = self.slot(*self.ring.origins[index])
            self.hand.append(remote(held, held, core_sems, index, self.device))

    def start(self):
        self.ring.start()
        for copy in self.hand[:2]:
            copy.start()

    def relay(self):
        self.ring.relay()
        for index in range(2):
            self.hand[2 + index].start()

    def finish(self):
        for index in range(2, 6):
            self.ring.wait(index)
            self.hand[2 + index].start()
        self.ring.finish()
        for copy in self.hand:
            copy.wait()


def forward_all(inputs, out_grad, shard, few, inner, pair, heads, whole_inner):
    _, part, width = inputs.shape
    rows, columns = shard.shape
    conv = inner + pair
    lead = conv - (width - conv)
    length = 4 * part
    _, saved_columns = columns_of(inner, conv)
    quarter = ROWS // 4
    chunks = ROWS // CHUNK
    selector, _ = constants(inner, heads)
    half = (2, 2, part // 2, width)
    shape = jax.ShapeDtypeStruct
    return pl.pallas_call(
        partial(forward_all_kernel, (inner, pair, heads, lead, whole_inner)),
        out_shape=[
            shape((2,) + few.shape, F32),
            shape((2, 16, rows, columns), BF16),
            shape((length, width), BF16),
            shape((2, length, width), BF16),
            shape((2, length, saved_columns), F32),
            shape((2, length // CHUNK, pair // 2, inner), F32),
            shape((2, 4, quarter, width), F32),
            shape((2, 4, 8, LANES), F32),
            shape((4, 4, 8, LANES), F32),
            shape((2, part, width), BF16),
            shape((4, quarter, width), BF16),
        ],
        in_specs=[ANY, ANY, ANY, VMEM, VMEM],
        out_specs=[VMEM, ANY, ANY, ANY, ANY, ANY, VMEM, VMEM, ANY, ANY, VMEM],
        scratch_shapes=[
            pltpu.VMEM((2, length, width), BF16),
            pltpu.VMEM((2, 16 * rows, columns), BF16),
            pltpu.VMEM((8, ROWS, width), BF16),
            pltpu.VMEM((8, 2, quarter // 2, width), BF16),
            pltpu.VMEM((8, 2, quarter // 2, width), BF16),
            pltpu.VMEM((8, 2, 2, quarter // 2, width), BF16),
            pltpu.VMEM((8, 4, 8, LANES), F32),
            pltpu.VMEM((8, 4, 8, LANES), F32),
            pltpu.VMEM((2, ROWS, saved_columns), F32),
            pltpu.VMEM((2, chunks, pair // 2, inner), F32),
            pltpu.VMEM((2, ROWS, width), BF16),
            pltpu.VMEM((4, quarter, width), BF16),
            pltpu.VMEM((4, 8, LANES), F32),
            pltpu.VMEM((pair // 2, inner), F32),
            pltpu.VMEM((ROWS + 8, conv), F32),
            pltpu.VMEM((4, rows, columns), BF16),
            pltpu.VMEM((2,) + few.shape, F32),
        ]
        + gather_sems() * 3
        + (gather_sems() + dma(8)) * 2
        + dma(1)
        + [pltpu.SemaphoreType.DMA((8, 6))] * 2
        + [pltpu.SemaphoreType.DMA((4, 6))] * 2
        + [pltpu.SemaphoreType.DMA((2,))]
        + [pltpu.SemaphoreType.DMA((8, 3))] * 2
        + [pltpu.SemaphoreType.DMA((4, 3))] * 2
        + dma(1)
        + [pltpu.SemaphoreType.DMA((3, 2)), pltpu.SemaphoreType.DMA((41,))],
        compiler_params=remote_params(0),
        name="forward_layers",
    )(inputs.reshape(half), out_grad.reshape(half), shard, few, selector)


class Deliver:
    def __init__(self, layer, source, target, sends, recvs, local):
        self.layer, self.source, self.target = layer, source, target
        self.sends, self.recvs, self.local_sem = sends, recvs, local
        z, _, _, self.x = place()
        self.pipe = z % 2
        self.here = self.pipe == layer

    def copy(self, step, pipe, device_pipe, block):
        return pltpu.make_async_remote_copy(
            src_ref=self.source.at[block],
            dst_ref=self.target.at[pipe, self.x],
            send_sem=self.sends.at[step],
            recv_sem=self.recvs.at[pipe * 4 + step],
            device_id={"pipe": device_pipe, "tensor": block},
            device_id_type=MESH,
        )

    def out(self, step):
        return self.copy(step, self.pipe, self.layer, (self.x + step) % 4)

    def local(self):
        return pltpu.make_async_copy(self.source.at[self.x], self.target.at[self.pipe, self.x], self.local_sem)

    def start(self):
        for step in (1, 2, 3):
            self.out(step).start()

        @pl.when(self.here)
        def _():
            self.local().start()

        @pl.when(jnp.logical_not(self.here))
        def _():
            self.out(0).start()

    def wait(self):
        for step in (1, 2, 3):
            self.out(step).wait_send()

        @pl.when(self.here)
        def _():
            self.local().wait()
            for step in (1, 2, 3):
                self.out(step).wait_recv()
            for step in range(4):
                self.copy(step, 1 - self.pipe, 1 - self.pipe, self.x).wait_recv()

        @pl.when(jnp.logical_not(self.here))
        def _():
            self.out(0).wait_send()


def both_pipes(x, pipe):
    return [{"pipe": 1 - pipe, "tensor": (x + step) % 4} for step in range(4)]


class CoreSum:
    def __init__(self, grads, arrived, sems):
        _, _, core, _ = place()
        self.grads, self.arrived, self.core = grads, arrived, core
        self.pieces = [(y, half) for y in range(4) for half in range(2)]
        self.sems = sems

    def copy(self, index):
        y, half = self.pieces[index]
        source = self.grads.at[half, y, 1 - self.core]
        return remote(source, self.arrived.at[y, half], self.sems, index, at_core(1 - self.core))

    def start(self):
        for index in range(8):
            self.copy(index).start()

    def finish(self):
        for index, (y, half) in enumerate(self.pieces):
            self.copy(index).wait_recv()
            value = self.grads[half, y, self.core].astype(F32) + self.arrived[y, half].astype(F32)
            self.grads[half, y, self.core] = value.astype(BF16)
        for index in range(8):
            self.copy(index).wait_send()


def back_through_norm(value, grad_out, summed, gain):
    scale = norm_scale(value)
    unit = value * scale
    scaled = summed * gain
    mean = jnp.mean(scaled * unit, -1, keepdims=True)
    return grad_out + scale * (scaled - unit * mean), jnp.sum(summed * unit, 0, keepdims=True)


def backward_block(sizes, first_block, e, scales, w, few, selector, collector, saved, states,
                   part, grad, mixed, few_out, state, later, pad):
    inner, pair, heads = sizes
    states_count = pair // 2
    split = inner + inner + pair
    conv = inner + pair
    quarter = ROWS // 4
    (z_at, p_at, c_at, raw_at, y_at), _ = columns_of(inner, conv)

    @pl.when(first_block)
    def _():
        state[...] = jnp.zeros_like(state)
        later[...] = jnp.zeros_like(later)
        pad[ROWS : ROWS + 8, :] = jnp.zeros((8, conv), F32)

    @pl.when(jnp.logical_not(first_block))
    def _():
        pad[ROWS : ROWS + 8, :] = pad[0:8, :]

    bias = few[5:6, inner : inner + LANES]
    rate = few[5:6, inner + LANES : inner + 2 * LANES]
    gain = few[5:6, :inner]
    skip = few[6:7, :inner]
    mask = (iota((1, LANES), 1) < heads).astype(F32)
    first = iota((CHUNK, LANES), 1) < LANES // 2
    later_in = iota((CHUNK, CHUNK), 1) >= iota((CHUNK, CHUNK), 0)
    last = iota((CHUNK, LANES), 0) == CHUNK - 1
    tri = later_in.astype(F32)
    column = lambda row: jnp.concatenate(
        [row_to_column(scales[owner, row : row + 1, :])[:quarter] for owner in range(4)], 0
    )
    inverse = column(0)
    inner_dot = column(1)
    mixed_grad = mm(e, w[:, split + LANES :])
    for chunk in reversed(range(ROWS // CHUNK)):
        at = slice(chunk * CHUNK, (chunk + 1) * CHUNK)
        z = saved[at, z_at]
        y = saved[at, y_at]
        sig = sigmoid(z)
        act = z * sig
        g = y * act * inverse[at]
        mixed[at, :] = (g * gain).astype(BF16)
        mixed_here = mixed_grad[at]
        gated_grad = inverse[at] * (mixed_here * gain - g * inner_dot[at])
        dy = gated_grad * act
        grad[at, :inner] = (gated_grad * y * (sig * (1.0 + z - act))).astype(BF16)
        c = saved[at, c_at]
        csig = sigmoid(c)
        value = c * csig
        slope = csig * (1.0 + c - value)
        xs = value[:, :inner]
        b_low = value[:, inner : inner + states_count].astype(BF16)
        c_low = value[:, inner + states_count :].astype(BF16)
        raw = saved[at, raw_at]
        delta, log_decay = steps(raw, bias, rate, mask)
        turned = log_decay.T
        final = log_decay[CHUNK - 1 : CHUNK, :]
        wide_delta = spread(delta, selector, heads)
        scaled = wide_delta * xs
        scaled_low = scaled.astype(BF16)
        dy_low = dy.astype(BF16)
        products = jnp.where(later_in, mm(b_low, c_low, ((1,), (1,))), 0.0)
        dproducts = jnp.zeros((CHUNK, CHUNK), F32)
        within = []
        for two in range(heads // 2):
            lanes = slice(two * LANES, (two + 1) * LANES)
            parts = []
            for odd in range(2):
                h = 2 * two + odd
                mine = first if odd == 0 else ~first
                decay = jnp.exp(jnp.minimum(turned[h : h + 1, :] - log_decay[:, h : h + 1], 0.0))
                parts.append(mm((products * decay).astype(BF16), dy_low[:, lanes]))
                own = jnp.where(mine, scaled_low[:, lanes], jnp.zeros((), BF16))
                dproducts = dproducts + decay * mm(own, dy_low[:, lanes], ((1,), (1,)))
            within.append(jnp.where(first, parts[0], parts[1]))
        dproducts = jnp.where(later_in, dproducts, 0.0).astype(BF16)
        old = states[chunk]
        old_low = old.astype(BF16)
        dstate = state[...]
        dstate_low = dstate.astype(BF16)
        to_end = spread(jnp.exp(final - log_decay) * mask, selector, heads)
        from_start = (spread(jnp.exp(log_decay) * mask, selector, heads) * dy).astype(BF16)
        dscaled = jnp.concatenate(within, 1) + to_end * mm(b_low, dstate_low)
        dc_state = mm(from_start, old_low, ((1,), (1,))) + mm(dproducts, b_low, ((0,), (0,)))
        db_state = mm((to_end * scaled).astype(BF16), dstate_low, ((1,), (1,))) + mm(dproducts, c_low)
        carry = jnp.broadcast_to(jnp.sum(later[...] * dstate, 0, keepdims=True), (8, inner))
        carry = per_head(carry, collector)[0:1]
        keep = spread(jnp.broadcast_to(jnp.exp(final) * mask, (8, LANES)), selector, heads)[0:1]
        state[...] = keep * dstate + mm(c_low, from_start, ((0,), (0,)))
        later[...] = old
        flow = dy_low.astype(F32) * (y - skip * xs) - scaled_low.astype(F32) * dscaled
        dlog = per_head(flow, collector) + jnp.where(last, carry, 0.0)
        dstep = mm_exact(tri, dlog)
        ddelta = per_head(xs * dscaled, collector) + rate * dstep
        draw = ddelta * sigmoid(raw + bias) * mask
        few_out[5:6, inner : inner + LANES] += jnp.sum(draw, 0, keepdims=True)
        few_out[5:6, inner + LANES : inner + 2 * LANES] += jnp.sum(delta * dstep, 0, keepdims=True)
        few_out[5:6, :inner] += jnp.sum(mixed_here * g, 0, keepdims=True)
        few_out[6:7, :inner] += jnp.sum(dy * xs, 0, keepdims=True)
        dxs = wide_delta * dscaled + skip * dy
        pad[at, :] = jnp.concatenate([dxs, db_state, dc_state], 1) * slope
        grad[at, split:] = draw.astype(BF16)
    for chunk in range(ROWS // CHUNK):
        at = slice(chunk * CHUNK, (chunk + 1) * CHUNK)
        p = saved[at, p_at]
        total = jnp.zeros((CHUNK, conv), F32)
        for tap in range(4):
            begin = chunk * CHUNK + 3 - tap
            shifted = pad[begin : begin + CHUNK, :]
            total = total + few[tap : tap + 1, :] * shifted
            few_out[tap : tap + 1, :] += jnp.sum(p * shifted, 0, keepdims=True)
        few_out[4:5, :] += jnp.sum(pad[at, :], 0, keepdims=True)
        grad[at, inner:split] = total.astype(BF16)
    part[...] = mm(grad[...], w[:, : split + LANES], ((1,), (1,))).astype(BF16)


def backward_all_kernel(sizes, errors_later, scales_later, weights, few, selector, collector, normed, saved, states,
                        res, inverses, last_low,
                        last_out, first_grad, second_grad, large, few_sum, few_shared, state_grad,
                        errors, scales, w_held, part, relays, sums, arrived, stage, state_stage, norm_stage,
                        grad, mixed, own_scales, own_grad, low_grad, few_grad, norm_grad, total, low_total,
                        core1, core0, u0, u1, u2, v0, v1, v2, e0, e1, e2, middle, z_blocks,
                        pair_few, y_few, z_few, x_few, state_parts, state, later, pad,
                        rs, rr, gs, gr, ss, sr, c1s, c1r, y1s, y1r, c0s, c0r, y0s, y0r, zs, zr,
                        ps, pr, fs, fr, hs, hr, js, jr, ks, kr, ws, wr, os, og, is_, ig, loads, load):
    inner, pair, heads, lead, whole_inner = sizes
    layer_sizes = (inner, pair, heads)
    z, y, core, x = place()
    pipe = z % 2
    every = (1, 2, 3)
    quarter = ROWS // 4
    split = 2 * inner + pair

    def at_step(op):
        return 1 - op // 4, 3 - op % 4

    def loads_of(op):
        layer, block = at_step(op)
        slot = op % 2
        at = pl.ds(pl.multiple_of(block * ROWS, ROWS), ROWS)
        count = ROWS // CHUNK
        return [
            pltpu.make_async_copy(saved.at[layer, at], stage.at[slot], loads.at[0, slot]),
            pltpu.make_async_copy(states.at[layer, pl.ds(block * count, count)], state_stage.at[slot], loads.at[1, slot]),
            pltpu.make_async_copy(normed.at[layer, at], norm_stage.at[slot], loads.at[2, slot]),
        ]

    def weight_load(layer):
        return pltpu.make_async_copy(weights.at[layer], w_held.at[layer], load.at[layer])

    error_load = pltpu.make_async_copy(errors_later, errors.at[1], load.at[2])
    error_load.start()
    weight_load(1).start()
    for copy in loads_of(0):
        copy.start()
    weight_load(0).start()
    greet(*around(x, at_x, every), *around(y, at_y, every), *around(z, at_z, every), at_core(1 - core),
          *both_pipes(x, pipe))
    output = Deliver(1, last_low, last_out, os, og, load.at[3])
    output.start()
    scales[1] = scales_later[...]
    few_grad[...] = jnp.zeros_like(few_grad)
    norm_grad[...] = jnp.zeros_like(norm_grad)
    own_scales[...] = jnp.zeros_like(own_scales)
    total[...] = jnp.zeros_like(total)
    error_load.wait()
    for block in range(4):
        own_grad[block] = errors[1, owned(block, x, quarter)].astype(F32)
    weight_load(1).wait()

    def sums_of(op):
        rows = lambda owner, half: part.at[
            op % 4, pl.ds(pl.multiple_of(owner * quarter + half * (quarter // 2), quarter // 2), quarter // 2)
        ]
        return BlockSums(x, rows, relays, sums, arrived, (rs, rr), op)

    def gather_of(block):
        place_of = lambda origin, half: errors.at[
            0, pl.ds(pl.multiple_of(block * ROWS + origin * quarter + half * (quarter // 2), quarter // 2), quarter // 2)
        ]
        return RingGather(x, at_x, lambda half: place_of(x, half), place_of, (gs.at[block], gr.at[block]), local=False)

    def scales_of(block):
        return to_everyone(x, at_x, lambda to: own_scales.at[block], lambda me: scales.at[0, block, me], (ss, sr), block)

    def core_sum(layer):
        arrived_core, sems = ((core0, (c0s, c0r)), (core1, (c1s, c1r)))[layer]
        return CoreSum(low_total, arrived_core, sems)

    def y_sum(layer):
        buffers, sems = (((v0, v1, v2), (y0s, y0r)), ((u0, u1, u2), (y1s, y1r)))[layer]
        return RingScatter(y, at_y, lambda owner, half: low_total.at[half, owner, core], buffers, sems)

    def finish_sums(op):
        layer, block = at_step(op)
        job = sums_of(op)
        job.wait()
        gain = jnp.concatenate([few[layer, 6:7, lead:], few[layer, 7:8, :]], 1)
        value, gain_part = back_through_norm(res[layer, block], own_grad[block], job.result(), gain)
        own_grad[block] = value
        norm_grad[layer, 0:1, :] += gain_part
        low = value.astype(BF16)
        job.finish()

        @pl.when(layer == 1)
        def _():
            errors[0, owned(block, x, quarter)] = low
            gather_of(block).start()
            dots = jnp.sum(low.astype(F32) * (res[1, block] - res[0, block]), -1, keepdims=True) / whole_inner
            own_scales[block, 0:1, :] = inverses[0, block, 0:1, :]
            own_scales[block, 1:2, 0:quarter] = column_to_row(dots)
            scales[0, block, x] = own_scales[block]
            scales_of(block).start()

        @pl.when(layer == 0)
        def _():
            low_grad[block] = low

    def flush():
        piece = total.shape[0] // 16
        for index in range(16):
            z_hi, y_at, core_at = index // 8, (index // 2) % 4, index % 2
            low_total[z_hi, y_at, core_at] = total[index * piece : (index + 1) * piece, :].astype(BF16)

    own_block = errors.at[0, pl.ds(pl.multiple_of(x * ROWS, ROWS), ROWS)]
    second_copy = pltpu.make_async_copy(own_block, second_grad.at[pipe], load.at[4])
    swap = remote(own_block, second_grad.at[pipe], (ps, pr), 0, at_pipe(1 - pipe))

    def step(op, carry):
        layer, block = at_step(op)
        slot = op % 2

        @pl.when(layer == 0)
        def _():
            job = gather_of(block)
            job.wait(2, 3, 4, 5)
            job.finish()
            scales_of(block).wait()

        @pl.when(op == 4)
        def _():
            weight_load(0).wait()

        @pl.when(op == 7)
        def _():
            second_copy.start()
            swap.start()

        for copy in loads_of(op):
            copy.wait()

        @pl.when(op < 7)
        def _():
            for copy in loads_of(op + 1):
                copy.start()

        at = pl.ds(pl.multiple_of(block * ROWS, ROWS), ROWS)
        e = errors[layer, at]
        backward_block(layer_sizes, block == 3, e, scales.at[layer, block], w_held.at[layer], few.at[layer],
                       selector[...], collector[...], stage.at[slot], state_stage.at[slot],
                       part.at[op % 4], grad, mixed, few_grad.at[layer], state, later, pad)
        sums_of(op).start()

        @pl.when((op >= 3) & (op < 7))
        def _():
            gather_of(6 - op).relay()

        @pl.when(op >= 2)
        def _():
            finish_sums(op - 2)

        @pl.when(op >= 1)
        def _():
            sums_of(op - 1).relay()

        @pl.when(op == 4)
        def _():
            core_sum(1).finish()
            y_sum(1).start()

        @pl.when(op == 5)
        def _():
            y_sum(1).relay()

        @pl.when(op == 6)
        def _():
            job = y_sum(1)
            job.wait()
            for half in range(2):
                middle[half] = job.result(half).astype(BF16)
            job.finish()

        turn = ((0,), (0,))
        wide = split + LANES
        for index in range(total.shape[0] // ROWS):
            rows = slice(index * ROWS, (index + 1) * ROWS)
            total[rows, :wide] += mm(norm_stage[slot, :, rows], grad[...], turn)
            total[rows, wide:] += mm(errors[layer, at, rows], mixed[...], turn)

        @pl.when(op == 3)
        def _():
            flush()
            core_sum(1).start()
            total[...] = jnp.zeros_like(total)

        return carry

    lax.fori_loop(0, 8, step, 0)
    flush()
    cores = core_sum(0)
    cores.start()
    finish_sums(6)
    sums_of(7).relay()
    cores.finish()
    y_sums = y_sum(0)
    y_sums.start()
    finish_sums(7)
    gradient = Deliver(0, low_grad, first_grad, is_, ig, load.at[5])
    gradient.start()
    for layer in range(2):
        width = few_grad.shape[2] - lead
        few_grad[layer, 6:7, lead:] = norm_grad[layer, 0:1, :width]
        few_grad[layer, 7:8, :] = norm_grad[layer, 0:1, width:]
    few_core = remote(few_grad, pair_few, (fs, fr), 0, at_core(1 - core))
    few_core.start()
    few_core.wait()
    y_sums.relay()
    few_grad[...] = few_grad[...] + pair_few[...]
    few_y = Everyone(y, at_y, lambda to: few_grad, lambda me: y_few.at[me], (hs, hr))
    few_y.start()
    y_sums.wait()
    rows = z_blocks.shape[2]
    for z_hi in range(2):
        first = y_sums.result(z_hi).astype(BF16)
        second = middle[z_hi]
        for half in range(2):
            z_blocks[2 * z_hi, half] = first[half * rows : (half + 1) * rows]
            z_blocks[2 * z_hi + 1, half] = second[half * rows : (half + 1) * rows]
    z_sums = RingScatter(z, at_z, lambda owner, half: z_blocks.at[owner, half], (e0, e1, e2), (zs, zr))
    z_sums.start()
    y_sums.finish()
    few_y.wait()
    y_few[y] = few_grad[...]
    few_grad[...] = (y_few[0] + y_few[1]) + (y_few[2] + y_few[3])
    few_z = Everyone(z, at_z, lambda to: few_grad.at[to % 2], lambda me: z_few.at[me], (js, jr))
    few_z.start()
    z_sums.relay()
    few_z.wait()
    z_few[z] = few_grad[pipe]
    few_sum[...] = (z_few[0] + z_few[1]) + (z_few[2] + z_few[3])
    x_few[x] = few_sum[...]
    few_x = Everyone(x, at_x, lambda to: few_sum, lambda me: x_few.at[me], (ks, kr))
    few_x.start()
    z_sums.wait()
    for half in range(2):
        large[half * rows : (half + 1) * rows, :] = z_sums.result(half)
    state_rows = 2 * rows // 4
    for block in range(4):
        state_parts[0, block] = large[block * state_rows : (block + 1) * state_rows, 2 * inner : split]
    state_x = Everyone(x, at_x, lambda to: state_parts.at[0, to], lambda me: state_parts.at[1, me], (ws, wr))
    state_x.start()
    z_sums.finish()
    few_x.wait()
    few_shared[...] = (x_few[0] + x_few[1]) + (x_few[2] + x_few[3])
    state_x.wait()
    total_state = state_parts[0, x]
    for step_at in every:
        total_state = total_state + state_parts[1, (x + step_at) % 4]
    state_grad[...] = total_state
    second_copy.wait()
    swap.wait()
    output.wait()
    gradient.wait()


def backward_all(errors, scales, weights, few, normed, saved, states, res, inverses, last_low,
                 inner, pair, heads, whole_inner):
    length, width = errors.shape
    _, blocks, quarter, _ = res.shape
    conv = inner + pair
    lead = conv - (width - conv)
    split = 2 * inner + pair
    columns = weights.shape[2]
    piece = weights.shape[1] // 16
    chunks = ROWS // CHUNK
    selector, collector = constants(inner, heads)
    shape = jax.ShapeDtypeStruct
    delivered = shape((2, blocks, quarter, width), BF16)
    few_shape = few.shape[1:]
    half = (quarter // 2, width)
    semaphores = lambda *count: [pltpu.SemaphoreType.DMA(count)] * 2
    return pl.pallas_call(
        partial(backward_all_kernel, (inner, pair, heads, lead, whole_inner)),
        out_shape=[
            delivered,
            delivered,
            shape((2, blocks * quarter, width), BF16),
            shape((piece, columns), F32),
            shape(few_shape, F32),
            shape(few_shape, F32),
            shape((piece // 4, pair), F32),
        ],
        in_specs=[ANY, VMEM, ANY, VMEM, VMEM, VMEM, ANY, ANY, ANY, VMEM, VMEM, ANY],
        out_specs=[ANY, ANY, ANY, VMEM, VMEM, VMEM, VMEM],
        scratch_shapes=[
            pltpu.VMEM((2, length, width), BF16),
            pltpu.VMEM((2, blocks, 4, 8, LANES), F32),
            pltpu.VMEM(weights.shape, BF16),
            pltpu.VMEM((4, ROWS, width), BF16),
            pltpu.VMEM((8, 2) + half, BF16),
            pltpu.VMEM((8, 2) + half, BF16),
            pltpu.VMEM((8, 2, 2) + half, BF16),
            pltpu.VMEM((2, ROWS, saved.shape[2]), F32),
            pltpu.VMEM((2, chunks, pair // 2, inner), F32),
            pltpu.VMEM((2, ROWS, width), BF16),
            pltpu.VMEM((ROWS, split + LANES), BF16),
            pltpu.VMEM((ROWS, inner), BF16),
            pltpu.VMEM((blocks, 8, LANES), F32),
            pltpu.VMEM((blocks, quarter, width), F32),
            pltpu.VMEM((blocks, quarter, width), BF16),
            pltpu.VMEM((2,) + few_shape, F32),
            pltpu.VMEM((2, 8, width), F32),
            pltpu.VMEM((width, columns), F32),
            pltpu.VMEM((2, 4, 2, piece, columns), BF16),
            pltpu.VMEM((4, 2, piece, columns), BF16),
            pltpu.VMEM((4, 2, piece, columns), BF16),
        ]
        + scatter_buffers(piece, columns) * 2
        + scatter_buffers(piece // 2, columns)
        + [
            pltpu.VMEM((2, piece, columns), BF16),
            pltpu.VMEM((4, 2, piece // 2, columns), BF16),
            pltpu.VMEM((2,) + few_shape, F32),
            pltpu.VMEM((4, 2) + few_shape, F32),
            pltpu.VMEM((4,) + few_shape, F32),
            pltpu.VMEM((4,) + few_shape, F32),
            pltpu.VMEM((2, 4, piece // 4, pair), F32),
            pltpu.VMEM((pair // 2, inner), F32),
            pltpu.VMEM((pair // 2, inner), F32),
            pltpu.VMEM((ROWS + 8, conv), F32),
        ]
        + semaphores(8, 6) + semaphores(4, 6) + semaphores(4, 3)
        + dma(8) + dma(6) + dma(8) + dma(6) + dma(6)
        + dma(1) + dma(1) + dma(3) + dma(3) + dma(3) + dma(3)
        + [pltpu.SemaphoreType.DMA((4,)), pltpu.SemaphoreType.DMA((8,))] * 2
        + [pltpu.SemaphoreType.DMA((3, 2)), pltpu.SemaphoreType.DMA((6,))],
        compiler_params=pltpu.CompilerParams(collective_id=1, has_side_effects=True, vmem_limit_bytes=62 * 2**20),
        name="backward_layers",
    )(errors, scales, weights, few, selector, collector, normed, saved, states, res, inverses, last_low)


def body(inputs, out_grad, norm_gain, in_gate_x, in_read_write, in_step, conv_main, conv_state,
         step_bias, log_rate, skip_gain, gate_gain, out_weight):
    _, part, width = inputs.shape
    inner = out_weight.shape[2]
    pair = in_read_write.shape[2]
    heads = step_bias.shape[1]
    whole_inner = inner * lax.axis_size("tensor")
    split = 2 * inner + pair
    wide = inner + pair
    first = lax.axis_index("pipe") == 0
    shard = jnp.concatenate(
        [
            in_gate_x[0, :, 0],
            in_gate_x[0, :, 1],
            in_read_write[0],
            jnp.pad(in_step[0], ((0, 0), (0, LANES - heads))),
            out_weight[0],
        ],
        1,
    )
    rate = -jnp.exp(log_rate[0])
    pad = ((0, 0), (0, LANES - heads))
    skip = jnp.broadcast_to(skip_gain[0][:, None], (heads, inner // heads)).reshape(1, inner)
    few = jnp.concatenate(
        [
            jnp.concatenate([conv_main[0], conv_state[0]], 1),
            jnp.concatenate([gate_gain, jnp.pad(step_bias, pad), jnp.pad(rate[None], pad)], 1),
            jnp.concatenate([skip, norm_gain], 1).reshape(2, wide),
        ],
        0,
    )
    few, weights, errors, normed, saved, states, res, inverses, scales, firsts, last_low = forward_all(
        inputs, out_grad, shard, few, inner, pair, heads, whole_inner
    )
    weights = weights.reshape(2, width, -1)
    last_out, first_grad, second_grad, large, few_sum, few_shared, state_grad = backward_all(
        errors, scales, weights, few, normed, saved, states, res, inverses, last_low,
        inner, pair, heads, whole_inner
    )
    by_layer = lambda zero, one: jnp.where(
        first, zero.reshape(1, 2, part, width), one.reshape(1, 2, part, width)
    ).astype(F32)
    rates = few_sum[5, inner + LANES : inner + LANES + heads] * rate
    return (
        by_layer(firsts, last_out),
        by_layer(first_grad, second_grad),
        few_shared[6:].reshape(1, 2 * wide)[:, inner:],
        large[:, : 2 * inner].reshape(1, -1, 2, inner),
        state_grad[None],
        large[None, :, split : split + heads],
        few_sum[None, :5, :inner],
        few_shared[None, :5, inner:],
        few_sum[5:6, inner : inner + heads],
        rates[None],
        few_sum[6, :inner].reshape(1, heads, -1).sum(2),
        few_sum[5:6, :inner],
        large[None, :, split + LANES :],
    )


def solution(mesh):
    in_specs = (
        P("dp", "tensor", None),
        P("dp", "tensor", None),
        P("pipe", None),
        P("pipe", "dp", None, "tensor"),
        P("pipe", "dp", None),
        P("pipe", "dp", "tensor"),
        P("pipe", None, "tensor"),
        P("pipe", None, None),
        P("pipe", "tensor"),
        P("pipe", "tensor"),
        P("pipe", "tensor"),
        P("pipe", "tensor"),
        P("pipe", "dp", "tensor"),
    )
    out_specs = (
        P("pipe", "dp", "tensor", None),
        P("pipe", "dp", "tensor", None),
        P("pipe", None),
        P("pipe", "dp", None, "tensor"),
        P("pipe", ("dp", "tensor"), None),
        P("pipe", "dp", "tensor"),
        P("pipe", None, "tensor"),
        P("pipe", None, None),
        P("pipe", "tensor"),
        P("pipe", "tensor"),
        P("pipe", "tensor"),
        P("pipe", "tensor"),
        P("pipe", "dp", "tensor"),
    )
    return jax.shard_map(body, mesh=mesh, in_specs=in_specs, out_specs=out_specs, check_vma=False)
```

```python
from functools import partial

import jax
import jax.numpy as jnp
import numpy as np
from jax import lax
from jax.experimental import pallas as pl
from jax.experimental.pallas import tpu as pltpu
from jax.sharding import PartitionSpec as P

F32, BF16 = jnp.float32, jnp.bfloat16
EPS = 1e-05
ROWS = 256
CHUNK = 128
LANES = 128
EXACT = lax.Precision.HIGHEST


def mm(left, right, contract=((1,), (0,))):
    return lax.dot_general(left, right, (contract, ((), ())), preferred_element_type=F32)


def mm_exact(left, right, contract=((1,), (0,))):
    return lax.dot_general(
        left, right, (contract, ((), ())), precision=EXACT, preferred_element_type=F32
    )


def spread(value, selector, heads):
    high = value.astype(BF16).astype(F32)
    both = high + pltpu.roll(value - high, heads, 1)
    return mm(both.astype(BF16), selector)


def per_head(value, collector):
    high = value.astype(BF16)
    low = (value - high.astype(F32)).astype(BF16)
    return mm(high, collector) + mm(low, collector)


def softplus(value):
    small = jnp.exp(-jnp.abs(value))
    series = small * (1.0 - small * (0.5 - small * (1.0 / 3.0 - small * 0.25)))
    return jnp.maximum(value, 0.0) + jnp.where(small < 0.01, series, jnp.log(1.0 + small))


def sigmoid(value):
    return 1.0 / (1.0 + jnp.exp(-value))


def iota(shape, axis):
    return lax.broadcasted_iota(jnp.int32, shape, axis)


def column_to_row(column):
    size = column.shape[0]
    same = iota((size, size), 0) == iota((size, size), 1)
    return jnp.sum(jnp.where(same, column, 0.0), 0, keepdims=True)


def row_to_column(row):
    size = row.shape[1]
    same = iota((size, size), 0) == iota((size, size), 1)
    return jnp.sum(jnp.where(same, row, 0.0), 1, keepdims=True)


def steps(raw, bias, rate, mask):
    delta = softplus(raw + bias) * mask
    tri = (iota((CHUNK, CHUNK), 0) >= iota((CHUNK, CHUNK), 1)).astype(F32)
    log_decay = mm_exact(tri, delta * rate)
    return delta, log_decay


def constants(inner, heads):
    width = inner // heads
    lane = np.arange(LANES)[:, None]
    channel = np.arange(inner)[None, :] // width
    selector = ((lane % heads == channel) & (lane < 2 * heads)).astype(np.float32)
    collector = (lane == channel).astype(np.float32).T
    return jnp.asarray(selector, BF16), jnp.asarray(collector, BF16)


MESH = pl.DeviceIdType.MESH
ANY = pl.BlockSpec(memory_space=pl.ANY)
VMEM = pl.BlockSpec(memory_space=pltpu.VMEM)


def place():
    pipe, dp, x = lax.axis_index("pipe"), lax.axis_index("dp"), lax.axis_index("tensor")
    return (dp // 8) * 2 + pipe, (dp // 2) % 4, dp % 2, x


def at_z(z):
    _, y, core, _ = place()
    return {"pipe": z % 2, "dp": ((z // 2) * 4 + y) * 2 + core}


def at_y(y):
    z, _, core, _ = place()
    return {"dp": ((z // 2) * 4 + y) * 2 + core}


def at_core(core):
    z, y, _, _ = place()
    return {"dp": ((z // 2) * 4 + y) * 2 + core}


def at_x(x):
    return {"tensor": x}


def at_pipe(pipe):
    return {"pipe": pipe}


def greet(*devices):
    barrier = pltpu.get_barrier_semaphore()
    for device in devices:
        pl.semaphore_signal(barrier, inc=1, device_id=device, device_id_type=MESH)
    pl.semaphore_wait(barrier, len(devices))


def around(me, device, steps=(1, 3)):
    return [device((me + step) % 4) for step in steps]


def remote(source, target, sems, index, device):
    return pltpu.make_async_remote_copy(
        src_ref=source,
        dst_ref=target,
        send_sem=sems[0].at[index],
        recv_sem=sems[1].at[index],
        device_id=device,
        device_id_type=MESH,
    )


class RingGather:
    def __init__(self, me, device, own, slot, sems, local=True):
        right, left, across = (me + 1) % 4, (me + 3) % 4, (me + 2) % 4
        to_right, to_left = device(right), device(left)
        self.copies = [
            remote(own(0), slot(me, 0), sems, 0, to_right),
            remote(own(1), slot(me, 1), sems, 1, to_left),
            remote(own(1), slot(me, 1), sems, 2, to_right),
            remote(own(0), slot(me, 0), sems, 3, to_left),
            remote(slot(left, 0), slot(left, 0), sems, 4, to_right),
            remote(slot(right, 1), slot(right, 1), sems, 5, to_left),
        ]
        self.origins = [(left, 0), (right, 1), (left, 1), (right, 0), (across, 0), (across, 1)]
        self.local = [
            pltpu.make_async_copy(own(half), slot(me, half), sems[2].at[half]) for half in range(2 * local)
        ]

    def start(self):
        for copy in self.copies[:4] + self.local:
            copy.start()

    def start_half(self, half):
        for index in ((0, 3), (1, 2))[half]:
            self.copies[index].start()
        self.local[half].start()

    def relay(self):
        for index in range(2):
            self.copies[index].wait_recv()
            self.copies[4 + index].start()

    def wait(self, *indices):
        for index in indices:
            self.copies[index].wait_recv()

    def wait_local(self):
        for copy in self.local:
            copy.wait()

    def wait_sends(self):
        for copy in self.copies:
            copy.wait_send()

    def finish(self):
        self.wait_local()
        self.wait_sends()


class RingScatter:
    def __init__(self, me, device, piece, buffers, sems, near=None):
        self.me, self.right, self.left = me, (me + 1) % 4, (me + 3) % 4
        across = (me + 2) % 4
        self.buffers = buffers
        self.near = near or [piece(me, 0), piece(me, 1), piece(self.right, 0), piece(self.left, 1)]
        relays, sums, arrived = buffers
        to_right, to_left = device(self.right), device(self.left)
        self.copies = [
            remote(piece(across, 0), relays.at[0], sems, 0, to_right),
            remote(piece(across, 1), relays.at[1], sems, 1, to_left),
            remote(piece(self.right, 1), arrived.at[0, 1], sems, 2, to_right),
            remote(piece(self.left, 0), arrived.at[1, 0], sems, 3, to_left),
            remote(sums.at[0], arrived.at[0, 0], sems, 4, to_right),
            remote(sums.at[1], arrived.at[1, 1], sems, 5, to_left),
        ]

    def start(self):
        for copy in self.copies[:4]:
            copy.start()

    def relay(self):
        relays, sums, _ = self.buffers
        for half in range(2):
            self.copies[half].wait_recv()
            total = relays[half].astype(F32) + self.near[2 + half][...].astype(F32)
            sums[half] = total.astype(sums.dtype)
            self.copies[4 + half].start()

    def wait(self):
        for index in range(2, 6):
            self.copies[index].wait_recv()

    def result(self, half):
        arrived = self.buffers[2]
        mine = self.near[half][...].astype(F32)
        return mine + arrived[0, half].astype(F32) + arrived[1, half].astype(F32)

    def finish(self):
        for copy in self.copies:
            copy.wait_send()


class Everyone:
    def __init__(self, me, device, source, target, sems):
        self.copies = [
            remote(source((me + step) % 4), target(me), sems, step - 1, device((me + step) % 4))
            for step in (1, 2, 3)
        ]

    def start(self):
        for copy in self.copies:
            copy.start()

    def wait(self):
        for copy in self.copies:
            copy.wait()


def dma(count):
    return [pltpu.SemaphoreType.DMA((count,)), pltpu.SemaphoreType.DMA((count,))]


def gather_sems():
    return dma(6) + [pltpu.SemaphoreType.DMA((2,))]


def scatter_buffers(*half):
    return [pltpu.VMEM((2,) + half, BF16), pltpu.VMEM((2,) + half, BF16), pltpu.VMEM((2, 2) + half, BF16)]


def norm_scale(value):
    return lax.rsqrt(jnp.mean(value * value, -1, keepdims=True) + EPS)


def norm_gain_of(few, layer, lead):
    return jnp.concatenate([few[layer, 6:7, lead:], few[layer, 7:8, :]], 1)


def remote_params(collective_id):
    return pltpu.CompilerParams(
        collective_id=collective_id, has_side_effects=True, vmem_limit_bytes=56 * 2**20
    )


def owned(block, x, rows):
    return pl.ds(pl.multiple_of(block * ROWS + x * rows, rows), rows)


class BlockSums:
    def __init__(self, x, piece, relays, sums, arrived, sems, op):
        self.right, self.left, self.me = (x + 1) % 4, (x + 3) % 4, x
        across = (x + 2) % 4
        self.piece, self.relays, self.sums, self.arrived = piece, relays, sums, arrived
        at_op = [sem.at[op] for sem in sems]
        to_right, to_left = at_x(self.right), at_x(self.left)
        self.copies = [
            remote(piece(across, 0), relays.at[op, 0], at_op, 0, to_right),
            remote(piece(across, 1), relays.at[op, 1], at_op, 1, to_left),
            remote(piece(self.right, 1), arrived.at[op, 0, 1], at_op, 2, to_right),
            remote(piece(self.left, 0), arrived.at[op, 1, 0], at_op, 3, to_left),
            remote(sums.at[op % 2, 0], arrived.at[op, 0, 0], at_op, 4, to_right),
            remote(sums.at[op % 2, 1], arrived.at[op, 1, 1], at_op, 5, to_left),
        ]
        self.op = op

    def start(self):
        for copy in self.copies[:4]:
            copy.start()

    def relay(self):
        for half, block in ((0, self.right), (1, self.left)):
            self.copies[half].wait_recv()
            total = self.relays[self.op, half].astype(F32) + self.piece(block, half)[...].astype(F32)
            self.sums[self.op % 2, half] = total.astype(BF16)
            self.copies[4 + half].start()

    def wait(self):
        for index in range(2, 6):
            self.copies[index].wait_recv()

    def result(self):
        return jnp.concatenate(
            [
                self.piece(self.me, half)[...].astype(F32)
                + self.arrived[self.op, 0, half].astype(F32)
                + self.arrived[self.op, 1, half].astype(F32)
                for half in range(2)
            ],
            0,
        )

    def finish(self):
        for copy in self.copies:
            copy.wait_send()


def to_everyone(me, device, source, target, sems, op):
    at_op = [sem.at[op] for sem in sems]
    return Everyone(me, device, source, target, at_op)


def columns_of(inner, conv):
    ends = np.cumsum([0, inner, conv, LANES, inner])
    return [slice(int(begin), int(end)) for begin, end in zip(ends[:-1], ends[1:])], int(ends[-1])


def forward_block(sizes, first_block, last_layer, rows, e, w_in, w_out, few, selector, save, save_p, states, part,
                  squares, mixed, state, pad, serve):
    inner, pair, heads = sizes
    states_count = pair // 2
    split = inner + inner + pair
    conv = inner + pair
    (z_at, c_at, raw_at, y_at), _ = columns_of(inner, conv)

    @pl.when(first_block)
    def _():
        state[...] = jnp.zeros_like(state)
        pad[0:8, :] = jnp.zeros((8, conv), F32)

    @pl.when(jnp.logical_not(first_block))
    def _():
        pad[0:8, :] = pad[ROWS : ROWS + 8, :]

    projected = mm(rows, w_in)
    save[:, z_at] = projected[:, :inner]
    save_p[...] = projected[:, inner:split].astype(BF16)
    pad[8 : ROWS + 8, :] = projected[:, inner:split]
    save[:, raw_at] = projected[:, split:]
    bias = few[5:6, inner : inner + LANES]
    rate = few[5:6, inner + LANES : inner + 2 * LANES]
    gain = few[5:6, :inner]
    skip = few[6:7, :inner]
    mask = (iota((1, LANES), 1) < heads).astype(F32)
    first = iota((CHUNK, LANES), 1) < LANES // 2
    causal = iota((CHUNK, CHUNK), 0) >= iota((CHUNK, CHUNK), 1)
    owner_rows = ROWS // 4
    for chunk in range(ROWS // CHUNK):
        at = slice(chunk * CHUNK, (chunk + 1) * CHUNK)
        c = jnp.broadcast_to(few[4:5, :], (CHUNK, conv))
        for tap in range(4):
            begin = chunk * CHUNK + 5 + tap
            c = c + few[tap : tap + 1, :] * pad[begin : begin + CHUNK, :]
        save[at, c_at] = c
        value = c * sigmoid(c)
        xs = value[:, :inner]
        b_low = value[:, inner : inner + states_count].astype(BF16)
        c_low = value[:, inner + states_count :].astype(BF16)
        delta, log_decay = steps(save[at, raw_at], bias, rate, mask)
        turned = log_decay.T
        final = log_decay[CHUNK - 1 : CHUNK, :]
        scaled = spread(delta, selector, heads) * xs
        scaled_low = scaled.astype(BF16)
        products = jnp.where(causal, mm(c_low, b_low, ((1,), (1,))), 0.0)
        within = []
        for two in range(heads // 2):
            lanes = slice(two * LANES, (two + 1) * LANES)
            parts = []
            for h in (2 * two, 2 * two + 1):
                gap = jnp.minimum(log_decay[:, h : h + 1] - turned[h : h + 1, :], 0.0)
                parts.append(mm((products * jnp.exp(gap)).astype(BF16), scaled_low[:, lanes]))
            within.append(jnp.where(first, parts[0], parts[1]))
        old = state[...]
        states[chunk] = old
        carried = mm(c_low, old.astype(BF16)) * spread(jnp.exp(log_decay) * mask, selector, heads)
        y = jnp.concatenate(within, 1) + carried + skip * xs
        save[at, y_at] = y
        ends = (spread(jnp.exp(final - log_decay) * mask, selector, heads) * scaled).astype(BF16)
        keep = spread(jnp.broadcast_to(jnp.exp(final) * mask, (8, LANES)), selector, heads)[0:1]
        state[...] = keep * old + mm(b_low, ends, ((0,), (0,)))
        z = save[at, z_at]
        gated = y * (z * sigmoid(z))
        total = jnp.sum(gated * gated, 1, keepdims=True)
        for piece in range(CHUNK // owner_rows):
            row = column_to_row(total[piece * owner_rows : (piece + 1) * owner_rows])
            squares[chunk * (CHUNK // owner_rows) + piece, 0:1, 0:owner_rows] = row
        mixed[at, :] = (gated * gain).astype(BF16)
        if chunk == 0:
            serve()
    part[...] = mm(mixed[...], w_out(), ((1,), (1,))).astype(BF16)

    @pl.when(last_layer)
    def _():
        total = jnp.sum(mm(e[...], w_out()) * mixed[...].astype(F32), 1, keepdims=True)
        for piece in range(4):
            squares[piece, 1:2, 0:owner_rows] = column_to_row(total[piece * owner_rows : (piece + 1) * owner_rows])


class HandedRing:
    def __init__(self, me, device, source, slot, sems, core_sems):
        _, _, core, _ = place()
        self.slot = lambda origin, half: slot(origin, half, core)
        self.ring = RingGather(me, device, source, self.slot, sems)
        self.pieces = [(source(half), self.slot(me, half), 6 + half) for half in range(2)]
        for index in range(6):
            held = self.slot(*self.ring.origins[index])
            self.pieces.append((held, held, index))
        self.core_sems, self.device = core_sems, at_core(1 - core)

    def hand(self, at):
        source, target, index = self.pieces[at]
        return remote(source, target, self.core_sems, index, self.device)

    def start_half(self, half):
        self.ring.start_half(half)
        self.hand(half).start()

    def start(self):
        for half in range(2):
            self.start_half(half)

    def relay(self):
        self.ring.relay()
        for index in range(2):
            self.hand(2 + index).start()

    def finish(self):
        for index in range(2, 6):
            self.ring.wait(index)
            self.hand(2 + index).start()
        self.ring.finish()
        for at in range(8):
            self.hand(at).wait()


def gather_parameters(sizes, few, shard, gate_x, read_write, step, main, of_state, bias, log_rate, skip, gate, norm):
    inner, pair, heads, lead = sizes
    width = inner // heads
    few[...] = jnp.zeros_like(few)
    for tap in range(5):
        few[tap : tap + 1, :inner] = main[tap]
        few[tap : tap + 1, inner:] = of_state[tap]
    few[5:6, :inner] = gate[...]
    few[5:6, inner : inner + heads] = bias[...]
    few[5:6, inner + LANES : inner + LANES + heads] = -jnp.exp(log_rate[...])
    for head in range(heads):
        few[6:7, head * width : (head + 1) * width] = jnp.broadcast_to(skip[0:1, head : head + 1], (1, width))
    first = few.shape[1] - lead
    few[6:7, lead:] = norm[:, :first]
    few[7:8, :] = norm[:, first:]
    split = 2 * inner + pair
    both = gate_x[...]
    for index in range(2):
        shard[:, index * inner : (index + 1) * inner] = both[:, index, :]
    shard[:, 2 * inner : split] = read_write[0]
    same = (iota((heads, LANES), 0) == iota((heads, LANES), 1)).astype(BF16)
    shard[:, split:] = mm(step[0], same, ((0,), (0,))).astype(BF16)


def forward_all_kernel(sizes, inputs, out_grad, shard_out, gate_x, read_write, step_in, main, of_state, bias, log_rate,
                       skip, gate, norm, selector,
                       few_both, weights_in, weights_out, errors_out, normed, saved, saved_p, states, res, inverses, scales,
                       firsts, last_part,
                       hidden, w_in, w_out, errors, part, relays, sums, arrived, squares, others, stage, p_stage, state_stage,
                       norm_stage, mixed, state, pad, shard_in, z_weights, y_weights, few,
                       xs, xr, xl, es, er, el, zs, zr, zl, ys, yr, yl, cs, cr, y1s, y1r, y1l, c1s, c1r,
                       bs, br, bl, os, og, ol, c2s, c2r, fs, fr, rs, rr, gs, gr, qs, qr, outs, load):
    inner, pair, heads, lead, whole_inner = sizes
    layer_sizes = (inner, pair, heads)
    z, y, core, x = place()
    pipe = z % 2
    quarter = ROWS // 4
    gather_parameters((inner, pair, heads, lead), few.at[pipe], shard_in, gate_x, read_write, step_in, main, of_state,
                      bias, log_rate, skip, gate, norm)
    squares[...] = jnp.zeros_like(squares)
    greet(*around(x, at_x, (1, 2, 3)), *around(y, at_y), *around(z, at_z), at_core(1 - core), at_pipe(1 - pipe))
    few_swap = remote(few.at[pipe], few.at[pipe], (fs, fr), 0, at_pipe(1 - pipe))
    few_swap.start()
    piece = shard_in.shape[0]
    by_half = lambda half: pl.ds(half * (piece // 2), piece // 2)
    z_ring = RingGather(z, at_z, lambda half: shard_in.at[by_half(half)],
                        lambda origin, half: z_weights.at[origin, by_half(half)], (zs, zr, zl))
    z_ring.start()
    y_ring = RingGather(y, at_y, lambda half: shard_out.at[by_half(half)],
                        lambda origin, half: y_weights.at[origin, by_half(half)], (bs, br, bl))
    y_ring.start()
    block_rows = lambda origin, half: pl.ds(pl.multiple_of(origin * ROWS + half * (ROWS // 2), ROWS // 2), ROWS // 2)
    x_ring = RingGather(x, at_x, lambda half: inputs.at[pipe, half],
                        lambda origin, half: hidden.at[0, block_rows(origin, half)], (xs, xr, xl))
    x_ring.start()
    e_ring = RingGather(x, at_x, lambda half: out_grad.at[pipe, half],
                        lambda origin, half: errors.at[block_rows(origin, half)], (es, er, el))

    def in_ring(layer, sems, core_sems):
        away = pipe * (1 - layer) + (1 - pipe) * layer
        from_z = lambda half: (z + 3 * away + 2 * half) % 4
        return HandedRing(
            y, at_y, lambda half: z_weights.at[from_z(half)],
            lambda origin, half, core: w_in.at[layer, from_z(half) // 2, origin, core], sems, core_sems,
        )

    rings = [in_ring(0, (ys, yr, yl), (cs, cr)), in_ring(1, (y1s, y1r, y1l), (c1s, c1r))]
    out_ring = HandedRing(
        z, at_z, lambda half: y_weights.at[pl.ds(2 * half, 2)],
        lambda origin, half, core: w_out.at[origin % 2, origin // 2, pl.ds(2 * half, 2), core],
        (os, og, ol), (c2s, c2r),
    )
    z_ring.wait_local()

    @pl.when(pipe == 0)
    def _():
        rings[0].start_half(0)

    y_ring.relay()
    z_ring.relay()
    z_ring.wait(2)

    @pl.when(pipe == 1)
    def _():
        rings[0].start_half(0)

    z_ring.wait(3)

    @pl.when(pipe == 1)
    def _():
        rings[0].start_half(1)

    y_ring.wait(2, 3, 4, 5)
    y_ring.wait_local()
    out_ring.start()
    z_ring.wait(4, 5)

    @pl.when(pipe == 0)
    def _():
        rings[0].start_half(1)

    x_ring.relay()
    e_ring.start()
    out_ring.relay()
    rings[0].relay()
    z_ring.wait_sends()
    y_ring.wait_sends()
    few_swap.wait()
    few_both[...] = few[...]
    x_ring.wait(2, 3, 4, 5)
    x_ring.finish()
    for block in range(4):
        res[0, block] = hidden[0, owned(block, x, quarter)].astype(F32)
    rings[0].finish()
    rings[1].start()
    def sums_of(op):
        rows = lambda owner, half: part.at[op, pl.ds(pl.multiple_of(owner * quarter + half * (quarter // 2), quarter // 2), quarter // 2)]
        return BlockSums(x, rows, relays, sums, arrived, (rs, rr), op)

    def squares_of(op):
        return to_everyone(x, at_x, lambda to: squares.at[op], lambda me: others.at[op, me], (qs, qr), op)

    def gather_of(block):
        place_of = lambda origin, half: hidden.at[
            1, pl.ds(pl.multiple_of(block * ROWS + origin * quarter + half * (quarter // 2), quarter // 2), quarter // 2)
        ]
        return RingGather(x, at_x, lambda half: place_of(x, half), place_of, (gs.at[block], gr.at[block]), local=False)

    def outs_of(op):
        layer, block = op // 4, op % 4
        slot = op % 2
        at = pl.ds(pl.multiple_of(block * ROWS, ROWS), ROWS)
        count = ROWS // CHUNK
        return [
            pltpu.make_async_copy(stage.at[slot], saved.at[layer, at], outs.at[0, slot]),
            pltpu.make_async_copy(state_stage.at[slot], states.at[layer, pl.ds(block * count, count)], outs.at[1, slot]),
            pltpu.make_async_copy(norm_stage.at[slot], normed.at[layer, at], outs.at[2, slot]),
            pltpu.make_async_copy(p_stage.at[slot], saved_p.at[layer, at], outs.at[3, slot]),
        ]

    def row_sums(op, owner):
        total = others[op, 0, owner, 0:2, :]
        for device in (1, 2, 3):
            total = total + others[op, device, owner, 0:2, :]
        return lax.rsqrt(total[0:1] / whole_inner + EPS), total[1:2]

    def finish_sums(block):
        job = sums_of(block)
        squares_of(block).wait()
        others[block, x] = squares[block]
        inverse, _ = row_sums(block, x)
        inverses[block] = jnp.broadcast_to(inverse, (8, LANES))
        column = row_to_column(inverse)[:quarter]
        job.wait()
        value = res[0, block] + column * job.result()
        job.finish()
        res[1, block] = value
        hidden[1, owned(block, x, quarter)] = value.astype(BF16)
        gather_of(block).start()

    def finish_scales(block):
        squares_of(4 + block).wait()
        others[4 + block, x] = squares[4 + block]
        for owner in range(4):
            inverse, dots = row_sums(4 + block, owner)
            scales[block, owner, 0:1, :] = inverse
            scales[block, owner, 1:2, :] = dots * inverse / whole_inner

    own_block = hidden.at[1, pl.ds(pl.multiple_of(x * ROWS, ROWS), ROWS)]
    ends = [
        pltpu.make_async_copy(w_in.at[0], weights_in.at[0], load.at[0]),
        pltpu.make_async_copy(w_in.at[1], weights_in.at[1], load.at[1]),
        pltpu.make_async_copy(w_out, weights_out, load.at[2]),
        pltpu.make_async_copy(errors, errors_out, load.at[3]),
        pltpu.make_async_copy(own_block, firsts, load.at[4]),
    ]

    def part_copy(block):
        at = pl.ds(pl.multiple_of(block * ROWS, ROWS), ROWS)
        return pltpu.make_async_copy(part.at[4 + block], last_part.at[at], load.at[5 + block])

    def step(op, carry):
        layer, block = op // 4, op % 4

        @pl.when(layer == 1)
        def _():
            job = gather_of(block)
            job.wait(2, 3, 4, 5)
            job.finish()

        @pl.when(op == 7)
        def _():
            ends[4].start()

        @pl.when(op >= 2)
        def _():
            for copy in outs_of(op - 2):
                copy.wait()

        def serve():
            @pl.when(op == 0)
            def _():
                out_ring.finish()

            @pl.when(op == 1)
            def _():
                e_ring.relay()
                rings[1].relay()

            @pl.when((op >= 1) & (op < 5))
            def _():
                sums_of(op - 1).relay()

            @pl.when((op >= 2) & (op < 6))
            def _():
                gather_of(op - 2).relay()

            @pl.when(op == 3)
            def _():
                e_ring.wait(2, 3, 4, 5)
                e_ring.finish()
                rings[1].finish()
                for copy in ends[:4]:
                    copy.start()

            @pl.when(op >= 5)
            def _():
                finish_scales(op - 5)

        slot = op % 2
        at = pl.ds(pl.multiple_of(block * ROWS, ROWS), ROWS)
        value = hidden[layer, at].astype(F32)
        gain = jnp.concatenate([few[layer, 6:7, lead:], few[layer, 7:8, :]], 1)
        norm_stage[slot] = (value * norm_scale(value) * gain).astype(BF16)
        width = value.shape[1]
        forward_block(layer_sizes, block == 0, layer == 1, norm_stage[slot], errors.at[at],
                      w_in[layer].reshape(width, -1), lambda: w_out[layer].reshape(width, -1), few.at[layer], selector[...],
                      stage.at[slot], p_stage.at[slot], state_stage.at[slot], part.at[op], squares.at[op], mixed, state, pad, serve)
        for copy in outs_of(op):
            copy.start()
        squares_of(op).start()

        @pl.when(op < 4)
        def _():
            sums_of(op).start()

        @pl.when(op >= 4)
        def _():
            part_copy(op - 4).start()

        @pl.when((op >= 1) & (op < 5))
        def _():
            finish_sums(op - 1)

        return carry

    lax.fori_loop(0, 8, step, 0)
    finish_scales(3)
    for op in (6, 7):
        for copy in outs_of(op):
            copy.wait()
    for copy in ends:
        copy.wait()
    for block in range(4):
        part_copy(block).wait()


def forward_all(inputs, out_grad, shard_out, gate_x, read_write, step, main, of_state, bias, log_rate, skip, gate, norm,
                inner, pair, heads, whole_inner):
    _, part, width = inputs.shape
    rows = shard_out.shape[0]
    conv = inner + pair
    columns = inner + conv + LANES
    lead = conv - (width - conv)
    length = 4 * part
    _, saved_columns = columns_of(inner, conv)
    quarter = ROWS // 4
    chunks = ROWS // CHUNK
    selector, _ = constants(inner, heads)
    half = (2, 2, part // 2, width)
    shape = jax.ShapeDtypeStruct
    w_in = (2, 2, 4, 2, rows, columns)
    w_out = (2, 2, 4, 2, rows, inner)
    semaphores = lambda *count: [pltpu.SemaphoreType.DMA(count)] * 2
    return pl.pallas_call(
        partial(forward_all_kernel, (inner, pair, heads, lead, whole_inner)),
        out_shape=[
            shape((2, 8, conv), F32),
            shape(w_in, BF16),
            shape(w_out, BF16),
            shape((length, width), BF16),
            shape((2, length, width), BF16),
            shape((2, length, saved_columns), F32),
            shape((2, length, conv), BF16),
            shape((2, length // CHUNK, pair // 2, inner), F32),
            shape((2, 4, quarter, width), F32),
            shape((4, 8, LANES), F32),
            shape((4, 4, 8, LANES), F32),
            shape((part, width), BF16),
            shape((length, width), BF16),
        ],
        in_specs=[ANY, ANY, ANY] + [VMEM] * 11,
        out_specs=[VMEM, ANY, ANY, ANY, ANY, ANY, ANY, ANY, VMEM, VMEM, VMEM, ANY, ANY],
        scratch_shapes=[
            pltpu.VMEM((2, length, width), BF16),
            pltpu.VMEM(w_in, BF16),
            pltpu.VMEM(w_out, BF16),
            pltpu.VMEM((length, width), BF16),
            pltpu.VMEM((8, ROWS, width), BF16),
            pltpu.VMEM((4, 2, quarter // 2, width), BF16),
            pltpu.VMEM((4, 2, quarter // 2, width), BF16),
            pltpu.VMEM((4, 2, 2, quarter // 2, width), BF16),
            pltpu.VMEM((8, 4, 8, LANES), F32),
            pltpu.VMEM((8, 4, 4, 8, LANES), F32),
            pltpu.VMEM((2, ROWS, saved_columns), F32),
            pltpu.VMEM((2, ROWS, conv), BF16),
            pltpu.VMEM((2, chunks, pair // 2, inner), F32),
            pltpu.VMEM((2, ROWS, width), BF16),
            pltpu.VMEM((ROWS, inner), BF16),
            pltpu.VMEM((pair // 2, inner), F32),
            pltpu.VMEM((ROWS + 8, conv), F32),
            pltpu.VMEM((rows, columns), BF16),
            pltpu.VMEM((4, rows, columns), BF16),
            pltpu.VMEM((4, rows, inner), BF16),
            pltpu.VMEM((2, 8, conv), F32),
        ]
        + gather_sems() * 3
        + (gather_sems() + dma(8)) * 2
        + gather_sems()
        + gather_sems() + dma(8)
        + dma(1)
        + semaphores(4, 6) + semaphores(4, 6) + semaphores(8, 3)
        + [pltpu.SemaphoreType.DMA((4, 2)), pltpu.SemaphoreType.DMA((9,))],
        compiler_params=remote_params(0),
        name="forward_layers",
    )(inputs.reshape(half), out_grad.reshape(half), shard_out, gate_x, read_write, step, main, of_state, bias, log_rate,
      skip, gate, norm, selector)


class Deliver:
    def __init__(self, layer, source, target, sends, recvs, local):
        self.layer, self.source, self.target = layer, source, target
        self.sends, self.recvs, self.local_sem = sends, recvs, local
        z, _, _, self.x = place()
        self.pipe = z % 2
        self.here = self.pipe == layer

    def copy(self, step, pipe, device_pipe, block):
        return pltpu.make_async_remote_copy(
            src_ref=self.source.at[block],
            dst_ref=self.target.at[pipe, self.x],
            send_sem=self.sends.at[step],
            recv_sem=self.recvs.at[pipe * 4 + step],
            device_id={"pipe": device_pipe, "tensor": block},
            device_id_type=MESH,
        )

    def out(self, step):
        return self.copy(step, self.pipe, self.layer, (self.x + step) % 4)

    def local(self):
        return pltpu.make_async_copy(self.source.at[self.x], self.target.at[self.pipe, self.x], self.local_sem)

    def start(self):
        for step in (1, 2, 3):
            self.out(step).start()

        @pl.when(self.here)
        def _():
            self.local().start()

        @pl.when(jnp.logical_not(self.here))
        def _():
            self.out(0).start()

    def wait(self):
        for step in (1, 2, 3):
            self.out(step).wait_send()

        @pl.when(self.here)
        def _():
            self.local().wait()
            for step in (1, 2, 3):
                self.out(step).wait_recv()
            for step in range(4):
                self.copy(step, 1 - self.pipe, 1 - self.pipe, self.x).wait_recv()

        @pl.when(jnp.logical_not(self.here))
        def _():
            self.out(0).wait_send()


def both_pipes(x, pipe):
    return [{"pipe": 1 - pipe, "tensor": (x + step) % 4} for step in range(4)]


class CoreSum:
    def __init__(self, grads, arrived, sems):
        _, _, core, _ = place()
        self.grads, self.arrived, self.core = grads, arrived, core
        self.pieces = [(y, half) for y in range(4) for half in range(2)]
        self.sems = sems

    def copy(self, index):
        y, half = self.pieces[index]
        source = self.grads.at[half, y, 1 - self.core]
        return remote(source, self.arrived.at[y, half], self.sems, index, at_core(1 - self.core))

    def start(self):
        for index in range(8):
            self.copy(index).start()

    def finish(self):
        for index, (y, half) in enumerate(self.pieces):
            self.copy(index).wait_recv()
            value = self.grads[half, y, self.core].astype(F32) + self.arrived[y, half].astype(F32)
            self.grads[half, y, self.core] = value.astype(BF16)
        for index in range(8):
            self.copy(index).wait_send()


def back_through_norm(value, grad_out, summed, gain):
    scale = norm_scale(value)
    unit = value * scale
    scaled = summed * gain
    mean = jnp.mean(scaled * unit, -1, keepdims=True)
    return grad_out + scale * (scaled - unit * mean), jnp.sum(summed * unit, 0, keepdims=True)


def backward_block(sizes, first_block, e, scales, w_in, w_out, few, selector, collector, saved, saved_p, states,
                   part, grad, mixed, few_out, state, later, pad, serve):
    inner, pair, heads = sizes
    states_count = pair // 2
    split = inner + inner + pair
    conv = inner + pair
    quarter = ROWS // 4
    (z_at, c_at, raw_at, y_at), _ = columns_of(inner, conv)

    @pl.when(first_block)
    def _():
        state[...] = jnp.zeros_like(state)
        later[...] = jnp.zeros_like(later)
        pad[ROWS : ROWS + 8, :] = jnp.zeros((8, conv), F32)

    @pl.when(jnp.logical_not(first_block))
    def _():
        pad[ROWS : ROWS + 8, :] = pad[0:8, :]

    bias = few[5:6, inner : inner + LANES]
    rate = few[5:6, inner + LANES : inner + 2 * LANES]
    gain = few[5:6, :inner]
    skip = few[6:7, :inner]
    mask = (iota((1, LANES), 1) < heads).astype(F32)
    first = iota((CHUNK, LANES), 1) < LANES // 2
    later_in = iota((CHUNK, CHUNK), 1) >= iota((CHUNK, CHUNK), 0)
    last = iota((CHUNK, LANES), 0) == CHUNK - 1
    tri = later_in.astype(F32)
    column = lambda row: jnp.concatenate(
        [row_to_column(scales[owner, row : row + 1, :])[:quarter] for owner in range(4)], 0
    )
    inverse = column(0)
    inner_dot = column(1)
    mixed_grad = mm(e, w_out)
    for chunk in reversed(range(ROWS // CHUNK)):
        at = slice(chunk * CHUNK, (chunk + 1) * CHUNK)
        z = saved[at, z_at]
        y = saved[at, y_at]
        sig = sigmoid(z)
        act = z * sig
        g = y * act * inverse[at]
        mixed[at, :] = (g * gain).astype(BF16)
        mixed_here = mixed_grad[at]
        gated_grad = inverse[at] * (mixed_here * gain - g * inner_dot[at])
        dy = gated_grad * act
        grad[at, :inner] = (gated_grad * y * (sig * (1.0 + z - act))).astype(BF16)
        c = saved[at, c_at]
        csig = sigmoid(c)
        value = c * csig
        slope = csig * (1.0 + c - value)
        xs = value[:, :inner]
        b_low = value[:, inner : inner + states_count].astype(BF16)
        c_low = value[:, inner + states_count :].astype(BF16)
        raw = saved[at, raw_at]
        delta, log_decay = steps(raw, bias, rate, mask)
        turned = log_decay.T
        final = log_decay[CHUNK - 1 : CHUNK, :]
        wide_delta = spread(delta, selector, heads)
        scaled = wide_delta * xs
        scaled_low = scaled.astype(BF16)
        dy_low = dy.astype(BF16)
        products = jnp.where(later_in, mm(b_low, c_low, ((1,), (1,))), 0.0)
        dproducts = jnp.zeros((CHUNK, CHUNK), F32)
        within = []
        for two in range(heads // 2):
            lanes = slice(two * LANES, (two + 1) * LANES)
            parts = []
            for odd in range(2):
                h = 2 * two + odd
                mine = first if odd == 0 else ~first
                decay = jnp.exp(jnp.minimum(turned[h : h + 1, :] - log_decay[:, h : h + 1], 0.0))
                parts.append(mm((products * decay).astype(BF16), dy_low[:, lanes]))
                own = jnp.where(mine, scaled_low[:, lanes], jnp.zeros((), BF16))
                dproducts = dproducts + decay * mm(own, dy_low[:, lanes], ((1,), (1,)))
            within.append(jnp.where(first, parts[0], parts[1]))
        dproducts = jnp.where(later_in, dproducts, 0.0).astype(BF16)
        old = states[chunk]
        old_low = old.astype(BF16)
        dstate = state[...]
        dstate_low = dstate.astype(BF16)
        to_end = spread(jnp.exp(final - log_decay) * mask, selector, heads)
        from_start = (spread(jnp.exp(log_decay) * mask, selector, heads) * dy).astype(BF16)
        dscaled = jnp.concatenate(within, 1) + to_end * mm(b_low, dstate_low)
        dc_state = mm(from_start, old_low, ((1,), (1,))) + mm(dproducts, b_low, ((0,), (0,)))
        db_state = mm((to_end * scaled).astype(BF16), dstate_low, ((1,), (1,))) + mm(dproducts, c_low)
        carry = jnp.broadcast_to(jnp.sum(later[...] * dstate, 0, keepdims=True), (8, inner))
        carry = per_head(carry, collector)[0:1]
        keep = spread(jnp.broadcast_to(jnp.exp(final) * mask, (8, LANES)), selector, heads)[0:1]
        state[...] = keep * dstate + mm(c_low, from_start, ((0,), (0,)))
        later[...] = old
        flow = dy_low.astype(F32) * (y - skip * xs) - scaled_low.astype(F32) * dscaled
        dlog = per_head(flow, collector) + jnp.where(last, carry, 0.0)
        dstep = mm_exact(tri, dlog)
        ddelta = per_head(xs * dscaled, collector) + rate * dstep
        draw = ddelta * sigmoid(raw + bias) * mask
        few_out[5:6, inner : inner + LANES] += jnp.sum(draw, 0, keepdims=True)
        few_out[5:6, inner + LANES : inner + 2 * LANES] += jnp.sum(delta * dstep, 0, keepdims=True)
        few_out[5:6, :inner] += jnp.sum(mixed_here * g, 0, keepdims=True)
        few_out[6:7, :inner] += jnp.sum(dy * xs, 0, keepdims=True)
        dxs = wide_delta * dscaled + skip * dy
        pad[at, :] = jnp.concatenate([dxs, db_state, dc_state], 1) * slope
        grad[at, split:] = draw.astype(BF16)
        if chunk == ROWS // CHUNK - 1:
            serve()
    for chunk in range(ROWS // CHUNK):
        at = slice(chunk * CHUNK, (chunk + 1) * CHUNK)
        p = saved_p[at, :].astype(F32)
        total = jnp.zeros((CHUNK, conv), F32)
        for tap in range(4):
            begin = chunk * CHUNK + 3 - tap
            shifted = pad[begin : begin + CHUNK, :]
            total = total + few[tap : tap + 1, :] * shifted
            few_out[tap : tap + 1, :] += jnp.sum(p * shifted, 0, keepdims=True)
        few_out[4:5, :] += jnp.sum(pad[at, :], 0, keepdims=True)
        grad[at, inner:split] = total.astype(BF16)
    part[...] = mm(grad[...], w_in, ((1,), (1,))).astype(BF16)


class WeightParts:
    def __init__(self, refs):
        (self.columns, self.low, self.core, self.y, self.z, self.middle, self.z_blocks, self.core_sems, self.y_sems,
         self.z_sems) = refs

    @staticmethod
    def scratch(piece, columns):
        grads = pltpu.VMEM((4, 2, piece, columns), BF16)
        return [
            [
                pltpu.VMEM((2, 4, 2, piece, columns), BF16),
                grads,
                scatter_buffers(piece, columns),
                scatter_buffers(piece // 2, columns),
                pltpu.VMEM((2, piece, columns), BF16),
                pltpu.VMEM((4, 2, piece // 2, columns), BF16),
            ],
            [[dma(8), dma(8)], [dma(6), dma(6)], dma(6)],
        ]

    def flush(self, total):
        piece = total.shape[0] // 16
        for index in range(16):
            z_hi, y_at, core_at = index // 8, (index // 2) % 4, index % 2
            self.low[z_hi, y_at, core_at] = total[index * piece : (index + 1) * piece, self.columns].astype(BF16)

    def core_sum(self, layer):
        return CoreSum(self.low, self.core, self.core_sems[layer])

    def y_sum(self, layer):
        _, y, core, _ = place()
        return RingScatter(y, at_y, lambda owner, half: self.low.at[half, owner, core], self.y, self.y_sems[layer])

    def z_sum(self):
        z, _, _, _ = place()
        return RingScatter(z, at_z, lambda owner, half: self.z_blocks.at[owner, half], self.z, self.z_sems)

    def to_z(self, sums):
        rows = self.z_blocks.shape[2]
        for z_hi in range(2):
            first = sums.result(z_hi).astype(BF16)
            second = self.middle[z_hi]
            for half in range(2):
                self.z_blocks[2 * z_hi, half] = first[half * rows : (half + 1) * rows]
                self.z_blocks[2 * z_hi + 1, half] = second[half * rows : (half + 1) * rows]


def flat(tree):
    return jax.tree.leaves(tree)


def backward_all_kernel(sizes, errors_later, scales_later, weights_in, weights_out, few, selector, collector, normed,
                        saved, saved_p, states, res, inverses, first_own, last_part,
                        firsts, last_out, first_grad, second_grad, large, few_sum, few_shared, state_grad,
                        errors, scales, w_in, w_out, part, relays, sums, arrived, stage, p_stage, state_stage,
                        norm_stage, e_stage, grad, mixed, own_scales, own_grad, low_grad, few_grad, norm_grad, total,
                        t0, t1, t2, last_held, first_rows, pair_few, y_few, z_few, x_few, state_parts, state, later, pad,
                        rs, rr, gs, gr, ss, sr, ts, tr, ls, lr, ps, pr, fs, fr, hs, hr, js, jr, ks, kr, ws, wr, is_, ig,
                        loads, load, core_free, y_free, *rest):
    inner, pair, heads, lead, whole_inner = sizes
    layer_sizes = (inner, pair, heads)
    z, y, core, x = place()
    pipe = z % 2
    every = (1, 2, 3)
    quarter = ROWS // 4
    split = 2 * inner + pair
    ends = (slice(2 * inner, total.shape[1]), slice(0, 2 * inner))
    layout = [WeightParts.scratch(total.shape[0] // 16, at.stop - at.start) for at in ends]
    refs = iter(rest)
    memory = [jax.tree.map(lambda _: next(refs), of_part[0]) for of_part in layout]
    signals = [jax.tree.map(lambda _: next(refs), of_part[1]) for of_part in layout]
    parts = [WeightParts([at] + held + sems) for at, held, sems in zip(ends, memory, signals)]

    block_rows = lambda owner, half: pl.ds(pl.multiple_of(owner * ROWS + half * (ROWS // 2), ROWS // 2), ROWS // 2)

    def at_step(op):
        return 1 - op // 4, 3 - op % 4

    def loads_of(op):
        layer, block = at_step(op)
        slot = op % 2
        at = pl.ds(pl.multiple_of(block * ROWS, ROWS), ROWS)
        count = ROWS // CHUNK
        return [
            pltpu.make_async_copy(saved.at[layer, at], stage.at[slot], loads.at[0, slot]),
            pltpu.make_async_copy(states.at[layer, pl.ds(block * count, count)], state_stage.at[slot], loads.at[1, slot]),
            pltpu.make_async_copy(normed.at[layer, at], norm_stage.at[slot], loads.at[2, slot]),
            pltpu.make_async_copy(saved_p.at[layer, at], p_stage.at[slot], loads.at[3, slot]),
        ]

    def weight_loads(layer):
        return [
            pltpu.make_async_copy(weights_in.at[layer], w_in.at[layer], load.at[layer]),
            pltpu.make_async_copy(weights_out.at[layer], w_out.at[layer], load.at[6 + layer]),
        ]

    def error_load(op):
        _, block = at_step(op)
        at = pl.ds(pl.multiple_of(block * ROWS, ROWS), ROWS)
        return pltpu.make_async_copy(errors_later.at[at], e_stage.at[op % 2], loads.at[4, op % 2])

    own_loads = [
        pltpu.make_async_copy(errors_later.at[owned(block, x, quarter)], low_grad.at[block], load.at[9 + block])
        for block in range(4)
    ]
    sum_loads = [
        pltpu.make_async_copy(last_part.at[block_rows(owner, half)], last_held.at[index], load.at[13 + index])
        for index, (owner, half) in enumerate(((x, 0), (x, 1), ((x + 1) % 4, 0), ((x + 3) % 4, 1)))
    ]
    error_load(0).start()
    for copy in weight_loads(1) + loads_of(0):
        copy.start()
    first_load = pltpu.make_async_copy(first_own, first_rows, load.at[8])
    first_load.start()
    for copy in own_loads + sum_loads + weight_loads(0):
        copy.start()
    greet(*around(x, at_x, every), *around(y, at_y, every), *around(z, at_z, every), at_core(1 - core),
          *both_pipes(x, pipe))
    last_sums = RingScatter(x, at_x, lambda owner, half: last_part.at[block_rows(owner, half)], (t0, t1, t2), (ts, tr),
                            [last_held.at[index] for index in range(4)])
    first_copy = pltpu.make_async_copy(first_own, firsts.at[pipe], load.at[2])
    first_swap = remote(first_own, firsts.at[pipe], (ps, pr), 1, at_pipe(1 - pipe))
    first_copy.start()
    first_swap.start()
    scales[1] = scales_later[...]
    few_grad[...] = jnp.zeros_like(few_grad)
    norm_grad[...] = jnp.zeros_like(norm_grad)
    own_scales[...] = jnp.zeros_like(own_scales)
    total[...] = jnp.zeros_like(total)
    for block, copy in enumerate(own_loads):
        copy.wait()
        own_grad[block] = low_grad[block].astype(F32)
    for copy in sum_loads:
        copy.wait()
    for copy in weight_loads(1):
        copy.wait()

    def sums_of(op):
        rows = lambda owner, half: part.at[
            op % 3, pl.ds(pl.multiple_of(owner * quarter + half * (quarter // 2), quarter // 2), quarter // 2)
        ]
        return BlockSums(x, rows, relays, sums, arrived, (rs, rr), op)

    def gather_of(block):
        place_of = lambda origin, half: errors.at[
            pl.ds(pl.multiple_of(block * ROWS + origin * quarter + half * (quarter // 2), quarter // 2), quarter // 2)
        ]
        return RingGather(x, at_x, lambda half: place_of(x, half), place_of, (gs.at[block], gr.at[block]), local=False)

    def scales_of(block):
        return to_everyone(x, at_x, lambda to: own_scales.at[block], lambda me: scales.at[0, block, me], (ss, sr), block)

    def finish_sums(op):
        layer, block = at_step(op)
        job = sums_of(op)
        job.wait()
        gain = jnp.concatenate([few[layer, 6:7, lead:], few[layer, 7:8, :]], 1)
        value, gain_part = back_through_norm(res[layer, block], own_grad[block], job.result(), gain)
        own_grad[block] = value
        norm_grad[layer, 0:1, :] += gain_part
        low = value.astype(BF16)
        job.finish()

        @pl.when(layer == 1)
        def _():
            errors[owned(block, x, quarter)] = low
            gather_of(block).start()
            dots = jnp.sum(low.astype(F32) * (res[1, block] - res[0, block]), -1, keepdims=True) / whole_inner
            own_scales[block, 0:1, :] = inverses[block, 0:1, :]
            own_scales[block, 1:2, 0:quarter] = column_to_row(dots)
            scales[0, block, x] = own_scales[block]
            scales_of(block).start()

        @pl.when(layer == 0)
        def _():
            low_grad[block] = low

    own_block = errors.at[pl.ds(pl.multiple_of(x * ROWS, ROWS), ROWS)]
    second_copy = pltpu.make_async_copy(own_block, second_grad.at[pipe], load.at[4])
    swap = remote(own_block, second_grad.at[pipe], (ps, pr), 0, at_pipe(1 - pipe))

    last_copy = pltpu.make_async_copy(first_rows, last_out.at[pipe], load.at[3])
    last_swap = remote(first_rows, last_out.at[pipe], (ls, lr), 0, at_pipe(1 - pipe))

    def finish_last():
        last_sums.wait()
        first_load.wait()
        column = jnp.concatenate(
            [row_to_column(scales_later[x, owner, 0:1, :])[:quarter] for owner in range(4)], 0
        )
        for half in range(2):
            at = slice(half * (ROWS // 2), (half + 1) * (ROWS // 2))
            first_rows[at, :] = (first_rows[at, :].astype(F32) + column[at] * last_sums.result(half)).astype(BF16)
        last_sums.finish()
        last_copy.start()
        last_swap.start()

    def step(op, carry):
        layer, block = at_step(op)
        slot = op % 2

        @pl.when(layer == 0)
        def _():
            job = gather_of(block)
            job.wait(2, 3, 4, 5)
            job.finish()
            scales_of(block).wait()

        @pl.when(op == 4)
        def _():
            for copy in weight_loads(0):
                copy.wait()

        @pl.when(op == 7)
        def _():
            second_copy.start()
            swap.start()

        for copy in loads_of(op):
            copy.wait()

        @pl.when(op < 7)
        def _():
            for copy in loads_of(op + 1):
                copy.start()

        at = pl.ds(pl.multiple_of(block * ROWS, ROWS), ROWS)

        @pl.when(layer == 0)
        def _():
            e_stage[slot] = errors[at]

        @pl.when(layer == 1)
        def _():
            error_load(op).wait()

        @pl.when(op < 3)
        def _():
            error_load(op + 1).start()

        e = e_stage[slot]
        def serve():
            @pl.when(op >= 1)
            def _():
                sums_of(op - 1).relay()

            @pl.when((op >= 2) & (op < 6))
            def _():
                gather_of(5 - op).relay()

            @pl.when(op == 4)
            def _():
                for of_part in parts:
                    of_part.core_sum(1).finish()
                    of_part.y_sum(1).start()
                pl.semaphore_signal(core_free, inc=1, device_id=at_core(1 - core), device_id_type=MESH)

            @pl.when(op == 5)
            def _():
                for of_part in parts:
                    of_part.y_sum(1).relay()

            @pl.when(op == 6)
            def _():
                for of_part in parts:
                    job = of_part.y_sum(1)
                    job.wait()
                    for half in range(2):
                        of_part.middle[half] = job.result(half).astype(BF16)
                    job.finish()
                for device in around(y, at_y):
                    pl.semaphore_signal(y_free, inc=1, device_id=device, device_id_type=MESH)

        backward_block(layer_sizes, block == 3, e, scales.at[layer, block], w_in[layer].reshape(e.shape[1], -1),
                       w_out[layer].reshape(e.shape[1], -1), few.at[layer],
                       selector[...], collector[...], stage.at[slot], p_stage.at[slot], state_stage.at[slot],
                       part.at[op % 3], grad, mixed, few_grad.at[layer], state, later, pad, serve)
        sums_of(op).start()

        @pl.when(op >= 1)
        def _():
            finish_sums(op - 1)

        turn = ((0,), (0,))
        wide = split + LANES
        for index in range(total.shape[0] // ROWS):
            rows = slice(index * ROWS, (index + 1) * ROWS)
            total[rows, :wide] += mm(norm_stage[slot, :, rows], grad[...], turn)
            total[rows, wide:] += mm(e_stage[slot, :, rows], mixed[...], turn)

        @pl.when(op == 3)
        def _():
            for of_part in parts:
                of_part.flush(total)
                of_part.core_sum(1).start()
            total[...] = jnp.zeros_like(total)

        return carry

    lax.fori_loop(0, 8, step, 0)
    pl.semaphore_wait(core_free, 1)
    for of_part in parts:
        of_part.flush(total)
        of_part.core_sum(0).start()
    pl.semaphore_wait(y_free, 2)
    last_sums.start()
    sums_of(7).relay()
    y_sums = [of_part.y_sum(0) for of_part in parts]
    z_sums = [of_part.z_sum() for of_part in parts]
    for of_part, job in zip(parts, y_sums):
        of_part.core_sum(0).finish()
        job.start()
    finish_sums(7)
    gradient = Deliver(0, low_grad, first_grad, is_, ig, load.at[5])
    gradient.start()
    for layer in range(2):
        width = few_grad.shape[2] - lead
        few_grad[layer, 6:7, lead:] = norm_grad[layer, 0:1, :width]
        few_grad[layer, 7:8, :] = norm_grad[layer, 0:1, width:]
    few_core = remote(few_grad, pair_few, (fs, fr), 0, at_core(1 - core))
    few_core.start()
    y_sums[0].relay()
    few_core.wait()
    few_grad[...] = few_grad[...] + pair_few[...]
    few_y = Everyone(y, at_y, lambda to: few_grad, lambda me: y_few.at[me], (hs, hr))
    few_y.start()
    last_sums.relay()
    y_sums[0].wait()
    parts[0].to_z(y_sums[0])
    z_sums[0].start()
    y_sums[1].relay()
    few_y.wait()
    y_few[y] = few_grad[...]
    few_grad[...] = (y_few[0] + y_few[1]) + (y_few[2] + y_few[3])
    few_z = Everyone(z, at_z, lambda to: few_grad.at[to % 2], lambda me: z_few.at[me], (js, jr))
    few_z.start()
    z_sums[0].relay()
    few_z.wait()
    z_few[z] = few_grad[pipe]
    few_sum[...] = (z_few[0] + z_few[1]) + (z_few[2] + z_few[3])
    x_few[x] = few_sum[...]
    few_x = Everyone(x, at_x, lambda to: few_sum, lambda me: x_few.at[me], (ks, kr))
    few_x.start()
    finish_last()
    z_sums[0].wait()
    rows = parts[0].z_blocks.shape[2]
    for half in range(2):
        large[half * rows : (half + 1) * rows, ends[0]] = z_sums[0].result(half)
    state_rows = 2 * rows // 4
    for block in range(4):
        state_parts[0, block] = large[block * state_rows : (block + 1) * state_rows, 2 * inner : split]
    state_x = Everyone(x, at_x, lambda to: state_parts.at[0, to], lambda me: state_parts.at[1, me], (ws, wr))
    state_x.start()
    y_sums[1].wait()
    parts[1].to_z(y_sums[1])
    z_sums[1].start()
    few_x.wait()
    few_shared[...] = (x_few[0] + x_few[1]) + (x_few[2] + x_few[3])
    state_x.wait()
    total_state = state_parts[0, x]
    for step_at in every:
        total_state = total_state + state_parts[1, (x + step_at) % 4]
    state_grad[...] = total_state
    z_sums[1].relay()
    second_copy.wait()
    swap.wait()
    first_copy.wait()
    first_swap.wait()
    last_copy.wait()
    last_swap.wait()
    gradient.wait()
    z_sums[1].wait()
    for half in range(2):
        large[half * rows : (half + 1) * rows, ends[1]] = z_sums[1].result(half)
    for job in y_sums + z_sums:
        job.finish()


def backward_all(errors, scales, weights_in, weights_out, few, normed, saved, saved_p, states, res, inverses, first_own, last_part,
                 inner, pair, heads, whole_inner):
    length, width = errors.shape
    _, blocks, quarter, _ = res.shape
    conv = inner + pair
    lead = conv - (width - conv)
    split = 2 * inner + pair
    piece = weights_in.shape[4]
    layout = [WeightParts.scratch(piece, pair + LANES + inner), WeightParts.scratch(piece, 2 * inner)]
    columns = weights_in.shape[5] + inner
    chunks = ROWS // CHUNK
    selector, collector = constants(inner, heads)
    shape = jax.ShapeDtypeStruct
    delivered = shape((2, blocks, quarter, width), BF16)
    few_shape = few.shape[1:]
    half = (quarter // 2, width)
    semaphores = lambda *count: [pltpu.SemaphoreType.DMA(count)] * 2
    return pl.pallas_call(
        partial(backward_all_kernel, (inner, pair, heads, lead, whole_inner)),
        out_shape=[
            shape((2, blocks * quarter, width), BF16),
            shape((2, blocks * quarter, width), BF16),
            delivered,
            shape((2, blocks * quarter, width), BF16),
            shape((piece, columns), F32),
            shape(few_shape, F32),
            shape(few_shape, F32),
            shape((piece // 4, pair), F32),
        ],
        in_specs=[ANY, VMEM, ANY, ANY, VMEM, VMEM, VMEM, ANY, ANY, ANY, ANY, VMEM, VMEM, ANY, ANY],
        out_specs=[ANY, ANY, ANY, ANY, VMEM, VMEM, VMEM, VMEM],
        scratch_shapes=[
            pltpu.VMEM((length, width), BF16),
            pltpu.VMEM((2, blocks, 4, 8, LANES), F32),
            pltpu.VMEM(weights_in.shape, BF16),
            pltpu.VMEM(weights_out.shape, BF16),
            pltpu.VMEM((3, ROWS, width), BF16),
            pltpu.VMEM((8, 2) + half, BF16),
            pltpu.VMEM((2, 2) + half, BF16),
            pltpu.VMEM((8, 2, 2) + half, BF16),
            pltpu.VMEM((2, ROWS, saved.shape[2]), F32),
            pltpu.VMEM((2, ROWS, conv), BF16),
            pltpu.VMEM((2, chunks, pair // 2, inner), F32),
            pltpu.VMEM((2, ROWS, width), BF16),
            pltpu.VMEM((2, ROWS, width), BF16),
            pltpu.VMEM((ROWS, split + LANES), BF16),
            pltpu.VMEM((ROWS, inner), BF16),
            pltpu.VMEM((blocks, 8, LANES), F32),
            pltpu.VMEM((blocks, quarter, width), F32),
            pltpu.VMEM((blocks, quarter, width), BF16),
            pltpu.VMEM((2,) + few_shape, F32),
            pltpu.VMEM((2, 8, width), F32),
            pltpu.VMEM((width, columns), F32),
        ]
        + scatter_buffers(ROWS // 2, width)
        + [
            pltpu.VMEM((4, ROWS // 2, width), BF16),
            pltpu.VMEM((ROWS, width), BF16),
            pltpu.VMEM((2,) + few_shape, F32),
            pltpu.VMEM((4, 2) + few_shape, F32),
            pltpu.VMEM((4,) + few_shape, F32),
            pltpu.VMEM((4,) + few_shape, F32),
            pltpu.VMEM((2, 4, piece // 4, pair), F32),
            pltpu.VMEM((pair // 2, inner), F32),
            pltpu.VMEM((pair // 2, inner), F32),
            pltpu.VMEM((ROWS + 8, conv), F32),
        ]
        + semaphores(8, 6) + semaphores(4, 6) + semaphores(4, 3)
        + dma(6) + dma(1) + dma(2) + dma(1) + dma(3) + dma(3) + dma(3) + dma(3)
        + [pltpu.SemaphoreType.DMA((4,)), pltpu.SemaphoreType.DMA((8,))]
        + [pltpu.SemaphoreType.DMA((5, 2)), pltpu.SemaphoreType.DMA((17,))]
        + [pltpu.SemaphoreType.REGULAR, pltpu.SemaphoreType.REGULAR]
        + flat([of_part[0] for of_part in layout])
        + flat([of_part[1] for of_part in layout]),
        compiler_params=pltpu.CompilerParams(collective_id=1, has_side_effects=True, vmem_limit_bytes=62 * 2**20),
        name="backward_layers",
    )(errors, scales, weights_in, weights_out, few, selector, collector, normed, saved, saved_p, states, res, inverses,
      first_own, last_part)


def finish_kernel(sizes, firsts, last_out, first_grad, second_grad, large, few_sum, few_shared, state_grad, few,
                  activations, input_grads, norm, gate_x, read_write, step, main, of_state, bias, rates, skip, gate,
                  out_weight):
    inner, pair, heads, lead = sizes
    first = lax.axis_index("pipe") == 0
    activations[0] = jnp.where(first, firsts[...], last_out[...]).astype(F32)
    input_grads[0] = jnp.where(first, first_grad[...], second_grad[...]).astype(F32)
    split = 2 * inner + pair

    @pl.when(pl.program_id(0) == 0)
    def _():
        norm[:, : few_shared.shape[1] - lead] = few_shared[6:7, lead:]
        norm[:, few_shared.shape[1] - lead :] = few_shared[7:8, :]
        for index in range(2):
            gate_x[0, :, index, :] = large[:, index * inner : (index + 1) * inner]
        read_write[0] = state_grad[...]
        step[0] = mm_exact((iota((heads, LANES), 0) == iota((heads, LANES), 1)).astype(F32),
                           large[:, split : split + LANES], ((1,), (1,)))
        for tap in range(5):
            main[tap] = few_sum[tap : tap + 1, :inner]
            of_state[tap] = few_shared[tap : tap + 1, inner:]
        bias[...] = few_sum[5:6, inner : inner + heads]
        rate = jnp.where(first, few[0, 5:6, inner + LANES :], few[1, 5:6, inner + LANES :])
        rates[...] = (few_sum[5:6, inner + LANES :] * rate)[:, :heads]
        width = inner // heads
        skip[...] = jnp.concatenate(
            [jnp.sum(few_sum[6:7, head * width : (head + 1) * width], 1, keepdims=True) for head in range(heads)], 1
        )
        gate[...] = few_sum[5:6, :inner]
        out_weight[0] = large[:, split + LANES :]


def finish_call(firsts, last_out, first_grad, second_grad, large, few_sum, few_shared, state_grad, few, inner, pair, heads):
    two, part, width = firsts.shape
    conv = few.shape[2]
    lead = conv - (width - conv)
    rows = part // 4
    piece = large.shape[0]
    by_rows = pl.BlockSpec((two, rows, width), lambda i: (0, i, 0))
    out_rows = pl.BlockSpec((1, two, rows, width), lambda i: (0, 0, i, 0))
    shape = lambda *sizes: jax.ShapeDtypeStruct(sizes, F32)
    small = [
        shape(1, width),
        shape(1, piece, 2, inner),
        shape(1, piece // 4, pair),
        shape(1, heads, piece),
        shape(5, 1, inner),
        shape(5, 1, pair),
        shape(1, heads),
        shape(1, heads),
        shape(1, heads),
        shape(1, inner),
        shape(1, piece, inner),
    ]
    return pl.pallas_call(
        partial(finish_kernel, (inner, pair, heads, lead)),
        grid=(4,),
        in_specs=[by_rows] * 4 + [whole(item) for item in (large, few_sum, few_shared, state_grad, few)],
        out_specs=[out_rows] * 2 + [whole(item) for item in small],
        out_shape=[shape(1, two, part, width)] * 2 + small,
        compiler_params=pltpu.CompilerParams(vmem_limit_bytes=60 * 2**20),
        name="outputs",
    )(firsts, last_out, first_grad.reshape(firsts.shape), second_grad, large, few_sum, few_shared, state_grad, few)


def whole(array):
    rank = len(array.shape)
    return pl.BlockSpec(array.shape, lambda i: (0,) * rank)


def body(inputs, out_grad, norm_gain, in_gate_x, in_read_write, in_step, conv_main, conv_state,
         step_bias, log_rate, skip_gain, gate_gain, out_weight):
    inner = out_weight.shape[2]
    pair = in_read_write.shape[2]
    heads = step_bias.shape[1]
    whole_inner = inner * lax.axis_size("tensor")
    few, weights_in, weights_out, errors, normed, saved, saved_p, states, res, inverses, scales, first_own, last_part = (
        forward_all(
            inputs, out_grad, out_weight[0], in_gate_x[0], in_read_write, in_step.transpose(0, 2, 1),
            conv_main.transpose(1, 0, 2), conv_state.transpose(1, 0, 2), step_bias, log_rate, skip_gain, gate_gain, norm_gain, inner, pair, heads, whole_inner
        )
    )
    firsts, last_out, first_grad, second_grad, large, few_sum, few_shared, state_grad = backward_all(
        errors, scales, weights_in, weights_out, few, normed, saved, saved_p, states, res, inverses, first_own, last_part,
        inner, pair, heads, whole_inner
    )
    outputs = finish_call(
        firsts, last_out, first_grad, second_grad, large, few_sum, few_shared, state_grad, few, inner, pair, heads
    )
    turned = [item.transpose(axes) for item, axes in zip(outputs[5:8], ((0, 2, 1), (1, 0, 2), (1, 0, 2)))]
    return (*outputs[:5], *turned, *outputs[8:])


def solution(mesh):
    in_specs = (
        P("dp", "tensor", None),
        P("dp", "tensor", None),
        P("pipe", None),
        P("pipe", "dp", None, "tensor"),
        P("pipe", "dp", None),
        P("pipe", "dp", "tensor"),
        P("pipe", None, "tensor"),
        P("pipe", None, None),
        P("pipe", "tensor"),
        P("pipe", "tensor"),
        P("pipe", "tensor"),
        P("pipe", "tensor"),
        P("pipe", "dp", "tensor"),
    )
    out_specs = (
        P("pipe", "dp", "tensor", None),
        P("pipe", "dp", "tensor", None),
        P("pipe", None),
        P("pipe", "dp", None, "tensor"),
        P("pipe", ("dp", "tensor"), None),
        P("pipe", "dp", "tensor"),
        P("pipe", None, "tensor"),
        P("pipe", None, None),
        P("pipe", "tensor"),
        P("pipe", "tensor"),
        P("pipe", "tensor"),
        P("pipe", "tensor"),
        P("pipe", "dp", "tensor"),
    )
    return jax.shard_map(body, mesh=mesh, in_specs=in_specs, out_specs=out_specs, check_vma=False)
```

```python
from functools import partial

import jax
import jax.numpy as jnp
import numpy as np
from jax import lax
from jax.experimental import pallas as pl
from jax.experimental.pallas import tpu as pltpu
from jax.sharding import PartitionSpec as P

F32, BF16 = jnp.float32, jnp.bfloat16
EPS = 1e-05
ROWS = 256
CHUNK = 128
LANES = 128
EXACT = lax.Precision.HIGHEST


def mm(left, right, contract=((1,), (0,))):
    return lax.dot_general(left, right, (contract, ((), ())), preferred_element_type=F32)


def mm_exact(left, right, contract=((1,), (0,))):
    return lax.dot_general(
        left, right, (contract, ((), ())), precision=EXACT, preferred_element_type=F32
    )


def spread(value, selector, heads):
    high = value.astype(BF16).astype(F32)
    both = high + pltpu.roll(value - high, heads, 1)
    return mm(both.astype(BF16), selector)


def per_head(value, collector):
    high = value.astype(BF16)
    low = (value - high.astype(F32)).astype(BF16)
    return mm(high, collector) + mm(low, collector)


def softplus(value):
    small = jnp.exp(-jnp.abs(value))
    series = small * (1.0 - small * (0.5 - small * (1.0 / 3.0 - small * 0.25)))
    return jnp.maximum(value, 0.0) + jnp.where(small < 0.01, series, jnp.log(1.0 + small))


def sigmoid(value):
    return 1.0 / (1.0 + jnp.exp(-value))


def iota(shape, axis):
    return lax.broadcasted_iota(jnp.int32, shape, axis)


def column_to_row(column):
    size = column.shape[0]
    same = iota((size, size), 0) == iota((size, size), 1)
    return jnp.sum(jnp.where(same, column, 0.0), 0, keepdims=True)


def row_to_column(row):
    size = row.shape[1]
    same = iota((size, size), 0) == iota((size, size), 1)
    return jnp.sum(jnp.where(same, row, 0.0), 1, keepdims=True)


def steps(raw, bias, rate, mask):
    delta = softplus(raw + bias) * mask
    tri = (iota((CHUNK, CHUNK), 0) >= iota((CHUNK, CHUNK), 1)).astype(F32)
    log_decay = mm_exact(tri, delta * rate)
    return delta, log_decay


def constants(inner, heads):
    width = inner // heads
    lane = np.arange(LANES)[:, None]
    channel = np.arange(inner)[None, :] // width
    selector = ((lane % heads == channel) & (lane < 2 * heads)).astype(np.float32)
    collector = (lane == channel).astype(np.float32).T
    return jnp.asarray(selector, BF16), jnp.asarray(collector, BF16)


MESH = pl.DeviceIdType.MESH
ANY = pl.BlockSpec(memory_space=pl.ANY)
VMEM = pl.BlockSpec(memory_space=pltpu.VMEM)


def place():
    pipe, dp, x = lax.axis_index("pipe"), lax.axis_index("dp"), lax.axis_index("tensor")
    return (dp // 8) * 2 + pipe, (dp // 2) % 4, dp % 2, x


def at_z(z):
    _, y, core, _ = place()
    return {"pipe": z % 2, "dp": ((z // 2) * 4 + y) * 2 + core}


def at_y(y):
    z, _, core, _ = place()
    return {"dp": ((z // 2) * 4 + y) * 2 + core}


def at_core(core):
    z, y, _, _ = place()
    return {"dp": ((z // 2) * 4 + y) * 2 + core}


def at_x(x):
    return {"tensor": x}


def at_pipe(pipe):
    return {"pipe": pipe}


def greet(*devices):
    barrier = pltpu.get_barrier_semaphore()
    for device in devices:
        pl.semaphore_signal(barrier, inc=1, device_id=device, device_id_type=MESH)
    pl.semaphore_wait(barrier, len(devices))


def around(me, device, steps=(1, 3)):
    return [device((me + step) % 4) for step in steps]


def remote(source, target, sems, index, device):
    return pltpu.make_async_remote_copy(
        src_ref=source,
        dst_ref=target,
        send_sem=sems[0].at[index],
        recv_sem=sems[1].at[index],
        device_id=device,
        device_id_type=MESH,
    )


class RingGather:
    def __init__(self, me, device, own, slot, sems, local=True):
        right, left, across = (me + 1) % 4, (me + 3) % 4, (me + 2) % 4
        to_right, to_left = device(right), device(left)
        self.copies = [
            remote(own(0), slot(me, 0), sems, 0, to_right),
            remote(own(1), slot(me, 1), sems, 1, to_left),
            remote(own(1), slot(me, 1), sems, 2, to_right),
            remote(own(0), slot(me, 0), sems, 3, to_left),
            remote(slot(left, 0), slot(left, 0), sems, 4, to_right),
            remote(slot(right, 1), slot(right, 1), sems, 5, to_left),
        ]
        self.origins = [(left, 0), (right, 1), (left, 1), (right, 0), (across, 0), (across, 1)]
        self.local = [
            pltpu.make_async_copy(own(half), slot(me, half), sems[2].at[half]) for half in range(2 * local)
        ]

    def start(self):
        for copy in self.copies[:4] + self.local:
            copy.start()

    def start_half(self, half):
        for index in ((0, 3), (1, 2))[half]:
            self.copies[index].start()
        self.local[half].start()

    def relay(self):
        for index in range(2):
            self.copies[index].wait_recv()
            self.copies[4 + index].start()

    def wait(self, *indices):
        for index in indices:
            self.copies[index].wait_recv()

    def wait_local(self):
        for copy in self.local:
            copy.wait()

    def wait_sends(self):
        for copy in self.copies:
            copy.wait_send()

    def finish(self):
        self.wait_local()
        self.wait_sends()


class RingScatter:
    def __init__(self, me, device, piece, buffers, sems, near=None):
        self.me, self.right, self.left = me, (me + 1) % 4, (me + 3) % 4
        across = (me + 2) % 4
        self.buffers = buffers
        self.near = near or [piece(me, 0), piece(me, 1), piece(self.right, 0), piece(self.left, 1)]
        relays, sums, arrived = buffers
        to_right, to_left = device(self.right), device(self.left)
        self.copies = [
            remote(piece(across, 0), relays.at[0], sems, 0, to_right),
            remote(piece(across, 1), relays.at[1], sems, 1, to_left),
            remote(piece(self.right, 1), arrived.at[0, 1], sems, 2, to_right),
            remote(piece(self.left, 0), arrived.at[1, 0], sems, 3, to_left),
            remote(sums.at[0], arrived.at[0, 0], sems, 4, to_right),
            remote(sums.at[1], arrived.at[1, 1], sems, 5, to_left),
        ]

    def start(self):
        for copy in self.copies[:4]:
            copy.start()

    def relay(self):
        relays, sums, _ = self.buffers
        for half in range(2):
            self.copies[half].wait_recv()
            total = relays[half].astype(F32) + self.near[2 + half][...].astype(F32)
            sums[half] = total.astype(sums.dtype)
            self.copies[4 + half].start()

    def wait(self):
        for index in range(2, 6):
            self.copies[index].wait_recv()

    def result(self, half):
        arrived = self.buffers[2]
        mine = self.near[half][...].astype(F32)
        return mine + arrived[0, half].astype(F32) + arrived[1, half].astype(F32)

    def finish(self):
        for copy in self.copies:
            copy.wait_send()


class Everyone:
    def __init__(self, me, device, source, target, sems):
        self.copies = [
            remote(source((me + step) % 4), target(me), sems, step - 1, device((me + step) % 4))
            for step in (1, 2, 3)
        ]

    def start(self):
        for copy in self.copies:
            copy.start()

    def wait(self):
        for copy in self.copies:
            copy.wait()


def dma(count):
    return [pltpu.SemaphoreType.DMA((count,)), pltpu.SemaphoreType.DMA((count,))]


def gather_sems():
    return dma(6) + [pltpu.SemaphoreType.DMA((2,))]


def scatter_buffers(*half):
    return [pltpu.VMEM((2,) + half, BF16), pltpu.VMEM((2,) + half, BF16), pltpu.VMEM((2, 2) + half, BF16)]


def norm_scale(value):
    return lax.rsqrt(jnp.mean(value * value, -1, keepdims=True) + EPS)


def norm_gain_of(few, layer, lead):
    return jnp.concatenate([few[layer, 6:7, lead:], few[layer, 7:8, :]], 1)


def remote_params(collective_id):
    return pltpu.CompilerParams(
        collective_id=collective_id, has_side_effects=True, vmem_limit_bytes=56 * 2**20
    )


def owned(block, x, rows):
    return pl.ds(pl.multiple_of(block * ROWS + x * rows, rows), rows)


class BlockSums:
    def __init__(self, x, piece, relays, sums, arrived, sems, op, near=None):
        self.right, self.left, self.me = (x + 1) % 4, (x + 3) % 4, x
        across = (x + 2) % 4
        self.relays, self.sums, self.arrived = relays, sums, arrived
        self.near = near or [piece(x, 0), piece(x, 1), piece(self.right, 0), piece(self.left, 1)]
        at_op = [sem.at[op] for sem in sems]
        to_right, to_left = at_x(self.right), at_x(self.left)
        self.copies = [
            remote(piece(across, 0), relays.at[op, 0], at_op, 0, to_right),
            remote(piece(across, 1), relays.at[op, 1], at_op, 1, to_left),
            remote(piece(self.right, 1), arrived.at[op, 0, 1], at_op, 2, to_right),
            remote(piece(self.left, 0), arrived.at[op, 1, 0], at_op, 3, to_left),
            remote(sums.at[op % 2, 0], arrived.at[op, 0, 0], at_op, 4, to_right),
            remote(sums.at[op % 2, 1], arrived.at[op, 1, 1], at_op, 5, to_left),
        ]
        self.op = op

    def start(self):
        for copy in self.copies[:4]:
            copy.start()

    def relay(self):
        for half in range(2):
            self.copies[half].wait_recv()
            total = self.relays[self.op, half].astype(F32) + self.near[2 + half][...].astype(F32)
            self.sums[self.op % 2, half] = total.astype(BF16)
            self.copies[4 + half].start()

    def wait(self):
        for index in range(2, 6):
            self.copies[index].wait_recv()

    def result(self):
        return jnp.concatenate(
            [
                self.near[half][...].astype(F32)
                + self.arrived[self.op, 0, half].astype(F32)
                + self.arrived[self.op, 1, half].astype(F32)
                for half in range(2)
            ],
            0,
        )

    def finish(self):
        for copy in self.copies:
            copy.wait_send()


def to_everyone(me, device, source, target, sems, op):
    at_op = [sem.at[op] for sem in sems]
    return Everyone(me, device, source, target, at_op)


def columns_of(inner, conv):
    ends = np.cumsum([0, inner, conv, LANES, inner])
    return [slice(int(begin), int(end)) for begin, end in zip(ends[:-1], ends[1:])], int(ends[-1])


def forward_block(sizes, first_block, last_layer, rows, e, w_in, w_out, few, selector, save, save_p, states, part,
                  squares, mixed, state, pad, serve):
    inner, pair, heads = sizes
    states_count = pair // 2
    split = inner + inner + pair
    conv = inner + pair
    (z_at, c_at, raw_at, y_at), _ = columns_of(inner, conv)

    @pl.when(first_block)
    def _():
        state[...] = jnp.zeros_like(state)
        pad[0:8, :] = jnp.zeros((8, conv), F32)

    @pl.when(jnp.logical_not(first_block))
    def _():
        pad[0:8, :] = pad[ROWS : ROWS + 8, :]

    projected = mm(rows, w_in)
    save[:, z_at] = projected[:, :inner]
    save_p[...] = projected[:, inner:split].astype(BF16)
    pad[8 : ROWS + 8, :] = projected[:, inner:split]
    save[:, raw_at] = projected[:, split:]
    bias = few[5:6, inner : inner + LANES]
    rate = few[5:6, inner + LANES : inner + 2 * LANES]
    gain = few[5:6, :inner]
    skip = few[6:7, :inner]
    mask = (iota((1, LANES), 1) < heads).astype(F32)
    first = iota((CHUNK, LANES), 1) < LANES // 2
    causal = iota((CHUNK, CHUNK), 0) >= iota((CHUNK, CHUNK), 1)
    owner_rows = ROWS // 4
    for chunk in range(ROWS // CHUNK):
        at = slice(chunk * CHUNK, (chunk + 1) * CHUNK)
        c = jnp.broadcast_to(few[4:5, :], (CHUNK, conv))
        for tap in range(4):
            begin = chunk * CHUNK + 5 + tap
            c = c + few[tap : tap + 1, :] * pad[begin : begin + CHUNK, :]
        save[at, c_at] = c
        value = c * sigmoid(c)
        xs = value[:, :inner]
        b_low = value[:, inner : inner + states_count].astype(BF16)
        c_low = value[:, inner + states_count :].astype(BF16)
        delta, log_decay = steps(save[at, raw_at], bias, rate, mask)
        turned = log_decay.T
        final = log_decay[CHUNK - 1 : CHUNK, :]
        scaled = spread(delta, selector, heads) * xs
        scaled_low = scaled.astype(BF16)
        products = jnp.where(causal, mm(c_low, b_low, ((1,), (1,))), 0.0)
        within = []
        for two in range(heads // 2):
            lanes = slice(two * LANES, (two + 1) * LANES)
            parts = []
            for h in (2 * two, 2 * two + 1):
                gap = jnp.minimum(log_decay[:, h : h + 1] - turned[h : h + 1, :], 0.0)
                parts.append(mm((products * jnp.exp(gap)).astype(BF16), scaled_low[:, lanes]))
            within.append(jnp.where(first, parts[0], parts[1]))
        old = state[...]
        states[chunk] = old
        carried = mm(c_low, old.astype(BF16)) * spread(jnp.exp(log_decay) * mask, selector, heads)
        y = jnp.concatenate(within, 1) + carried + skip * xs
        save[at, y_at] = y
        ends = (spread(jnp.exp(final - log_decay) * mask, selector, heads) * scaled).astype(BF16)
        keep = spread(jnp.broadcast_to(jnp.exp(final) * mask, (8, LANES)), selector, heads)[0:1]
        state[...] = keep * old + mm(b_low, ends, ((0,), (0,)))
        z = save[at, z_at]
        gated = y * (z * sigmoid(z))
        total = jnp.sum(gated * gated, 1, keepdims=True)
        for piece in range(CHUNK // owner_rows):
            row = column_to_row(total[piece * owner_rows : (piece + 1) * owner_rows])
            squares[chunk * (CHUNK // owner_rows) + piece, 0:1, 0:owner_rows] = row
        mixed[at, :] = (gated * gain).astype(BF16)
        if chunk == 0:
            serve()
    part[...] = mm(mixed[...], w_out(), ((1,), (1,))).astype(BF16)

    @pl.when(last_layer)
    def _():
        total = jnp.sum(mm(e[...], w_out()) * mixed[...].astype(F32), 1, keepdims=True)
        for piece in range(4):
            squares[piece, 1:2, 0:owner_rows] = column_to_row(total[piece * owner_rows : (piece + 1) * owner_rows])


class HandedRing:
    def __init__(self, me, device, source, slot, sems, core_sems):
        _, _, core, _ = place()
        self.slot = lambda origin, half: slot(origin, half, core)
        self.ring = RingGather(me, device, source, self.slot, sems)
        self.pieces = [(source(half), self.slot(me, half), 6 + half) for half in range(2)]
        for index in range(6):
            held = self.slot(*self.ring.origins[index])
            self.pieces.append((held, held, index))
        self.core_sems, self.device = core_sems, at_core(1 - core)

    def hand(self, at):
        source, target, index = self.pieces[at]
        return remote(source, target, self.core_sems, index, self.device)

    def start_half(self, half):
        self.ring.start_half(half)
        self.hand(half).start()

    def start(self):
        for half in range(2):
            self.start_half(half)

    def relay(self):
        self.ring.relay()
        for index in range(2):
            self.hand(2 + index).start()

    def finish(self):
        for index in range(2, 6):
            self.ring.wait(index)
            self.hand(2 + index).start()
        self.ring.finish()
        for at in range(8):
            self.hand(at).wait()


def gather_parameters(sizes, few, shard, gate_x, read_write, step, main, of_state, bias, log_rate, skip, gate, norm):
    inner, pair, heads, lead = sizes
    width = inner // heads
    few[...] = jnp.zeros_like(few)
    for tap in range(5):
        few[tap : tap + 1, :inner] = main[tap]
        few[tap : tap + 1, inner:] = of_state[tap]
    few[5:6, :inner] = gate[...]
    few[5:6, inner : inner + heads] = bias[...]
    few[5:6, inner + LANES : inner + LANES + heads] = -jnp.exp(log_rate[...])
    for head in range(heads):
        few[6:7, head * width : (head + 1) * width] = jnp.broadcast_to(skip[0:1, head : head + 1], (1, width))
    first = few.shape[1] - lead
    few[6:7, lead:] = norm[:, :first]
    few[7:8, :] = norm[:, first:]
    split = 2 * inner + pair
    both = gate_x[...]
    for index in range(2):
        shard[:, index * inner : (index + 1) * inner] = both[:, index, :]
    shard[:, 2 * inner : split] = read_write[0]
    same = (iota((heads, LANES), 0) == iota((heads, LANES), 1)).astype(BF16)
    shard[:, split:] = mm(step[0], same, ((0,), (0,))).astype(BF16)


def forward_all_kernel(sizes, inputs, out_grad, shard_out, gate_x, read_write, step_in, main, of_state, bias, log_rate,
                       skip, gate, norm, selector,
                       few_both, weights_in, weights_out, errors_out, normed, saved, saved_p, states, res, inverses, scales,
                       firsts, last_part,
                       hidden, w_in, w_out, errors, part, relays, sums, arrived, squares, others, stage, p_stage, state_stage,
                       norm_stage, mixed, state, pad, shard_in, z_weights, y_weights, few,
                       xs, xr, xl, es, er, el, zs, zr, zl, ys, yr, yl, cs, cr, y1s, y1r, y1l, c1s, c1r,
                       bs, br, bl, os, og, ol, c2s, c2r, fs, fr, rs, rr, gs, gr, qs, qr, outs, load):
    inner, pair, heads, lead, whole_inner = sizes
    layer_sizes = (inner, pair, heads)
    z, y, core, x = place()
    pipe = z % 2
    quarter = ROWS // 4
    gather_parameters((inner, pair, heads, lead), few.at[pipe], shard_in, gate_x, read_write, step_in, main, of_state,
                      bias, log_rate, skip, gate, norm)
    squares[...] = jnp.zeros_like(squares)
    greet(*around(x, at_x, (1, 2, 3)), *around(y, at_y), *around(z, at_z), at_core(1 - core), at_pipe(1 - pipe))
    few_swap = remote(few.at[pipe], few.at[pipe], (fs, fr), 0, at_pipe(1 - pipe))
    few_swap.start()
    piece = shard_in.shape[0]
    by_half = lambda half: pl.ds(half * (piece // 2), piece // 2)
    z_ring = RingGather(z, at_z, lambda half: shard_in.at[by_half(half)],
                        lambda origin, half: z_weights.at[origin, by_half(half)], (zs, zr, zl))
    z_ring.start()
    y_ring = RingGather(y, at_y, lambda half: shard_out.at[by_half(half)],
                        lambda origin, half: y_weights.at[origin, by_half(half)], (bs, br, bl))
    y_ring.start()
    block_rows = lambda origin, half: pl.ds(pl.multiple_of(origin * ROWS + half * (ROWS // 2), ROWS // 2), ROWS // 2)
    x_ring = RingGather(x, at_x, lambda half: inputs.at[pipe, half],
                        lambda origin, half: hidden.at[0, block_rows(origin, half)], (xs, xr, xl))
    x_ring.start()
    e_ring = RingGather(x, at_x, lambda half: out_grad.at[pipe, half],
                        lambda origin, half: errors.at[block_rows(origin, half)], (es, er, el))

    def in_ring(layer, sems, core_sems):
        away = pipe * (1 - layer) + (1 - pipe) * layer
        from_z = lambda half: (z + 3 * away + 2 * half) % 4
        return HandedRing(
            y, at_y, lambda half: z_weights.at[from_z(half)],
            lambda origin, half, core: w_in.at[layer, from_z(half) // 2, origin, core], sems, core_sems,
        )

    rings = [in_ring(0, (ys, yr, yl), (cs, cr)), in_ring(1, (y1s, y1r, y1l), (c1s, c1r))]
    out_ring = HandedRing(
        z, at_z, lambda half: y_weights.at[pl.ds(2 * half, 2)],
        lambda origin, half, core: w_out.at[origin % 2, origin // 2, pl.ds(2 * half, 2), core],
        (os, og, ol), (c2s, c2r),
    )
    z_ring.wait_local()

    @pl.when(pipe == 0)
    def _():
        rings[0].start_half(0)

    y_ring.relay()
    z_ring.relay()
    z_ring.wait(2)

    @pl.when(pipe == 1)
    def _():
        rings[0].start_half(0)

    z_ring.wait(3)

    @pl.when(pipe == 1)
    def _():
        rings[0].start_half(1)

    y_ring.wait(2, 3, 4, 5)
    y_ring.wait_local()
    out_ring.start()
    z_ring.wait(4, 5)

    @pl.when(pipe == 0)
    def _():
        rings[0].start_half(1)

    x_ring.relay()
    e_ring.start()
    out_ring.relay()
    rings[0].relay()
    z_ring.wait_sends()
    y_ring.wait_sends()
    few_swap.wait()
    few_both[...] = few[...]
    x_ring.wait(2, 3, 4, 5)
    x_ring.finish()
    for block in range(4):
        res[0, block] = hidden[0, owned(block, x, quarter)].astype(F32)
    rings[0].finish()
    rings[1].start()
    def sums_of(op):
        rows = lambda owner, half: part.at[op, pl.ds(pl.multiple_of(owner * quarter + half * (quarter // 2), quarter // 2), quarter // 2)]
        return BlockSums(x, rows, relays, sums, arrived, (rs, rr), op)

    def squares_of(op):
        return to_everyone(x, at_x, lambda to: squares.at[op], lambda me: others.at[op, me], (qs, qr), op)

    def gather_of(block):
        place_of = lambda origin, half: hidden.at[
            1, pl.ds(pl.multiple_of(block * ROWS + origin * quarter + half * (quarter // 2), quarter // 2), quarter // 2)
        ]
        return RingGather(x, at_x, lambda half: place_of(x, half), place_of, (gs.at[block], gr.at[block]), local=False)

    def outs_of(op):
        layer, block = op // 4, op % 4
        slot = op % 2
        at = pl.ds(pl.multiple_of(block * ROWS, ROWS), ROWS)
        count = ROWS // CHUNK
        return [
            pltpu.make_async_copy(stage.at[slot], saved.at[layer, at], outs.at[0, slot]),
            pltpu.make_async_copy(state_stage.at[slot], states.at[layer, pl.ds(block * count, count)], outs.at[1, slot]),
            pltpu.make_async_copy(norm_stage.at[slot], normed.at[layer, at], outs.at[2, slot]),
            pltpu.make_async_copy(p_stage.at[slot], saved_p.at[layer, at], outs.at[3, slot]),
        ]

    def row_sums(op, owner):
        total = others[op, 0, owner, 0:2, :]
        for device in (1, 2, 3):
            total = total + others[op, device, owner, 0:2, :]
        return lax.rsqrt(total[0:1] / whole_inner + EPS), total[1:2]

    def finish_sums(block):
        job = sums_of(block)
        squares_of(block).wait()
        others[block, x] = squares[block]
        inverse, _ = row_sums(block, x)
        inverses[block] = jnp.broadcast_to(inverse, (8, LANES))
        column = row_to_column(inverse)[:quarter]
        job.wait()
        value = res[0, block] + column * job.result()
        job.finish()
        res[1, block] = value
        hidden[1, owned(block, x, quarter)] = value.astype(BF16)
        gather_of(block).start()

    def finish_scales(block):
        squares_of(4 + block).wait()
        others[4 + block, x] = squares[4 + block]
        for owner in range(4):
            inverse, dots = row_sums(4 + block, owner)
            scales[block, owner, 0:1, :] = inverse
            scales[block, owner, 1:2, :] = dots * inverse / whole_inner

    own_block = hidden.at[1, pl.ds(pl.multiple_of(x * ROWS, ROWS), ROWS)]
    ends = [
        pltpu.make_async_copy(w_in.at[0], weights_in.at[0], load.at[0]),
        pltpu.make_async_copy(w_in.at[1], weights_in.at[1], load.at[1]),
        pltpu.make_async_copy(w_out, weights_out, load.at[2]),
        pltpu.make_async_copy(errors, errors_out, load.at[3]),
        pltpu.make_async_copy(own_block, firsts, load.at[4]),
    ]

    def part_copy(block):
        at = pl.ds(pl.multiple_of(block * ROWS, ROWS), ROWS)
        return pltpu.make_async_copy(part.at[4 + block], last_part.at[at], load.at[5 + block])

    def step(op, carry):
        layer, block = op // 4, op % 4

        @pl.when(layer == 1)
        def _():
            job = gather_of(block)
            job.wait(2, 3, 4, 5)
            job.finish()

        @pl.when(op == 7)
        def _():
            ends[4].start()

        @pl.when(op >= 2)
        def _():
            for copy in outs_of(op - 2):
                copy.wait()

        def serve():
            @pl.when(op == 0)
            def _():
                out_ring.finish()

            @pl.when(op == 1)
            def _():
                e_ring.relay()
                rings[1].relay()

            @pl.when((op >= 1) & (op < 5))
            def _():
                sums_of(op - 1).relay()

            @pl.when((op >= 2) & (op < 6))
            def _():
                gather_of(op - 2).relay()

            @pl.when(op == 3)
            def _():
                e_ring.wait(2, 3, 4, 5)
                e_ring.finish()
                rings[1].finish()
                for copy in ends[:4]:
                    copy.start()

            @pl.when(op >= 5)
            def _():
                finish_scales(op - 5)

        slot = op % 2
        at = pl.ds(pl.multiple_of(block * ROWS, ROWS), ROWS)
        value = hidden[layer, at].astype(F32)
        gain = jnp.concatenate([few[layer, 6:7, lead:], few[layer, 7:8, :]], 1)
        norm_stage[slot] = (value * norm_scale(value) * gain).astype(BF16)
        width = value.shape[1]
        forward_block(layer_sizes, block == 0, layer == 1, norm_stage[slot], errors.at[at],
                      w_in[layer].reshape(width, -1), lambda: w_out[layer].reshape(width, -1), few.at[layer], selector[...],
                      stage.at[slot], p_stage.at[slot], state_stage.at[slot], part.at[op], squares.at[op], mixed, state, pad, serve)
        for copy in outs_of(op):
            copy.start()
        squares_of(op).start()

        @pl.when(op < 4)
        def _():
            sums_of(op).start()

        @pl.when(op >= 4)
        def _():
            part_copy(op - 4).start()

        @pl.when((op >= 1) & (op < 5))
        def _():
            finish_sums(op - 1)

        return carry

    lax.fori_loop(0, 8, step, 0)
    finish_scales(3)
    for op in (6, 7):
        for copy in outs_of(op):
            copy.wait()
    for copy in ends:
        copy.wait()
    for block in range(4):
        part_copy(block).wait()


def forward_all(inputs, out_grad, shard_out, gate_x, read_write, step, main, of_state, bias, log_rate, skip, gate, norm,
                inner, pair, heads, whole_inner):
    _, part, width = inputs.shape
    rows = shard_out.shape[0]
    conv = inner + pair
    columns = inner + conv + LANES
    lead = conv - (width - conv)
    length = 4 * part
    _, saved_columns = columns_of(inner, conv)
    quarter = ROWS // 4
    chunks = ROWS // CHUNK
    selector, _ = constants(inner, heads)
    half = (2, 2, part // 2, width)
    shape = jax.ShapeDtypeStruct
    w_in = (2, 2, 4, 2, rows, columns)
    w_out = (2, 2, 4, 2, rows, inner)
    semaphores = lambda *count: [pltpu.SemaphoreType.DMA(count)] * 2
    return pl.pallas_call(
        partial(forward_all_kernel, (inner, pair, heads, lead, whole_inner)),
        out_shape=[
            shape((2, 8, conv), F32),
            shape(w_in, BF16),
            shape(w_out, BF16),
            shape((length, width), BF16),
            shape((2, length, width), BF16),
            shape((2, length, saved_columns), F32),
            shape((2, length, conv), BF16),
            shape((2, length // CHUNK, pair // 2, inner), F32),
            shape((2, 4, quarter, width), F32),
            shape((4, 8, LANES), F32),
            shape((4, 4, 8, LANES), F32),
            shape((part, width), BF16),
            shape((length, width), BF16),
        ],
        in_specs=[ANY, ANY, ANY] + [VMEM] * 11,
        out_specs=[VMEM, ANY, ANY, ANY, ANY, ANY, ANY, ANY, VMEM, VMEM, VMEM, ANY, ANY],
        scratch_shapes=[
            pltpu.VMEM((2, length, width), BF16),
            pltpu.VMEM(w_in, BF16),
            pltpu.VMEM(w_out, BF16),
            pltpu.VMEM((length, width), BF16),
            pltpu.VMEM((8, ROWS, width), BF16),
            pltpu.VMEM((4, 2, quarter // 2, width), BF16),
            pltpu.VMEM((4, 2, quarter // 2, width), BF16),
            pltpu.VMEM((4, 2, 2, quarter // 2, width), BF16),
            pltpu.VMEM((8, 4, 8, LANES), F32),
            pltpu.VMEM((8, 4, 4, 8, LANES), F32),
            pltpu.VMEM((2, ROWS, saved_columns), F32),
            pltpu.VMEM((2, ROWS, conv), BF16),
            pltpu.VMEM((2, chunks, pair // 2, inner), F32),
            pltpu.VMEM((2, ROWS, width), BF16),
            pltpu.VMEM((ROWS, inner), BF16),
            pltpu.VMEM((pair // 2, inner), F32),
            pltpu.VMEM((ROWS + 8, conv), F32),
            pltpu.VMEM((rows, columns), BF16),
            pltpu.VMEM((4, rows, columns), BF16),
            pltpu.VMEM((4, rows, inner), BF16),
            pltpu.VMEM((2, 8, conv), F32),
        ]
        + gather_sems() * 3
        + (gather_sems() + dma(8)) * 2
        + gather_sems()
        + gather_sems() + dma(8)
        + dma(1)
        + semaphores(4, 6) + semaphores(4, 6) + semaphores(8, 3)
        + [pltpu.SemaphoreType.DMA((4, 2)), pltpu.SemaphoreType.DMA((9,))],
        compiler_params=remote_params(0),
        name="forward_layers",
    )(inputs.reshape(half), out_grad.reshape(half), shard_out, gate_x, read_write, step, main, of_state, bias, log_rate,
      skip, gate, norm, selector)


class CoreSum:
    def __init__(self, grads, arrived, sems):
        _, _, core, _ = place()
        self.grads, self.arrived, self.core = grads, arrived, core
        self.pieces = [(y, half) for y in range(4) for half in range(2)]
        self.sems = sems

    def copy(self, index):
        y, half = self.pieces[index]
        source = self.grads.at[half, y, 1 - self.core]
        return remote(source, self.arrived.at[y, half], self.sems, index, at_core(1 - self.core))

    def start(self):
        for index in range(8):
            self.copy(index).start()

    def finish(self):
        for index, (y, half) in enumerate(self.pieces):
            self.copy(index).wait_recv()
            value = self.grads[half, y, self.core].astype(F32) + self.arrived[y, half].astype(F32)
            self.grads[half, y, self.core] = value.astype(BF16)
        for index in range(8):
            self.copy(index).wait_send()


def back_through_norm(value, grad_out, summed, gain):
    scale = norm_scale(value)
    unit = value * scale
    scaled = summed * gain
    mean = jnp.mean(scaled * unit, -1, keepdims=True)
    return grad_out + scale * (scaled - unit * mean), jnp.sum(summed * unit, 0, keepdims=True)


def backward_block(sizes, first_block, e, scales, w_in, w_out, few, selector, collector, saved, saved_p, states,
                   part, grad, mixed, few_out, state, later, pad, serve):
    inner, pair, heads = sizes
    states_count = pair // 2
    split = inner + inner + pair
    conv = inner + pair
    quarter = ROWS // 4
    (z_at, c_at, raw_at, y_at), _ = columns_of(inner, conv)

    @pl.when(first_block)
    def _():
        state[...] = jnp.zeros_like(state)
        later[...] = jnp.zeros_like(later)
        pad[ROWS : ROWS + 8, :] = jnp.zeros((8, conv), F32)

    @pl.when(jnp.logical_not(first_block))
    def _():
        pad[ROWS : ROWS + 8, :] = pad[0:8, :]

    bias = few[5:6, inner : inner + LANES]
    rate = few[5:6, inner + LANES : inner + 2 * LANES]
    gain = few[5:6, :inner]
    skip = few[6:7, :inner]
    mask = (iota((1, LANES), 1) < heads).astype(F32)
    first = iota((CHUNK, LANES), 1) < LANES // 2
    later_in = iota((CHUNK, CHUNK), 1) >= iota((CHUNK, CHUNK), 0)
    last = iota((CHUNK, LANES), 0) == CHUNK - 1
    tri = later_in.astype(F32)
    column = lambda row: jnp.concatenate(
        [row_to_column(scales[owner, row : row + 1, :])[:quarter] for owner in range(4)], 0
    )
    inverse = column(0)
    inner_dot = column(1)
    mixed_grad = mm(e, w_out)
    for chunk in reversed(range(ROWS // CHUNK)):
        at = slice(chunk * CHUNK, (chunk + 1) * CHUNK)
        z = saved[at, z_at]
        y = saved[at, y_at]
        sig = sigmoid(z)
        act = z * sig
        g = y * act * inverse[at]
        mixed[at, :] = (g * gain).astype(BF16)
        mixed_here = mixed_grad[at]
        gated_grad = inverse[at] * (mixed_here * gain - g * inner_dot[at])
        dy = gated_grad * act
        grad[at, :inner] = (gated_grad * y * (sig * (1.0 + z - act))).astype(BF16)
        c = saved[at, c_at]
        csig = sigmoid(c)
        value = c * csig
        slope = csig * (1.0 + c - value)
        xs = value[:, :inner]
        b_low = value[:, inner : inner + states_count].astype(BF16)
        c_low = value[:, inner + states_count :].astype(BF16)
        raw = saved[at, raw_at]
        delta, log_decay = steps(raw, bias, rate, mask)
        turned = log_decay.T
        final = log_decay[CHUNK - 1 : CHUNK, :]
        wide_delta = spread(delta, selector, heads)
        scaled = wide_delta * xs
        scaled_low = scaled.astype(BF16)
        dy_low = dy.astype(BF16)
        products = jnp.where(later_in, mm(b_low, c_low, ((1,), (1,))), 0.0)
        dproducts = jnp.zeros((CHUNK, CHUNK), F32)
        within = []
        for two in range(heads // 2):
            lanes = slice(two * LANES, (two + 1) * LANES)
            parts = []
            for odd in range(2):
                h = 2 * two + odd
                mine = first if odd == 0 else ~first
                decay = jnp.exp(jnp.minimum(turned[h : h + 1, :] - log_decay[:, h : h + 1], 0.0))
                parts.append(mm((products * decay).astype(BF16), dy_low[:, lanes]))
                own = jnp.where(mine, scaled_low[:, lanes], jnp.zeros((), BF16))
                dproducts = dproducts + decay * mm(own, dy_low[:, lanes], ((1,), (1,)))
            within.append(jnp.where(first, parts[0], parts[1]))
        dproducts = jnp.where(later_in, dproducts, 0.0).astype(BF16)
        old = states[chunk]
        old_low = old.astype(BF16)
        dstate = state[...]
        dstate_low = dstate.astype(BF16)
        to_end = spread(jnp.exp(final - log_decay) * mask, selector, heads)
        from_start = (spread(jnp.exp(log_decay) * mask, selector, heads) * dy).astype(BF16)
        dscaled = jnp.concatenate(within, 1) + to_end * mm(b_low, dstate_low)
        dc_state = mm(from_start, old_low, ((1,), (1,))) + mm(dproducts, b_low, ((0,), (0,)))
        db_state = mm((to_end * scaled).astype(BF16), dstate_low, ((1,), (1,))) + mm(dproducts, c_low)
        carry = jnp.broadcast_to(jnp.sum(later[...] * dstate, 0, keepdims=True), (8, inner))
        carry = per_head(carry, collector)[0:1]
        keep = spread(jnp.broadcast_to(jnp.exp(final) * mask, (8, LANES)), selector, heads)[0:1]
        state[...] = keep * dstate + mm(c_low, from_start, ((0,), (0,)))
        later[...] = old
        flow = dy_low.astype(F32) * (y - skip * xs) - scaled_low.astype(F32) * dscaled
        dlog = per_head(flow, collector) + jnp.where(last, carry, 0.0)
        dstep = mm_exact(tri, dlog)
        ddelta = per_head(xs * dscaled, collector) + rate * dstep
        draw = ddelta * sigmoid(raw + bias) * mask
        few_out[5:6, inner : inner + LANES] += jnp.sum(draw, 0, keepdims=True)
        few_out[5:6, inner + LANES : inner + 2 * LANES] += jnp.sum(delta * dstep, 0, keepdims=True)
        few_out[5:6, :inner] += jnp.sum(mixed_here * g, 0, keepdims=True)
        few_out[6:7, :inner] += jnp.sum(dy * xs, 0, keepdims=True)
        dxs = wide_delta * dscaled + skip * dy
        pad[at, :] = jnp.concatenate([dxs, db_state, dc_state], 1) * slope
        grad[at, split:] = draw.astype(BF16)
        if chunk == ROWS // CHUNK - 1:
            serve()
    for chunk in range(ROWS // CHUNK):
        at = slice(chunk * CHUNK, (chunk + 1) * CHUNK)
        p = saved_p[at, :].astype(F32)
        total = jnp.zeros((CHUNK, conv), F32)
        for tap in range(4):
            begin = chunk * CHUNK + 3 - tap
            shifted = pad[begin : begin + CHUNK, :]
            total = total + few[tap : tap + 1, :] * shifted
            few_out[tap : tap + 1, :] += jnp.sum(p * shifted, 0, keepdims=True)
        few_out[4:5, :] += jnp.sum(pad[at, :], 0, keepdims=True)
        grad[at, inner:split] = total.astype(BF16)
    part[...] = mm(grad[...], w_in, ((1,), (1,))).astype(BF16)


class WeightParts:
    def __init__(self, refs):
        (self.columns, self.low, self.core, self.y, self.z, self.middle, self.z_blocks, self.core_sems, self.y_sems,
         self.z_sems) = refs

    @staticmethod
    def scratch(piece, columns):
        grads = pltpu.VMEM((4, 2, piece, columns), BF16)
        return [
            [
                pltpu.VMEM((2, 4, 2, piece, columns), BF16),
                grads,
                scatter_buffers(piece, columns),
                scatter_buffers(piece // 2, columns),
                pltpu.VMEM((2, piece, columns), BF16),
                pltpu.VMEM((4, 2, piece // 2, columns), BF16),
            ],
            [[pltpu.SemaphoreType.DMA((2, 8))] * 2, [dma(6), dma(6)], dma(6)],
        ]

    def flush(self, total):
        piece = total.shape[0] // 16
        for index in range(16):
            z_hi, y_at, core_at = index // 8, (index // 2) % 4, index % 2
            self.low[z_hi, y_at, core_at] = total[index * piece : (index + 1) * piece, self.columns].astype(BF16)

    def core_sum(self, layer):
        return CoreSum(self.low, self.core, [sem.at[layer] for sem in self.core_sems])

    def y_sum(self, layer):
        _, y, core, _ = place()
        return RingScatter(y, at_y, lambda owner, half: self.low.at[half, owner, core], self.y, self.y_sems[layer])

    def z_sum(self):
        z, _, _, _ = place()
        return RingScatter(z, at_z, lambda owner, half: self.z_blocks.at[owner, half], self.z, self.z_sems)

    def to_z(self, sums):
        rows = self.z_blocks.shape[2]
        for z_hi in range(2):
            first = sums.result(z_hi).astype(BF16)
            second = self.middle[z_hi]
            for half in range(2):
                self.z_blocks[2 * z_hi, half] = first[half * rows : (half + 1) * rows]
                self.z_blocks[2 * z_hi + 1, half] = second[half * rows : (half + 1) * rows]


def mix_rows(sizes, scales, few, saved, mixed):
    inner, pair, _ = sizes
    (z_at, _, _, y_at), _ = columns_of(inner, inner + pair)
    quarter = ROWS // 4
    inverse = jnp.concatenate([row_to_column(scales[owner, 0:1, :])[:quarter] for owner in range(4)], 0)
    for chunk in range(ROWS // CHUNK):
        at = slice(chunk * CHUNK, (chunk + 1) * CHUNK)
        z = saved[at, z_at]
        g = saved[at, y_at] * (z * sigmoid(z)) * inverse[at]
        mixed[at, :] = (g * few[5:6, :inner]).astype(BF16)


def flat(tree):
    return jax.tree.leaves(tree)


def backward_all_kernel(sizes, errors_later, scales_later, weights_in, weights_out, few, selector, collector, normed,
                        saved, saved_p, states, res, inverses, first_own, last_part,
                        firsts, last_out, first_grad, second_grad, large, few_sum, few_shared, state_grad,
                        errors, scales, w_in, w_out, part, relays, sums, arrived, stage, p_stage, state_stage,
                        norm_stage, e_stage, grad, mixed, own_scales, own_grad, both_grad, few_grad, norm_grad, total,
                        t0, t1, t2, last_held, first_rows, pair_few, y_few, z_few, x_few, state_parts, state, later, pad,
                        rs, rr, gs, gr, ss, sr, ts, tr, ls, lr, ps, pr, fs, fr, hs, hr, js, jr, ks, kr, ws, wr, is_, ig, ds, dr,
                        loads, load, core_free, y_free, *rest):
    inner, pair, heads, lead, whole_inner = sizes
    layer_sizes = (inner, pair, heads)
    z, y, core, x = place()
    pipe = z % 2
    every = (1, 2, 3)
    quarter = ROWS // 4
    split = 2 * inner + pair
    wide = split + LANES
    middle_at = inner + pair
    ends = (slice(wide, total.shape[1]), slice(middle_at, wide), slice(0, middle_at))
    layout = [WeightParts.scratch(total.shape[0] // 16, at.stop - at.start) for at in ends]
    refs = iter(rest)
    memory = [jax.tree.map(lambda _: next(refs), of_part[0]) for of_part in layout]
    signals = [jax.tree.map(lambda _: next(refs), of_part[1]) for of_part in layout]
    parts = [WeightParts([at] + held + sems) for at, held, sems in zip(ends, memory, signals)]

    block_rows = lambda owner, half: pl.ds(pl.multiple_of(owner * ROWS + half * (ROWS // 2), ROWS // 2), ROWS // 2)

    def at_step(op):
        return 1 - op // 4, 3 - op % 4

    def loads_of(op):
        layer, block = at_step(op)
        slot = op % 2
        at = pl.ds(pl.multiple_of(block * ROWS, ROWS), ROWS)
        count = ROWS // CHUNK
        return [
            pltpu.make_async_copy(saved.at[layer, at], stage.at[slot], loads.at[0, slot]),
            pltpu.make_async_copy(states.at[layer, pl.ds(block * count, count)], state_stage.at[slot], loads.at[1, slot]),
            pltpu.make_async_copy(normed.at[layer, at], norm_stage.at[slot], loads.at[2, slot]),
            pltpu.make_async_copy(saved_p.at[layer, at], p_stage.at[slot], loads.at[3, slot]),
        ]

    def weight_loads(layer):
        return [
            pltpu.make_async_copy(weights_in.at[layer], w_in.at[layer], load.at[layer]),
            pltpu.make_async_copy(weights_out.at[layer], w_out.at[layer], load.at[6 + layer]),
        ]

    def error_load(op):
        _, block = at_step(op)
        at = pl.ds(pl.multiple_of(block * ROWS, ROWS), ROWS)
        return pltpu.make_async_copy(errors_later.at[at], e_stage.at[op % 2], loads.at[4, op % 2])

    own_loads = [
        pltpu.make_async_copy(errors_later.at[owned(block, x, quarter)], both_grad.at[pipe, block], load.at[9 + block])
        for block in range(4)
    ]
    last_rows = lambda piece, owner, half: last_part.at[
        pl.ds(pl.multiple_of(owner * ROWS + piece * quarter + half * (quarter // 2), quarter // 2), quarter // 2)
    ]
    sum_loads = [
        pltpu.make_async_copy(last_rows(piece, owner, half), last_held.at[piece, index], load.at[13 + 4 * piece + index])
        for piece in range(4)
        for index, (owner, half) in enumerate(((x, 0), (x, 1), ((x + 1) % 4, 0), ((x + 3) % 4, 1)))
    ]
    error_load(0).start()
    for copy in weight_loads(1) + loads_of(0):
        copy.start()
    first_load = pltpu.make_async_copy(first_own, first_rows, load.at[8])
    first_load.start()
    for copy in own_loads + sum_loads + weight_loads(0):
        copy.start()
    greet(*around(x, at_x, every), *around(y, at_y, every), *around(z, at_z, every), at_core(1 - core))

    def last_sums(piece):
        return BlockSums(x, lambda owner, half: last_rows(piece, owner, half), t0, t1, t2, (ts, tr), piece,
                         [last_held.at[piece, index] for index in range(4)])

    first_copy = pltpu.make_async_copy(first_own, firsts.at[pipe], load.at[2])
    first_swap = remote(first_own, firsts.at[pipe], (ps, pr), 1, at_pipe(1 - pipe))
    first_copy.start()
    first_swap.start()
    scales[1] = scales_later[...]
    few_grad[...] = jnp.zeros_like(few_grad)
    norm_grad[...] = jnp.zeros_like(norm_grad)
    own_scales[...] = jnp.zeros_like(own_scales)
    total[...] = jnp.zeros_like(total)
    for block, copy in enumerate(own_loads):
        copy.wait()
        own_grad[block] = both_grad[pipe, block].astype(F32)
    for copy in sum_loads:
        copy.wait()
    for copy in weight_loads(1):
        copy.wait()

    def sums_of(op):
        rows = lambda owner, half: part.at[
            op % 3, pl.ds(pl.multiple_of(owner * quarter + half * (quarter // 2), quarter // 2), quarter // 2)
        ]
        return BlockSums(x, rows, relays, sums, arrived, (rs, rr), op)

    def gather_of(block):
        place_of = lambda origin, half: errors.at[
            pl.ds(pl.multiple_of(block * ROWS + origin * quarter + half * (quarter // 2), quarter // 2), quarter // 2)
        ]
        return RingGather(x, at_x, lambda half: place_of(x, half), place_of, (gs.at[block], gr.at[block]), local=False)

    def scales_of(block):
        return to_everyone(x, at_x, lambda to: own_scales.at[block], lambda me: scales.at[0, block, me], (ss, sr), block)

    def hand_over(block):
        mine = both_grad.at[pipe, block]
        return remote(mine, mine, (is_, ig), block, at_pipe(1 - pipe))

    def finish_sums(op):
        layer, block = at_step(op)
        job = sums_of(op)
        job.wait()
        gain = jnp.concatenate([few[layer, 6:7, lead:], few[layer, 7:8, :]], 1)
        value, gain_part = back_through_norm(res[layer, block], own_grad[block], job.result(), gain)
        own_grad[block] = value
        norm_grad[layer, 0:1, :] += gain_part
        low = value.astype(BF16)
        job.finish()

        @pl.when(layer == 1)
        def _():
            errors[owned(block, x, quarter)] = low
            gather_of(block).start()
            dots = jnp.sum(low.astype(F32) * (res[1, block] - res[0, block]), -1, keepdims=True) / whole_inner
            own_scales[block, 0:1, :] = inverses[block, 0:1, :]
            own_scales[block, 1:2, 0:quarter] = column_to_row(dots)
            scales[0, block, x] = own_scales[block]
            scales_of(block).start()

        @pl.when(layer == 0)
        def _():
            both_grad[pipe, block] = low
            hand_over(block).start()

    own_block = errors.at[pl.ds(pl.multiple_of(x * ROWS, ROWS), ROWS)]
    second_copy = pltpu.make_async_copy(own_block, second_grad.at[pipe], load.at[4])
    swap = remote(own_block, second_grad.at[pipe], (ps, pr), 0, at_pipe(1 - pipe))

    def last_copies(piece):
        at = pl.ds(pl.multiple_of(piece * quarter, quarter), quarter)
        return [
            pltpu.make_async_copy(first_rows.at[at], last_out.at[pipe, at], load.at[29 + piece]),
            remote(first_rows.at[at], last_out.at[pipe, at], (ls, lr), piece, at_pipe(1 - pipe)),
        ]

    def finish_last(piece):
        job = last_sums(piece)
        job.wait()
        column = row_to_column(scales_later[x, piece, 0:1, :])[:quarter]
        at = pl.ds(pl.multiple_of(piece * quarter, quarter), quarter)
        first_rows[at] = (first_rows[at].astype(F32) + column * job.result()).astype(BF16)
        job.finish()
        for copy in last_copies(piece):
            copy.start()

    def step(op, carry):
        layer, block = at_step(op)
        slot = op % 2

        @pl.when(layer == 0)
        def _():
            job = gather_of(block)
            job.wait(2, 3, 4, 5)
            job.finish()
            scales_of(block).wait()

        @pl.when(op == 4)
        def _():
            for copy in weight_loads(0):
                copy.wait()

        @pl.when((layer == 0) & (block == x))
        def _():
            second_copy.start()
            swap.start()

        for copy in loads_of(op):
            copy.wait()

        @pl.when(op < 7)
        def _():
            for copy in loads_of(op + 1):
                copy.start()

        at = pl.ds(pl.multiple_of(block * ROWS, ROWS), ROWS)

        @pl.when(layer == 0)
        def _():
            e_stage[slot] = errors[at]

        @pl.when(layer == 1)
        def _():
            error_load(op).wait()

        @pl.when(op < 3)
        def _():
            error_load(op + 1).start()

        e = e_stage[slot]
        def serve():
            @pl.when(op >= 1)
            def _():
                sums_of(op - 1).relay()

            @pl.when((op >= 2) & (op < 6))
            def _():
                gather_of(5 - op).relay()

            @pl.when(op == 7)
            def _():
                last_sums(0).relay()
                parts[0].core_sum(0).finish()
                pl.semaphore_wait(y_free, 2)
                parts[0].y_sum(0).start()

            @pl.when(op == 4)
            def _():
                first_load.wait()
                for of_part in parts:
                    of_part.core_sum(1).finish()
                    of_part.y_sum(1).start()
                pl.semaphore_signal(core_free, inc=1, device_id=at_core(1 - core), device_id_type=MESH)

            @pl.when(op == 5)
            def _():
                for of_part in parts:
                    of_part.y_sum(1).relay()

            @pl.when(op == 6)
            def _():
                for of_part in parts:
                    job = of_part.y_sum(1)
                    job.wait()
                    for half in range(2):
                        of_part.middle[half] = job.result(half).astype(BF16)
                    job.finish()
                for device in around(y, at_y):
                    pl.semaphore_signal(y_free, inc=1, device_id=device, device_id_type=MESH)

        turn = ((0,), (0,))

        def add_out():
            for index in range(total.shape[0] // ROWS):
                rows = slice(index * ROWS, (index + 1) * ROWS)
                total[rows, wide:] += mm(e_stage[slot, :, rows], mixed[...], turn)

        def send_on(of_part):
            of_part.flush(total)
            of_part.core_sum(layer).start()

        @pl.when(op == 7)
        def _():
            mix_rows(layer_sizes, scales.at[layer, block], few.at[layer], stage.at[slot], mixed)
            add_out()
            pl.semaphore_wait(core_free, 1)
            send_on(parts[0])

        backward_block(layer_sizes, block == 3, e, scales.at[layer, block], w_in[layer].reshape(e.shape[1], -1),
                       w_out[layer].reshape(e.shape[1], -1), few.at[layer],
                       selector[...], collector[...], stage.at[slot], p_stage.at[slot], state_stage.at[slot],
                       part.at[op % 3], grad, mixed, few_grad.at[layer], state, later, pad, serve)
        sums_of(op).start()

        @pl.when(op >= 1)
        def _():
            finish_sums(op - 1)

        @pl.when(op >= 6)
        def _():
            last_sums(op - 6).start()

        @pl.when(op < 7)
        def _():
            add_out()

        for index in range(total.shape[0] // ROWS):
            rows = slice(index * ROWS, (index + 1) * ROWS)
            total[rows, middle_at:wide] += mm(norm_stage[slot, :, rows], grad[:, middle_at:], turn)

        @pl.when(op == 3)
        def _():
            send_on(parts[0])

        @pl.when(block == 0)
        def _():
            send_on(parts[1])

        for index in range(total.shape[0] // ROWS):
            rows = slice(index * ROWS, (index + 1) * ROWS)
            total[rows, :middle_at] += mm(norm_stage[slot, :, rows], grad[:, :middle_at], turn)

        @pl.when(block == 0)
        def _():
            send_on(parts[2])

        @pl.when(op == 3)
        def _():
            total[...] = jnp.zeros_like(total)

        return carry

    lax.fori_loop(0, 8, step, 0)
    sums_of(7).relay()
    last_sums(1).relay()
    last_sums(2).start()
    last_sums(3).start()
    y_sums = [of_part.y_sum(0) for of_part in parts]
    z_sums = [of_part.z_sum() for of_part in parts]
    for of_part, job in zip(parts[1:], y_sums[1:]):
        of_part.core_sum(0).finish()
        job.start()
    y_sums[0].relay()
    finish_sums(7)
    for layer in range(2):
        width = few_grad.shape[2] - lead
        few_grad[layer, 6:7, lead:] = norm_grad[layer, 0:1, :width]
        few_grad[layer, 7:8, :] = norm_grad[layer, 0:1, width:]
    few_core = remote(few_grad, pair_few, (fs, fr), 0, at_core(1 - core))
    few_core.start()
    y_sums[0].wait()
    parts[0].to_z(y_sums[0])
    z_sums[0].start()
    y_sums[1].relay()
    y_sums[2].relay()
    few_core.wait()
    few_grad[...] = few_grad[...] + pair_few[...]
    few_y = Everyone(y, at_y, lambda to: few_grad, lambda me: y_few.at[me], (hs, hr))
    few_y.start()
    for block in range(4):
        hand_over(block).wait()
    deliveries = [
        Everyone(x, at_x, lambda to, sequence=sequence: both_grad.at[sequence, to],
                 lambda me, sequence=sequence: first_grad.at[sequence, me], [sem.at[sequence] for sem in (ds, dr)])
        for sequence in range(2)
    ]
    kept = [pltpu.make_async_copy(both_grad.at[sequence, x], first_grad.at[sequence, x], load.at[5 + 28 * sequence])
            for sequence in range(2)]
    for copy in deliveries + kept:
        copy.start()
    finish_last(0)
    last_sums(2).relay()
    finish_last(1)
    z_sums[0].relay()
    y_sums[1].wait()
    parts[1].to_z(y_sums[1])
    z_sums[1].start()
    last_sums(3).relay()
    finish_last(2)
    few_y.wait()
    y_few[y] = few_grad[...]
    few_grad[...] = (y_few[0] + y_few[1]) + (y_few[2] + y_few[3])
    few_z = Everyone(z, at_z, lambda to: few_grad.at[to % 2], lambda me: z_few.at[me], (js, jr))
    few_z.start()
    y_sums[2].wait()
    parts[2].to_z(y_sums[2])
    z_sums[2].start()
    z_sums[1].relay()
    finish_last(3)
    few_z.wait()
    z_few[z] = few_grad[pipe]
    few_sum[...] = (z_few[0] + z_few[1]) + (z_few[2] + z_few[3])
    x_few[x] = few_sum[...]
    few_x = Everyone(x, at_x, lambda to: few_sum, lambda me: x_few.at[me], (ks, kr))
    few_x.start()
    rows = parts[0].z_blocks.shape[2]

    def keep(at):
        z_sums[at].wait()
        for half in range(2):
            large[half * rows : (half + 1) * rows, ends[at]] = z_sums[at].result(half)

    keep(0)
    z_sums[2].relay()
    keep(1)
    state_rows = 2 * rows // 4
    for block in range(4):
        state_parts[0, block] = large[block * state_rows : (block + 1) * state_rows, 2 * inner : split]
    state_x = Everyone(x, at_x, lambda to: state_parts.at[0, to], lambda me: state_parts.at[1, me], (ws, wr))
    state_x.start()
    few_x.wait()
    few_shared[...] = (x_few[0] + x_few[1]) + (x_few[2] + x_few[3])
    state_x.wait()
    total_state = state_parts[0, x]
    for step_at in every:
        total_state = total_state + state_parts[1, (x + step_at) % 4]
    state_grad[...] = total_state
    keep(2)
    second_copy.wait()
    swap.wait()
    first_copy.wait()
    first_swap.wait()
    for piece in range(4):
        for copy in last_copies(piece):
            copy.wait()
    for copy in deliveries + kept:
        copy.wait()
    for job in y_sums + z_sums:
        job.finish()


def backward_all(errors, scales, weights_in, weights_out, few, normed, saved, saved_p, states, res, inverses, first_own, last_part,
                 inner, pair, heads, whole_inner):
    length, width = errors.shape
    _, blocks, quarter, _ = res.shape
    conv = inner + pair
    lead = conv - (width - conv)
    split = 2 * inner + pair
    piece = weights_in.shape[4]
    layout = [WeightParts.scratch(piece, columns) for columns in (inner, inner + LANES, inner + pair)]
    columns = weights_in.shape[5] + inner
    chunks = ROWS // CHUNK
    selector, collector = constants(inner, heads)
    shape = jax.ShapeDtypeStruct
    delivered = shape((2, blocks, quarter, width), BF16)
    few_shape = few.shape[1:]
    half = (quarter // 2, width)
    semaphores = lambda *count: [pltpu.SemaphoreType.DMA(count)] * 2
    return pl.pallas_call(
        partial(backward_all_kernel, (inner, pair, heads, lead, whole_inner)),
        out_shape=[
            shape((2, blocks * quarter, width), BF16),
            shape((2, blocks * quarter, width), BF16),
            delivered,
            shape((2, blocks * quarter, width), BF16),
            shape((piece, columns), F32),
            shape(few_shape, F32),
            shape(few_shape, F32),
            shape((piece // 4, pair), F32),
        ],
        in_specs=[ANY, VMEM, ANY, ANY, VMEM, VMEM, VMEM, ANY, ANY, ANY, ANY, VMEM, VMEM, ANY, ANY],
        out_specs=[ANY, ANY, ANY, ANY, VMEM, VMEM, VMEM, VMEM],
        scratch_shapes=[
            pltpu.VMEM((length, width), BF16),
            pltpu.VMEM((2, blocks, 4, 8, LANES), F32),
            pltpu.VMEM(weights_in.shape, BF16),
            pltpu.VMEM(weights_out.shape, BF16),
            pltpu.VMEM((3, ROWS, width), BF16),
            pltpu.VMEM((8, 2) + half, BF16),
            pltpu.VMEM((2, 2) + half, BF16),
            pltpu.VMEM((8, 2, 2) + half, BF16),
            pltpu.VMEM((2, ROWS, saved.shape[2]), F32),
            pltpu.VMEM((2, ROWS, conv), BF16),
            pltpu.VMEM((2, chunks, pair // 2, inner), F32),
            pltpu.VMEM((2, ROWS, width), BF16),
            pltpu.VMEM((2, ROWS, width), BF16),
            pltpu.VMEM((ROWS, split + LANES), BF16),
            pltpu.VMEM((ROWS, inner), BF16),
            pltpu.VMEM((blocks, 8, LANES), F32),
            pltpu.VMEM((blocks, quarter, width), F32),
            pltpu.VMEM((2, blocks, quarter, width), BF16),
            pltpu.VMEM((2,) + few_shape, F32),
            pltpu.VMEM((2, 8, width), F32),
            pltpu.VMEM((width, columns), F32),
        ]
        + [
            pltpu.VMEM((4, 2) + half, BF16),
            pltpu.VMEM((2, 2) + half, BF16),
            pltpu.VMEM((4, 2, 2) + half, BF16),
            pltpu.VMEM((4, 4) + half, BF16),
            pltpu.VMEM((ROWS, width), BF16),
            pltpu.VMEM((2,) + few_shape, F32),
            pltpu.VMEM((4, 2) + few_shape, F32),
            pltpu.VMEM((4,) + few_shape, F32),
            pltpu.VMEM((4,) + few_shape, F32),
            pltpu.VMEM((2, 4, piece // 4, pair), F32),
            pltpu.VMEM((pair // 2, inner), F32),
            pltpu.VMEM((pair // 2, inner), F32),
            pltpu.VMEM((ROWS + 8, conv), F32),
        ]
        + semaphores(8, 6) + semaphores(4, 6) + semaphores(4, 3)
        + semaphores(4, 6) + dma(4) + dma(2) + dma(1) + dma(3) + dma(3) + dma(3) + dma(3)
        + dma(4) + semaphores(2, 3)
        + [pltpu.SemaphoreType.DMA((5, 2)), pltpu.SemaphoreType.DMA((34,))]
        + [pltpu.SemaphoreType.REGULAR, pltpu.SemaphoreType.REGULAR]
        + flat([of_part[0] for of_part in layout])
        + flat([of_part[1] for of_part in layout]),
        compiler_params=pltpu.CompilerParams(collective_id=1, has_side_effects=True, vmem_limit_bytes=62 * 2**20),
        name="backward_layers",
    )(errors, scales, weights_in, weights_out, few, selector, collector, normed, saved, saved_p, states, res, inverses,
      first_own, last_part)


def finish_kernel(sizes, firsts, last_out, first_grad, second_grad, large, few_sum, few_shared, state_grad, few,
                  activations, input_grads, norm, gate_x, read_write, step, main, of_state, bias, rates, skip, gate,
                  out_weight):
    inner, pair, heads, lead = sizes
    first = lax.axis_index("pipe") == 0
    activations[0] = jnp.where(first, firsts[...], last_out[...]).astype(F32)
    input_grads[0] = jnp.where(first, first_grad[...], second_grad[...]).astype(F32)
    split = 2 * inner + pair

    @pl.when(pl.program_id(0) == 0)
    def _():
        norm[:, : few_shared.shape[1] - lead] = few_shared[6:7, lead:]
        norm[:, few_shared.shape[1] - lead :] = few_shared[7:8, :]
        for index in range(2):
            gate_x[0, :, index, :] = large[:, index * inner : (index + 1) * inner]
        read_write[0] = state_grad[...]
        step[0] = mm_exact((iota((heads, LANES), 0) == iota((heads, LANES), 1)).astype(F32),
                           large[:, split : split + LANES], ((1,), (1,)))
        for tap in range(5):
            main[tap] = few_sum[tap : tap + 1, :inner]
            of_state[tap] = few_shared[tap : tap + 1, inner:]
        bias[...] = few_sum[5:6, inner : inner + heads]
        rate = jnp.where(first, few[0, 5:6, inner + LANES :], few[1, 5:6, inner + LANES :])
        rates[...] = (few_sum[5:6, inner + LANES :] * rate)[:, :heads]
        width = inner // heads
        skip[...] = jnp.concatenate(
            [jnp.sum(few_sum[6:7, head * width : (head + 1) * width], 1, keepdims=True) for head in range(heads)], 1
        )
        gate[...] = few_sum[5:6, :inner]
        out_weight[0] = large[:, split + LANES :]


def finish_call(firsts, last_out, first_grad, second_grad, large, few_sum, few_shared, state_grad, few, inner, pair, heads):
    two, part, width = firsts.shape
    conv = few.shape[2]
    lead = conv - (width - conv)
    rows = part // 4
    piece = large.shape[0]
    by_rows = pl.BlockSpec((two, rows, width), lambda i: (0, i, 0))
    out_rows = pl.BlockSpec((1, two, rows, width), lambda i: (0, 0, i, 0))
    shape = lambda *sizes: jax.ShapeDtypeStruct(sizes, F32)
    small = [
        shape(1, width),
        shape(1, piece, 2, inner),
        shape(1, piece // 4, pair),
        shape(1, heads, piece),
        shape(5, 1, inner),
        shape(5, 1, pair),
        shape(1, heads),
        shape(1, heads),
        shape(1, heads),
        shape(1, inner),
        shape(1, piece, inner),
    ]
    return pl.pallas_call(
        partial(finish_kernel, (inner, pair, heads, lead)),
        grid=(4,),
        in_specs=[by_rows] * 4 + [whole(item) for item in (large, few_sum, few_shared, state_grad, few)],
        out_specs=[out_rows] * 2 + [whole(item) for item in small],
        out_shape=[shape(1, two, part, width)] * 2 + small,
        compiler_params=pltpu.CompilerParams(vmem_limit_bytes=60 * 2**20),
        name="outputs",
    )(firsts, last_out, first_grad.reshape(firsts.shape), second_grad, large, few_sum, few_shared, state_grad, few)


def whole(array):
    rank = len(array.shape)
    return pl.BlockSpec(array.shape, lambda i: (0,) * rank)


def body(inputs, out_grad, norm_gain, in_gate_x, in_read_write, in_step, conv_main, conv_state,
         step_bias, log_rate, skip_gain, gate_gain, out_weight):
    inner = out_weight.shape[2]
    pair = in_read_write.shape[2]
    heads = step_bias.shape[1]
    whole_inner = inner * lax.axis_size("tensor")
    few, weights_in, weights_out, errors, normed, saved, saved_p, states, res, inverses, scales, first_own, last_part = (
        forward_all(
            inputs, out_grad, out_weight[0], in_gate_x[0], in_read_write, in_step.transpose(0, 2, 1),
            conv_main.transpose(1, 0, 2), conv_state.transpose(1, 0, 2), step_bias, log_rate, skip_gain, gate_gain, norm_gain, inner, pair, heads, whole_inner
        )
    )
    firsts, last_out, first_grad, second_grad, large, few_sum, few_shared, state_grad = backward_all(
        errors, scales, weights_in, weights_out, few, normed, saved, saved_p, states, res, inverses, first_own, last_part,
        inner, pair, heads, whole_inner
    )
    outputs = finish_call(
        firsts, last_out, first_grad, second_grad, large, few_sum, few_shared, state_grad, few, inner, pair, heads
    )
    turned = [item.transpose(axes) for item, axes in zip(outputs[5:8], ((0, 2, 1), (1, 0, 2), (1, 0, 2)))]
    return (*outputs[:5], *turned, *outputs[8:])


def solution(mesh):
    in_specs = (
        P("dp", "tensor", None),
        P("dp", "tensor", None),
        P("pipe", None),
        P("pipe", "dp", None, "tensor"),
        P("pipe", "dp", None),
        P("pipe", "dp", "tensor"),
        P("pipe", None, "tensor"),
        P("pipe", None, None),
        P("pipe", "tensor"),
        P("pipe", "tensor"),
        P("pipe", "tensor"),
        P("pipe", "tensor"),
        P("pipe", "dp", "tensor"),
    )
    out_specs = (
        P("pipe", "dp", "tensor", None),
        P("pipe", "dp", "tensor", None),
        P("pipe", None),
        P("pipe", "dp", None, "tensor"),
        P("pipe", ("dp", "tensor"), None),
        P("pipe", "dp", "tensor"),
        P("pipe", None, "tensor"),
        P("pipe", None, None),
        P("pipe", "tensor"),
        P("pipe", "tensor"),
        P("pipe", "tensor"),
        P("pipe", "tensor"),
        P("pipe", "dp", "tensor"),
    )
    return jax.shard_map(body, mesh=mesh, in_specs=in_specs, out_specs=out_specs, check_vma=False)
```

```python
from functools import partial

import jax
import jax.numpy as jnp
import numpy as np
from jax import lax
from jax.experimental import pallas as pl
from jax.experimental.pallas import tpu as pltpu
from jax.sharding import PartitionSpec as P

F32, BF16 = jnp.float32, jnp.bfloat16
EPS = 1e-05
ROWS = 256
CHUNK = 128
LANES = 128
EXACT = lax.Precision.HIGHEST


def mm(left, right, contract=((1,), (0,))):
    return lax.dot_general(left, right, (contract, ((), ())), preferred_element_type=F32)


def mm_exact(left, right, contract=((1,), (0,))):
    return lax.dot_general(
        left, right, (contract, ((), ())), precision=EXACT, preferred_element_type=F32
    )


def spread(value, selector, heads):
    high = value.astype(BF16).astype(F32)
    both = high + pltpu.roll(value - high, heads, 1)
    return mm(both.astype(BF16), selector)


def per_head(value, collector):
    high = value.astype(BF16)
    low = (value - high.astype(F32)).astype(BF16)
    return mm(high, collector) + mm(low, collector)


def softplus(value):
    small = jnp.exp(-jnp.abs(value))
    series = small * (1.0 - small * (0.5 - small * (1.0 / 3.0 - small * 0.25)))
    return jnp.maximum(value, 0.0) + jnp.where(small < 0.01, series, jnp.log(1.0 + small))


def sigmoid(value):
    return 1.0 / (1.0 + jnp.exp(-value))


def iota(shape, axis):
    return lax.broadcasted_iota(jnp.int32, shape, axis)


def column_to_row(column):
    size = column.shape[0]
    same = iota((size, size), 0) == iota((size, size), 1)
    return jnp.sum(jnp.where(same, column, 0.0), 0, keepdims=True)


def row_to_column(row):
    size = row.shape[1]
    same = iota((size, size), 0) == iota((size, size), 1)
    return jnp.sum(jnp.where(same, row, 0.0), 1, keepdims=True)


def steps(raw, bias, rate, mask):
    delta = softplus(raw + bias) * mask
    tri = (iota((CHUNK, CHUNK), 0) >= iota((CHUNK, CHUNK), 1)).astype(F32)
    log_decay = mm_exact(tri, delta * rate)
    return delta, log_decay


def constants(inner, heads):
    width = inner // heads
    lane = np.arange(LANES)[:, None]
    channel = np.arange(inner)[None, :] // width
    selector = ((lane % heads == channel) & (lane < 2 * heads)).astype(np.float32)
    collector = (lane == channel).astype(np.float32).T
    return jnp.asarray(selector, BF16), jnp.asarray(collector, BF16)


MESH = pl.DeviceIdType.MESH
ANY = pl.BlockSpec(memory_space=pl.ANY)
VMEM = pl.BlockSpec(memory_space=pltpu.VMEM)


def place():
    pipe, dp, x = lax.axis_index("pipe"), lax.axis_index("dp"), lax.axis_index("tensor")
    return (dp // 8) * 2 + pipe, (dp // 2) % 4, dp % 2, x


def at_z(z):
    _, y, core, _ = place()
    return {"pipe": z % 2, "dp": ((z // 2) * 4 + y) * 2 + core}


def at_y(y):
    z, _, core, _ = place()
    return {"dp": ((z // 2) * 4 + y) * 2 + core}


def at_core(core):
    z, y, _, _ = place()
    return {"dp": ((z // 2) * 4 + y) * 2 + core}


def at_x(x):
    return {"tensor": x}


def at_pipe(pipe):
    return {"pipe": pipe}


def greet(*devices):
    barrier = pltpu.get_barrier_semaphore()
    for device in devices:
        pl.semaphore_signal(barrier, inc=1, device_id=device, device_id_type=MESH)
    pl.semaphore_wait(barrier, len(devices))


def around(me, device, steps=(1, 3)):
    return [device((me + step) % 4) for step in steps]


def remote(source, target, sems, index, device):
    return pltpu.make_async_remote_copy(
        src_ref=source,
        dst_ref=target,
        send_sem=sems[0].at[index],
        recv_sem=sems[1].at[index],
        device_id=device,
        device_id_type=MESH,
    )


class RingGather:
    def __init__(self, me, device, own, slot, sems, local=True):
        right, left, across = (me + 1) % 4, (me + 3) % 4, (me + 2) % 4
        to_right, to_left = device(right), device(left)
        self.copies = [
            remote(own(0), slot(me, 0), sems, 0, to_right),
            remote(own(1), slot(me, 1), sems, 1, to_left),
            remote(own(1), slot(me, 1), sems, 2, to_right),
            remote(own(0), slot(me, 0), sems, 3, to_left),
            remote(slot(left, 0), slot(left, 0), sems, 4, to_right),
            remote(slot(right, 1), slot(right, 1), sems, 5, to_left),
        ]
        self.origins = [(left, 0), (right, 1), (left, 1), (right, 0), (across, 0), (across, 1)]
        self.local = [
            pltpu.make_async_copy(own(half), slot(me, half), sems[2].at[half]) for half in range(2 * local)
        ]

    def start(self):
        for copy in self.copies[:4] + self.local:
            copy.start()

    def start_half(self, half):
        for index in ((0, 3), (1, 2))[half]:
            self.copies[index].start()
        self.local[half].start()

    def relay(self):
        for index in range(2):
            self.copies[index].wait_recv()
            self.copies[4 + index].start()

    def wait(self, *indices):
        for index in indices:
            self.copies[index].wait_recv()

    def wait_local(self):
        for copy in self.local:
            copy.wait()

    def wait_sends(self):
        for copy in self.copies:
            copy.wait_send()

    def finish(self):
        self.wait_local()
        self.wait_sends()


class RingScatter:
    def __init__(self, me, device, piece, buffers, sems, near=None):
        self.me, self.right, self.left = me, (me + 1) % 4, (me + 3) % 4
        across = (me + 2) % 4
        self.buffers = buffers
        self.near = near or [piece(me, 0), piece(me, 1), piece(self.right, 0), piece(self.left, 1)]
        relays, sums, arrived = buffers
        to_right, to_left = device(self.right), device(self.left)
        self.copies = [
            remote(piece(across, 0), relays.at[0], sems, 0, to_right),
            remote(piece(across, 1), relays.at[1], sems, 1, to_left),
            remote(piece(self.right, 1), arrived.at[0, 1], sems, 2, to_right),
            remote(piece(self.left, 0), arrived.at[1, 0], sems, 3, to_left),
            remote(sums.at[0], arrived.at[0, 0], sems, 4, to_right),
            remote(sums.at[1], arrived.at[1, 1], sems, 5, to_left),
        ]

    def start(self):
        for copy in self.copies[:4]:
            copy.start()

    def relay(self):
        relays, sums, _ = self.buffers
        for half in range(2):
            self.copies[half].wait_recv()
            total = relays[half].astype(F32) + self.near[2 + half][...].astype(F32)
            sums[half] = total.astype(sums.dtype)
            self.copies[4 + half].start()

    def wait(self):
        for index in range(2, 6):
            self.copies[index].wait_recv()

    def result(self, half):
        arrived = self.buffers[2]
        mine = self.near[half][...].astype(F32)
        return mine + arrived[0, half].astype(F32) + arrived[1, half].astype(F32)

    def finish(self):
        for copy in self.copies:
            copy.wait_send()


class Everyone:
    def __init__(self, me, device, source, target, sems):
        self.copies = [
            remote(source((me + step) % 4), target(me), sems, step - 1, device((me + step) % 4))
            for step in (1, 2, 3)
        ]

    def start(self):
        for copy in self.copies:
            copy.start()

    def wait(self):
        for copy in self.copies:
            copy.wait()


def dma(count):
    return [pltpu.SemaphoreType.DMA((count,)), pltpu.SemaphoreType.DMA((count,))]


def gather_sems():
    return dma(6) + [pltpu.SemaphoreType.DMA((2,))]


def scatter_buffers(*half):
    return [pltpu.VMEM((2,) + half, BF16), pltpu.VMEM((2,) + half, BF16), pltpu.VMEM((2, 2) + half, BF16)]


def norm_scale(value):
    return lax.rsqrt(jnp.mean(value * value, -1, keepdims=True) + EPS)


def norm_gain_of(few, layer, lead):
    return jnp.concatenate([few[layer, 6:7, lead:], few[layer, 7:8, :]], 1)


def remote_params(collective_id):
    return pltpu.CompilerParams(
        collective_id=collective_id, has_side_effects=True, vmem_limit_bytes=56 * 2**20
    )


def owned(block, x, rows):
    return pl.ds(pl.multiple_of(block * ROWS + x * rows, rows), rows)


class BlockSums:
    def __init__(self, x, piece, relays, sums, arrived, sems, op, near=None):
        self.right, self.left, self.me = (x + 1) % 4, (x + 3) % 4, x
        across = (x + 2) % 4
        self.relays, self.sums, self.arrived = relays, sums, arrived
        self.near = near or [piece(x, 0), piece(x, 1), piece(self.right, 0), piece(self.left, 1)]
        at_op = [sem.at[op] for sem in sems]
        to_right, to_left = at_x(self.right), at_x(self.left)
        self.copies = [
            remote(piece(across, 0), relays.at[op, 0], at_op, 0, to_right),
            remote(piece(across, 1), relays.at[op, 1], at_op, 1, to_left),
            remote(piece(self.right, 1), arrived.at[op, 0, 1], at_op, 2, to_right),
            remote(piece(self.left, 0), arrived.at[op, 1, 0], at_op, 3, to_left),
            remote(sums.at[op % 2, 0], arrived.at[op, 0, 0], at_op, 4, to_right),
            remote(sums.at[op % 2, 1], arrived.at[op, 1, 1], at_op, 5, to_left),
        ]
        self.op = op

    def start(self):
        for copy in self.copies[:4]:
            copy.start()

    def relay(self):
        for half in range(2):
            self.copies[half].wait_recv()
            total = self.relays[self.op, half].astype(F32) + self.near[2 + half][...].astype(F32)
            self.sums[self.op % 2, half] = total.astype(BF16)
            self.copies[4 + half].start()

    def wait(self):
        for index in range(2, 6):
            self.copies[index].wait_recv()

    def result(self):
        return jnp.concatenate(
            [
                self.near[half][...].astype(F32)
                + self.arrived[self.op, 0, half].astype(F32)
                + self.arrived[self.op, 1, half].astype(F32)
                for half in range(2)
            ],
            0,
        )

    def finish(self):
        for copy in self.copies:
            copy.wait_send()


def to_everyone(me, device, source, target, sems, op):
    at_op = [sem.at[op] for sem in sems]
    return Everyone(me, device, source, target, at_op)


def columns_of(inner, conv):
    ends = np.cumsum([0, inner, conv, LANES, inner])
    return [slice(int(begin), int(end)) for begin, end in zip(ends[:-1], ends[1:])], int(ends[-1])


def forward_block(sizes, first_block, last_layer, rows, e, w_in, w_out, few, selector, save, save_p, states, part,
                  squares, mixed, state, pad, serve):
    inner, pair, heads = sizes
    states_count = pair // 2
    split = inner + inner + pair
    conv = inner + pair
    (z_at, c_at, raw_at, y_at), _ = columns_of(inner, conv)

    @pl.when(first_block)
    def _():
        state[...] = jnp.zeros_like(state)
        pad[0:8, :] = jnp.zeros((8, conv), F32)

    @pl.when(jnp.logical_not(first_block))
    def _():
        pad[0:8, :] = pad[ROWS : ROWS + 8, :]

    projected = mm(rows, w_in)
    save[:, z_at] = projected[:, :inner]
    save_p[...] = projected[:, inner:split].astype(BF16)
    pad[8 : ROWS + 8, :] = projected[:, inner:split]
    save[:, raw_at] = projected[:, split:]
    bias = few[5:6, inner : inner + LANES]
    rate = few[5:6, inner + LANES : inner + 2 * LANES]
    gain = few[5:6, :inner]
    skip = few[6:7, :inner]
    mask = (iota((1, LANES), 1) < heads).astype(F32)
    first = iota((CHUNK, LANES), 1) < LANES // 2
    causal = iota((CHUNK, CHUNK), 0) >= iota((CHUNK, CHUNK), 1)
    owner_rows = ROWS // 4
    for chunk in range(ROWS // CHUNK):
        at = slice(chunk * CHUNK, (chunk + 1) * CHUNK)
        c = jnp.broadcast_to(few[4:5, :], (CHUNK, conv))
        for tap in range(4):
            begin = chunk * CHUNK + 5 + tap
            c = c + few[tap : tap + 1, :] * pad[begin : begin + CHUNK, :]
        save[at, c_at] = c
        value = c * sigmoid(c)
        xs = value[:, :inner]
        b_low = value[:, inner : inner + states_count].astype(BF16)
        c_low = value[:, inner + states_count :].astype(BF16)
        delta, log_decay = steps(save[at, raw_at], bias, rate, mask)
        turned = log_decay.T
        final = log_decay[CHUNK - 1 : CHUNK, :]
        scaled = spread(delta, selector, heads) * xs
        scaled_low = scaled.astype(BF16)
        products = jnp.where(causal, mm(c_low, b_low, ((1,), (1,))), 0.0)
        within = []
        for two in range(heads // 2):
            lanes = slice(two * LANES, (two + 1) * LANES)
            parts = []
            for h in (2 * two, 2 * two + 1):
                gap = jnp.minimum(log_decay[:, h : h + 1] - turned[h : h + 1, :], 0.0)
                parts.append(mm((products * jnp.exp(gap)).astype(BF16), scaled_low[:, lanes]))
            within.append(jnp.where(first, parts[0], parts[1]))
        old = state[...]
        states[chunk] = old
        carried = mm(c_low, old.astype(BF16)) * spread(jnp.exp(log_decay) * mask, selector, heads)
        y = jnp.concatenate(within, 1) + carried + skip * xs
        save[at, y_at] = y
        ends = (spread(jnp.exp(final - log_decay) * mask, selector, heads) * scaled).astype(BF16)
        keep = spread(jnp.broadcast_to(jnp.exp(final) * mask, (8, LANES)), selector, heads)[0:1]
        state[...] = keep * old + mm(b_low, ends, ((0,), (0,)))
        z = save[at, z_at]
        gated = y * (z * sigmoid(z))
        total = jnp.sum(gated * gated, 1, keepdims=True)
        for piece in range(CHUNK // owner_rows):
            row = column_to_row(total[piece * owner_rows : (piece + 1) * owner_rows])
            squares[chunk * (CHUNK // owner_rows) + piece, 0:1, 0:owner_rows] = row
        mixed[at, :] = (gated * gain).astype(BF16)
        if chunk == 0:
            serve()
    part[...] = mm(mixed[...], w_out(), ((1,), (1,))).astype(BF16)

    @pl.when(last_layer)
    def _():
        total = jnp.sum(mm(e[...], w_out()) * mixed[...].astype(F32), 1, keepdims=True)
        for piece in range(4):
            squares[piece, 1:2, 0:owner_rows] = column_to_row(total[piece * owner_rows : (piece + 1) * owner_rows])


class HandedRing:
    def __init__(self, me, device, source, slot, sems, core_sems):
        _, _, core, _ = place()
        self.slot = lambda origin, half: slot(origin, half, core)
        self.ring = RingGather(me, device, source, self.slot, sems)
        self.pieces = [(source(half), self.slot(me, half), 6 + half) for half in range(2)]
        for index in range(6):
            held = self.slot(*self.ring.origins[index])
            self.pieces.append((held, held, index))
        self.core_sems, self.device = core_sems, at_core(1 - core)

    def hand(self, at):
        source, target, index = self.pieces[at]
        return remote(source, target, self.core_sems, index, self.device)

    def start_half(self, half):
        self.ring.start_half(half)
        self.hand(half).start()

    def start(self):
        for half in range(2):
            self.start_half(half)

    def relay(self):
        self.ring.relay()
        for index in range(2):
            self.hand(2 + index).start()

    def finish(self):
        for index in range(2, 6):
            self.ring.wait(index)
            self.hand(2 + index).start()
        self.ring.finish()
        for at in range(8):
            self.hand(at).wait()


def gather_parameters(sizes, few, shard, gate_x, read_write, step, main, of_state, bias, log_rate, skip, gate, norm):
    inner, pair, heads, lead = sizes
    width = inner // heads
    few[...] = jnp.zeros_like(few)
    for tap in range(5):
        few[tap : tap + 1, :inner] = main[tap]
        few[tap : tap + 1, inner:] = of_state[tap]
    few[5:6, :inner] = gate[...]
    few[5:6, inner : inner + heads] = bias[...]
    few[5:6, inner + LANES : inner + LANES + heads] = -jnp.exp(log_rate[...])
    for head in range(heads):
        few[6:7, head * width : (head + 1) * width] = jnp.broadcast_to(skip[0:1, head : head + 1], (1, width))
    first = few.shape[1] - lead
    few[6:7, lead:] = norm[:, :first]
    few[7:8, :] = norm[:, first:]
    split = 2 * inner + pair
    both = gate_x[...]
    for index in range(2):
        shard[:, index * inner : (index + 1) * inner] = both[:, index, :]
    shard[:, 2 * inner : split] = read_write[0]
    same = (iota((heads, LANES), 0) == iota((heads, LANES), 1)).astype(BF16)
    shard[:, split:] = mm(step[0], same, ((0,), (0,))).astype(BF16)


def forward_all_kernel(sizes, inputs, out_grad, shard_out, gate_x, read_write, step_in, main, of_state, bias, log_rate,
                       skip, gate, norm, selector,
                       few_both, weights_in, weights_out, errors_out, normed, saved, saved_p, states, res, inverses, scales,
                       firsts, last_part,
                       hidden, w_in, w_out, errors, part, relays, sums, arrived, squares, others, stage, p_stage, state_stage,
                       norm_stage, mixed, state, pad, shard_in, z_weights, y_weights, few,
                       xs, xr, xl, es, er, el, zs, zr, zl, ys, yr, yl, cs, cr, y1s, y1r, y1l, c1s, c1r,
                       bs, br, bl, os, og, ol, c2s, c2r, fs, fr, rs, rr, gs, gr, qs, qr, outs, load):
    inner, pair, heads, lead, whole_inner = sizes
    layer_sizes = (inner, pair, heads)
    z, y, core, x = place()
    pipe = z % 2
    quarter = ROWS // 4
    gather_parameters((inner, pair, heads, lead), few.at[pipe], shard_in, gate_x, read_write, step_in, main, of_state,
                      bias, log_rate, skip, gate, norm)
    squares[...] = jnp.zeros_like(squares)
    greet(*around(x, at_x, (1, 2, 3)), *around(y, at_y), *around(z, at_z), at_core(1 - core), at_pipe(1 - pipe))
    few_swap = remote(few.at[pipe], few.at[pipe], (fs, fr), 0, at_pipe(1 - pipe))
    few_swap.start()
    piece = shard_in.shape[0]
    by_half = lambda half: pl.ds(half * (piece // 2), piece // 2)
    z_ring = RingGather(z, at_z, lambda half: shard_in.at[by_half(half)],
                        lambda origin, half: z_weights.at[origin, by_half(half)], (zs, zr, zl))
    z_ring.start()
    y_ring = RingGather(y, at_y, lambda half: shard_out.at[by_half(half)],
                        lambda origin, half: y_weights.at[origin, by_half(half)], (bs, br, bl))
    y_ring.start()
    block_rows = lambda origin, half: pl.ds(pl.multiple_of(origin * ROWS + half * (ROWS // 2), ROWS // 2), ROWS // 2)
    x_ring = RingGather(x, at_x, lambda half: inputs.at[pipe, half],
                        lambda origin, half: hidden.at[0, block_rows(origin, half)], (xs, xr, xl))
    x_ring.start()
    e_ring = RingGather(x, at_x, lambda half: out_grad.at[pipe, half],
                        lambda origin, half: errors.at[block_rows(origin, half)], (es, er, el))

    def in_ring(layer, sems, core_sems):
        away = pipe * (1 - layer) + (1 - pipe) * layer
        from_z = lambda half: (z + 3 * away + 2 * half) % 4
        return HandedRing(
            y, at_y, lambda half: z_weights.at[from_z(half)],
            lambda origin, half, core: w_in.at[layer, from_z(half) // 2, origin, core], sems, core_sems,
        )

    rings = [in_ring(0, (ys, yr, yl), (cs, cr)), in_ring(1, (y1s, y1r, y1l), (c1s, c1r))]
    out_ring = HandedRing(
        z, at_z, lambda half: y_weights.at[pl.ds(2 * half, 2)],
        lambda origin, half, core: w_out.at[origin % 2, origin // 2, pl.ds(2 * half, 2), core],
        (os, og, ol), (c2s, c2r),
    )
    z_ring.wait_local()

    @pl.when(pipe == 0)
    def _():
        rings[0].start_half(0)

    y_ring.relay()
    z_ring.relay()
    z_ring.wait(2)

    @pl.when(pipe == 1)
    def _():
        rings[0].start_half(0)

    z_ring.wait(3)

    @pl.when(pipe == 1)
    def _():
        rings[0].start_half(1)

    y_ring.wait(2, 3, 4, 5)
    y_ring.wait_local()
    out_ring.start()
    z_ring.wait(4, 5)

    @pl.when(pipe == 0)
    def _():
        rings[0].start_half(1)

    x_ring.relay()
    e_ring.start()
    out_ring.relay()
    rings[0].relay()
    z_ring.wait_sends()
    y_ring.wait_sends()
    few_swap.wait()
    few_both[...] = few[...]
    x_ring.wait(2, 3, 4, 5)
    x_ring.finish()
    for block in range(4):
        res[0, block] = hidden[0, owned(block, x, quarter)].astype(F32)
    rings[0].finish()
    rings[1].start()
    def sums_of(op):
        rows = lambda owner, half: part.at[op, pl.ds(pl.multiple_of(owner * quarter + half * (quarter // 2), quarter // 2), quarter // 2)]
        return BlockSums(x, rows, relays, sums, arrived, (rs, rr), op)

    def squares_of(op):
        return to_everyone(x, at_x, lambda to: squares.at[op], lambda me: others.at[op, me], (qs, qr), op)

    def gather_of(block):
        place_of = lambda origin, half: hidden.at[
            1, pl.ds(pl.multiple_of(block * ROWS + origin * quarter + half * (quarter // 2), quarter // 2), quarter // 2)
        ]
        return RingGather(x, at_x, lambda half: place_of(x, half), place_of, (gs.at[block], gr.at[block]), local=False)

    def outs_of(op):
        layer, block = op // 4, op % 4
        slot = op % 2
        at = pl.ds(pl.multiple_of(block * ROWS, ROWS), ROWS)
        count = ROWS // CHUNK
        return [
            pltpu.make_async_copy(stage.at[slot], saved.at[layer, at], outs.at[0, slot]),
            pltpu.make_async_copy(state_stage.at[slot], states.at[layer, pl.ds(block * count, count)], outs.at[1, slot]),
            pltpu.make_async_copy(norm_stage.at[slot], normed.at[layer, at], outs.at[2, slot]),
            pltpu.make_async_copy(p_stage.at[slot], saved_p.at[layer, at], outs.at[3, slot]),
        ]

    def row_sums(op, owner):
        total = others[op, 0, owner, 0:2, :]
        for device in (1, 2, 3):
            total = total + others[op, device, owner, 0:2, :]
        return lax.rsqrt(total[0:1] / whole_inner + EPS), total[1:2]

    def finish_sums(block):
        job = sums_of(block)
        squares_of(block).wait()
        others[block, x] = squares[block]
        inverse, _ = row_sums(block, x)
        inverses[block] = jnp.broadcast_to(inverse, (8, LANES))
        column = row_to_column(inverse)[:quarter]
        job.wait()
        value = res[0, block] + column * job.result()
        job.finish()
        res[1, block] = value
        hidden[1, owned(block, x, quarter)] = value.astype(BF16)
        gather_of(block).start()

    def finish_scales(block):
        squares_of(4 + block).wait()
        others[4 + block, x] = squares[4 + block]
        for owner in range(4):
            inverse, dots = row_sums(4 + block, owner)
            scales[block, owner, 0:1, :] = inverse
            scales[block, owner, 1:2, :] = dots * inverse / whole_inner

    own_block = hidden.at[1, pl.ds(pl.multiple_of(x * ROWS, ROWS), ROWS)]
    ends = [
        pltpu.make_async_copy(w_in.at[0], weights_in.at[0], load.at[0]),
        pltpu.make_async_copy(w_in.at[1], weights_in.at[1], load.at[1]),
        pltpu.make_async_copy(w_out, weights_out, load.at[2]),
        pltpu.make_async_copy(errors, errors_out, load.at[3]),
        pltpu.make_async_copy(own_block, firsts, load.at[4]),
    ]

    def part_copy(block):
        at = pl.ds(pl.multiple_of(block * ROWS, ROWS), ROWS)
        return pltpu.make_async_copy(part.at[4 + block], last_part.at[at], load.at[5 + block])

    def step(op, carry):
        layer, block = op // 4, op % 4

        @pl.when(layer == 1)
        def _():
            job = gather_of(block)
            job.wait(2, 3, 4, 5)
            job.finish()

        @pl.when(op == 7)
        def _():
            ends[4].start()

        @pl.when(op >= 2)
        def _():
            for copy in outs_of(op - 2):
                copy.wait()

        def serve():
            @pl.when(op == 0)
            def _():
                out_ring.finish()

            @pl.when(op == 1)
            def _():
                rings[1].relay()

            @pl.when((op >= 1) & (op < 5))
            def _():
                sums_of(op - 1).relay()

            @pl.when((op >= 2) & (op < 6))
            def _():
                gather_of(op - 2).relay()

            @pl.when(op == 3)
            def _():
                e_ring.wait(2, 3, 4, 5)
                e_ring.finish()
                rings[1].finish()
                for copy in ends[:4]:
                    copy.start()

            @pl.when(op >= 5)
            def _():
                finish_scales(op - 5)

        slot = op % 2
        at = pl.ds(pl.multiple_of(block * ROWS, ROWS), ROWS)
        value = hidden[layer, at].astype(F32)
        gain = jnp.concatenate([few[layer, 6:7, lead:], few[layer, 7:8, :]], 1)
        norm_stage[slot] = (value * norm_scale(value) * gain).astype(BF16)
        width = value.shape[1]
        forward_block(layer_sizes, block == 0, layer == 1, norm_stage[slot], errors.at[at],
                      w_in[layer].reshape(width, -1), lambda: w_out[layer].reshape(width, -1), few.at[layer], selector[...],
                      stage.at[slot], p_stage.at[slot], state_stage.at[slot], part.at[op], squares.at[op], mixed, state, pad, serve)
        for copy in outs_of(op):
            copy.start()
        squares_of(op).start()

        @pl.when(op < 4)
        def _():
            sums_of(op).start()

        @pl.when(op == 0)
        def _():
            e_ring.relay()

        @pl.when(op >= 4)
        def _():
            part_copy(op - 4).start()

        @pl.when((op >= 1) & (op < 5))
        def _():
            finish_sums(op - 1)

        return carry

    lax.fori_loop(0, 8, step, 0)
    finish_scales(3)
    for op in (6, 7):
        for copy in outs_of(op):
            copy.wait()
    for copy in ends:
        copy.wait()
    for block in range(4):
        part_copy(block).wait()


def forward_all(inputs, out_grad, shard_out, gate_x, read_write, step, main, of_state, bias, log_rate, skip, gate, norm,
                inner, pair, heads, whole_inner):
    _, part, width = inputs.shape
    rows = shard_out.shape[0]
    conv = inner + pair
    columns = inner + conv + LANES
    lead = conv - (width - conv)
    length = 4 * part
    _, saved_columns = columns_of(inner, conv)
    quarter = ROWS // 4
    chunks = ROWS // CHUNK
    selector, _ = constants(inner, heads)
    half = (2, 2, part // 2, width)
    shape = jax.ShapeDtypeStruct
    w_in = (2, 2, 4, 2, rows, columns)
    w_out = (2, 2, 4, 2, rows, inner)
    semaphores = lambda *count: [pltpu.SemaphoreType.DMA(count)] * 2
    return pl.pallas_call(
        partial(forward_all_kernel, (inner, pair, heads, lead, whole_inner)),
        out_shape=[
            shape((2, 8, conv), F32),
            shape(w_in, BF16),
            shape(w_out, BF16),
            shape((length, width), BF16),
            shape((2, length, width), BF16),
            shape((2, length, saved_columns), F32),
            shape((2, length, conv), BF16),
            shape((2, length // CHUNK, pair // 2, inner), F32),
            shape((2, 4, quarter, width), F32),
            shape((4, 8, LANES), F32),
            shape((4, 4, 8, LANES), F32),
            shape((part, width), BF16),
            shape((length, width), BF16),
        ],
        in_specs=[ANY, ANY, ANY] + [VMEM] * 11,
        out_specs=[VMEM, ANY, ANY, ANY, ANY, ANY, ANY, ANY, VMEM, VMEM, VMEM, ANY, ANY],
        scratch_shapes=[
            pltpu.VMEM((2, length, width), BF16),
            pltpu.VMEM(w_in, BF16),
            pltpu.VMEM(w_out, BF16),
            pltpu.VMEM((length, width), BF16),
            pltpu.VMEM((8, ROWS, width), BF16),
            pltpu.VMEM((4, 2, quarter // 2, width), BF16),
            pltpu.VMEM((4, 2, quarter // 2, width), BF16),
            pltpu.VMEM((4, 2, 2, quarter // 2, width), BF16),
            pltpu.VMEM((8, 4, 8, LANES), F32),
            pltpu.VMEM((8, 4, 4, 8, LANES), F32),
            pltpu.VMEM((2, ROWS, saved_columns), F32),
            pltpu.VMEM((2, ROWS, conv), BF16),
            pltpu.VMEM((2, chunks, pair // 2, inner), F32),
            pltpu.VMEM((2, ROWS, width), BF16),
            pltpu.VMEM((ROWS, inner), BF16),
            pltpu.VMEM((pair // 2, inner), F32),
            pltpu.VMEM((ROWS + 8, conv), F32),
            pltpu.VMEM((rows, columns), BF16),
            pltpu.VMEM((4, rows, columns), BF16),
            pltpu.VMEM((4, rows, inner), BF16),
            pltpu.VMEM((2, 8, conv), F32),
        ]
        + gather_sems() * 3
        + (gather_sems() + dma(8)) * 2
        + gather_sems()
        + gather_sems() + dma(8)
        + dma(1)
        + semaphores(4, 6) + semaphores(4, 6) + semaphores(8, 3)
        + [pltpu.SemaphoreType.DMA((4, 2)), pltpu.SemaphoreType.DMA((9,))],
        compiler_params=remote_params(0),
        name="forward_layers",
    )(inputs.reshape(half), out_grad.reshape(half), shard_out, gate_x, read_write, step, main, of_state, bias, log_rate,
      skip, gate, norm, selector)


class CoreSum:
    def __init__(self, grads, arrived, sems):
        _, _, core, _ = place()
        self.grads, self.arrived, self.core = grads, arrived, core
        self.pieces = [(y, half) for y in range(4) for half in range(2)]
        self.sems = sems

    def copy(self, index):
        y, half = self.pieces[index]
        source = self.grads.at[half, y, 1 - self.core]
        return remote(source, self.arrived.at[y, half], self.sems, index, at_core(1 - self.core))

    def start(self):
        for index in range(8):
            self.copy(index).start()

    def finish(self):
        for index, (y, half) in enumerate(self.pieces):
            self.copy(index).wait_recv()
            value = self.grads[half, y, self.core].astype(F32) + self.arrived[y, half].astype(F32)
            self.grads[half, y, self.core] = value.astype(BF16)
        for index in range(8):
            self.copy(index).wait_send()


def back_through_norm(value, grad_out, summed, gain):
    scale = norm_scale(value)
    unit = value * scale
    scaled = summed * gain
    mean = jnp.mean(scaled * unit, -1, keepdims=True)
    return grad_out + scale * (scaled - unit * mean), jnp.sum(summed * unit, 0, keepdims=True)


def backward_block(sizes, first_block, e, scales, w_in, w_out, few, selector, collector, saved, saved_p, states,
                   part, grad, mixed, few_out, state, later, pad, serve):
    inner, pair, heads = sizes
    states_count = pair // 2
    split = inner + inner + pair
    conv = inner + pair
    quarter = ROWS // 4
    (z_at, c_at, raw_at, y_at), _ = columns_of(inner, conv)

    @pl.when(first_block)
    def _():
        state[...] = jnp.zeros_like(state)
        later[...] = jnp.zeros_like(later)
        pad[ROWS : ROWS + 8, :] = jnp.zeros((8, conv), F32)

    @pl.when(jnp.logical_not(first_block))
    def _():
        pad[ROWS : ROWS + 8, :] = pad[0:8, :]

    bias = few[5:6, inner : inner + LANES]
    rate = few[5:6, inner + LANES : inner + 2 * LANES]
    gain = few[5:6, :inner]
    skip = few[6:7, :inner]
    mask = (iota((1, LANES), 1) < heads).astype(F32)
    first = iota((CHUNK, LANES), 1) < LANES // 2
    later_in = iota((CHUNK, CHUNK), 1) >= iota((CHUNK, CHUNK), 0)
    last = iota((CHUNK, LANES), 0) == CHUNK - 1
    tri = later_in.astype(F32)
    column = lambda row: jnp.concatenate(
        [row_to_column(scales[owner, row : row + 1, :])[:quarter] for owner in range(4)], 0
    )
    inverse = column(0)
    inner_dot = column(1)
    mixed_grad = mm(e, w_out)
    for chunk in reversed(range(ROWS // CHUNK)):
        at = slice(chunk * CHUNK, (chunk + 1) * CHUNK)
        z = saved[at, z_at]
        y = saved[at, y_at]
        sig = sigmoid(z)
        act = z * sig
        g = y * act * inverse[at]
        mixed[at, :] = (g * gain).astype(BF16)
        mixed_here = mixed_grad[at]
        gated_grad = inverse[at] * (mixed_here * gain - g * inner_dot[at])
        dy = gated_grad * act
        grad[at, :inner] = (gated_grad * y * (sig * (1.0 + z - act))).astype(BF16)
        c = saved[at, c_at]
        csig = sigmoid(c)
        value = c * csig
        slope = csig * (1.0 + c - value)
        xs = value[:, :inner]
        b_low = value[:, inner : inner + states_count].astype(BF16)
        c_low = value[:, inner + states_count :].astype(BF16)
        raw = saved[at, raw_at]
        delta, log_decay = steps(raw, bias, rate, mask)
        turned = log_decay.T
        final = log_decay[CHUNK - 1 : CHUNK, :]
        wide_delta = spread(delta, selector, heads)
        scaled = wide_delta * xs
        scaled_low = scaled.astype(BF16)
        dy_low = dy.astype(BF16)
        products = jnp.where(later_in, mm(b_low, c_low, ((1,), (1,))), 0.0)
        dproducts = jnp.zeros((CHUNK, CHUNK), F32)
        within = []
        for two in range(heads // 2):
            lanes = slice(two * LANES, (two + 1) * LANES)
            parts = []
            for odd in range(2):
                h = 2 * two + odd
                mine = first if odd == 0 else ~first
                decay = jnp.exp(jnp.minimum(turned[h : h + 1, :] - log_decay[:, h : h + 1], 0.0))
                parts.append(mm((products * decay).astype(BF16), dy_low[:, lanes]))
                own = jnp.where(mine, scaled_low[:, lanes], jnp.zeros((), BF16))
                dproducts = dproducts + decay * mm(own, dy_low[:, lanes], ((1,), (1,)))
            within.append(jnp.where(first, parts[0], parts[1]))
        dproducts = jnp.where(later_in, dproducts, 0.0).astype(BF16)
        old = states[chunk]
        old_low = old.astype(BF16)
        dstate = state[...]
        dstate_low = dstate.astype(BF16)
        to_end = spread(jnp.exp(final - log_decay) * mask, selector, heads)
        from_start = (spread(jnp.exp(log_decay) * mask, selector, heads) * dy).astype(BF16)
        dscaled = jnp.concatenate(within, 1) + to_end * mm(b_low, dstate_low)
        dc_state = mm(from_start, old_low, ((1,), (1,))) + mm(dproducts, b_low, ((0,), (0,)))
        db_state = mm((to_end * scaled).astype(BF16), dstate_low, ((1,), (1,))) + mm(dproducts, c_low)
        carry = jnp.broadcast_to(jnp.sum(later[...] * dstate, 0, keepdims=True), (8, inner))
        carry = per_head(carry, collector)[0:1]
        keep = spread(jnp.broadcast_to(jnp.exp(final) * mask, (8, LANES)), selector, heads)[0:1]
        state[...] = keep * dstate + mm(c_low, from_start, ((0,), (0,)))
        later[...] = old
        flow = dy_low.astype(F32) * (y - skip * xs) - scaled_low.astype(F32) * dscaled
        dlog = per_head(flow, collector) + jnp.where(last, carry, 0.0)
        dstep = mm_exact(tri, dlog)
        ddelta = per_head(xs * dscaled, collector) + rate * dstep
        draw = ddelta * sigmoid(raw + bias) * mask
        few_out[5:6, inner : inner + LANES] += jnp.sum(draw, 0, keepdims=True)
        few_out[5:6, inner + LANES : inner + 2 * LANES] += jnp.sum(delta * dstep, 0, keepdims=True)
        few_out[5:6, :inner] += jnp.sum(mixed_here * g, 0, keepdims=True)
        few_out[6:7, :inner] += jnp.sum(dy * xs, 0, keepdims=True)
        dxs = wide_delta * dscaled + skip * dy
        pad[at, :] = jnp.concatenate([dxs, db_state, dc_state], 1) * slope
        grad[at, split:] = draw.astype(BF16)
        if chunk == ROWS // CHUNK - 1:
            serve()
    for chunk in range(ROWS // CHUNK):
        at = slice(chunk * CHUNK, (chunk + 1) * CHUNK)
        p = saved_p[at, :].astype(F32)
        total = jnp.zeros((CHUNK, conv), F32)
        for tap in range(4):
            begin = chunk * CHUNK + 3 - tap
            shifted = pad[begin : begin + CHUNK, :]
            total = total + few[tap : tap + 1, :] * shifted
            few_out[tap : tap + 1, :] += jnp.sum(p * shifted, 0, keepdims=True)
        few_out[4:5, :] += jnp.sum(pad[at, :], 0, keepdims=True)
        grad[at, inner:split] = total.astype(BF16)
    part[...] = mm(grad[...], w_in, ((1,), (1,))).astype(BF16)


class WeightParts:
    def __init__(self, refs):
        (self.columns, self.low, self.core, self.y, self.z, self.middle, self.z_blocks, self.core_sems, self.y_sems,
         self.z_sems) = refs

    @staticmethod
    def scratch(piece, columns):
        grads = pltpu.VMEM((4, 2, piece, columns), BF16)
        return [
            [
                pltpu.VMEM((2, 4, 2, piece, columns), BF16),
                grads,
                scatter_buffers(piece, columns),
                scatter_buffers(piece // 2, columns),
                pltpu.VMEM((2, piece, columns), BF16),
                pltpu.VMEM((4, 2, piece // 2, columns), BF16),
            ],
            [[pltpu.SemaphoreType.DMA((2, 8))] * 2, [dma(6), dma(6)], dma(6)],
        ]

    def flush(self, total):
        piece = total.shape[0] // 16
        for index in range(16):
            z_hi, y_at, core_at = index // 8, (index // 2) % 4, index % 2
            self.low[z_hi, y_at, core_at] = total[index * piece : (index + 1) * piece, self.columns].astype(BF16)

    def core_sum(self, layer):
        return CoreSum(self.low, self.core, [sem.at[layer] for sem in self.core_sems])

    def y_sum(self, layer):
        _, y, core, _ = place()
        return RingScatter(y, at_y, lambda owner, half: self.low.at[half, owner, core], self.y, self.y_sems[layer])

    def z_sum(self):
        z, _, _, _ = place()
        return RingScatter(z, at_z, lambda owner, half: self.z_blocks.at[owner, half], self.z, self.z_sems)

    def to_z(self, sums):
        rows = self.z_blocks.shape[2]
        for z_hi in range(2):
            first = sums.result(z_hi).astype(BF16)
            second = self.middle[z_hi]
            for half in range(2):
                self.z_blocks[2 * z_hi, half] = first[half * rows : (half + 1) * rows]
                self.z_blocks[2 * z_hi + 1, half] = second[half * rows : (half + 1) * rows]


def mix_rows(sizes, scales, few, saved, mixed):
    inner, pair, _ = sizes
    (z_at, _, _, y_at), _ = columns_of(inner, inner + pair)
    quarter = ROWS // 4
    inverse = jnp.concatenate([row_to_column(scales[owner, 0:1, :])[:quarter] for owner in range(4)], 0)
    for chunk in range(ROWS // CHUNK):
        at = slice(chunk * CHUNK, (chunk + 1) * CHUNK)
        z = saved[at, z_at]
        g = saved[at, y_at] * (z * sigmoid(z)) * inverse[at]
        mixed[at, :] = (g * few[5:6, :inner]).astype(BF16)


def flat(tree):
    return jax.tree.leaves(tree)


def backward_all_kernel(sizes, errors_later, scales_later, weights_in, weights_out, few, selector, collector, normed,
                        saved, saved_p, states, res, inverses, first_own, last_part,
                        firsts, last_out, first_grad, second_grad, large, few_sum, few_shared, state_grad,
                        errors, scales, w_in, w_out, part, relays, sums, arrived, stage, p_stage, state_stage,
                        norm_stage, e_stage, grad, mixed, own_scales, own_grad, both_grad, few_grad, norm_grad, total,
                        t0, t1, t2, last_held, first_rows, pair_few, y_few, z_few, x_few, state_parts, state, later, pad,
                        rs, rr, gs, gr, ss, sr, ts, tr, ls, lr, ps, pr, fs, fr, hs, hr, js, jr, ks, kr, ws, wr, is_, ig, ds, dr,
                        loads, load, core_free, y_free, *rest):
    inner, pair, heads, lead, whole_inner = sizes
    layer_sizes = (inner, pair, heads)
    z, y, core, x = place()
    pipe = z % 2
    every = (1, 2, 3)
    quarter = ROWS // 4
    split = 2 * inner + pair
    wide = split + LANES
    middle_at = inner + pair
    ends = (slice(wide, total.shape[1]), slice(middle_at, wide), slice(0, middle_at))
    layout = [WeightParts.scratch(total.shape[0] // 16, at.stop - at.start) for at in ends]
    refs = iter(rest)
    memory = [jax.tree.map(lambda _: next(refs), of_part[0]) for of_part in layout]
    signals = [jax.tree.map(lambda _: next(refs), of_part[1]) for of_part in layout]
    parts = [WeightParts([at] + held + sems) for at, held, sems in zip(ends, memory, signals)]

    block_rows = lambda owner, half: pl.ds(pl.multiple_of(owner * ROWS + half * (ROWS // 2), ROWS // 2), ROWS // 2)

    def at_step(op):
        return 1 - op // 4, 3 - op % 4

    def loads_of(op):
        layer, block = at_step(op)
        slot = op % 2
        at = pl.ds(pl.multiple_of(block * ROWS, ROWS), ROWS)
        count = ROWS // CHUNK
        return [
            pltpu.make_async_copy(saved.at[layer, at], stage.at[slot], loads.at[0, slot]),
            pltpu.make_async_copy(states.at[layer, pl.ds(block * count, count)], state_stage.at[slot], loads.at[1, slot]),
            pltpu.make_async_copy(normed.at[layer, at], norm_stage.at[slot], loads.at[2, slot]),
            pltpu.make_async_copy(saved_p.at[layer, at], p_stage.at[slot], loads.at[3, slot]),
        ]

    def weight_loads(layer):
        return [
            pltpu.make_async_copy(weights_in.at[layer], w_in.at[layer], load.at[layer]),
            pltpu.make_async_copy(weights_out.at[layer], w_out.at[layer], load.at[6 + layer]),
        ]

    def error_load(op):
        _, block = at_step(op)
        at = pl.ds(pl.multiple_of(block * ROWS, ROWS), ROWS)
        return pltpu.make_async_copy(errors_later.at[at], e_stage.at[op % 2], loads.at[4, op % 2])

    own_loads = [
        pltpu.make_async_copy(errors_later.at[owned(block, x, quarter)], both_grad.at[pipe, block], load.at[9 + block])
        for block in range(4)
    ]
    last_rows = lambda piece, owner, half: last_part.at[
        pl.ds(pl.multiple_of(owner * ROWS + piece * quarter + half * (quarter // 2), quarter // 2), quarter // 2)
    ]
    sum_loads = [
        pltpu.make_async_copy(last_rows(piece, owner, half), last_held.at[piece, index], load.at[13 + 4 * piece + index])
        for piece in range(4)
        for index, (owner, half) in enumerate(((x, 0), (x, 1), ((x + 1) % 4, 0), ((x + 3) % 4, 1)))
    ]
    error_load(0).start()
    for copy in weight_loads(1) + loads_of(0):
        copy.start()
    first_load = pltpu.make_async_copy(first_own, first_rows, load.at[8])
    first_load.start()
    for copy in own_loads + sum_loads + weight_loads(0):
        copy.start()
    greet(*around(x, at_x, every), *around(y, at_y, every), *around(z, at_z, every), at_core(1 - core))

    def last_sums(piece):
        return BlockSums(x, lambda owner, half: last_rows(piece, owner, half), t0, t1, t2, (ts, tr), piece,
                         [last_held.at[piece, index] for index in range(4)])

    first_copy = pltpu.make_async_copy(first_own, firsts.at[pipe], load.at[2])
    first_swap = remote(first_own, firsts.at[pipe], (ps, pr), 1, at_pipe(1 - pipe))
    first_copy.start()
    first_swap.start()
    scales[1] = scales_later[...]
    few_grad[...] = jnp.zeros_like(few_grad)
    norm_grad[...] = jnp.zeros_like(norm_grad)
    own_scales[...] = jnp.zeros_like(own_scales)
    total[...] = jnp.zeros_like(total)
    for block, copy in enumerate(own_loads):
        copy.wait()
        own_grad[block] = both_grad[pipe, block].astype(F32)
    for copy in sum_loads:
        copy.wait()
    for copy in weight_loads(1):
        copy.wait()

    def sums_of(op):
        rows = lambda owner, half: part.at[
            op % 3, pl.ds(pl.multiple_of(owner * quarter + half * (quarter // 2), quarter // 2), quarter // 2)
        ]
        return BlockSums(x, rows, relays, sums, arrived, (rs, rr), op)

    def gather_of(block):
        place_of = lambda origin, half: errors.at[
            pl.ds(pl.multiple_of(block * ROWS + origin * quarter + half * (quarter // 2), quarter // 2), quarter // 2)
        ]
        return RingGather(x, at_x, lambda half: place_of(x, half), place_of, (gs.at[block], gr.at[block]), local=False)

    def scales_of(block):
        return to_everyone(x, at_x, lambda to: own_scales.at[block], lambda me: scales.at[0, block, me], (ss, sr), block)

    def hand_over(block):
        mine = both_grad.at[pipe, block]
        return remote(mine, mine, (is_, ig), block, at_pipe(1 - pipe))

    def finish_sums(op):
        layer, block = at_step(op)
        job = sums_of(op)
        job.wait()
        gain = jnp.concatenate([few[layer, 6:7, lead:], few[layer, 7:8, :]], 1)
        value, gain_part = back_through_norm(res[layer, block], own_grad[block], job.result(), gain)
        own_grad[block] = value
        norm_grad[layer, 0:1, :] += gain_part
        low = value.astype(BF16)
        job.finish()

        @pl.when(layer == 1)
        def _():
            errors[owned(block, x, quarter)] = low
            gather_of(block).start()
            dots = jnp.sum(low.astype(F32) * (res[1, block] - res[0, block]), -1, keepdims=True) / whole_inner
            own_scales[block, 0:1, :] = inverses[block, 0:1, :]
            own_scales[block, 1:2, 0:quarter] = column_to_row(dots)
            scales[0, block, x] = own_scales[block]
            scales_of(block).start()

        @pl.when(layer == 0)
        def _():
            both_grad[pipe, block] = low
            hand_over(block).start()

    own_block = errors.at[pl.ds(pl.multiple_of(x * ROWS, ROWS), ROWS)]
    second_copy = pltpu.make_async_copy(own_block, second_grad.at[pipe], load.at[4])
    swap = remote(own_block, second_grad.at[pipe], (ps, pr), 0, at_pipe(1 - pipe))

    def last_copies(piece):
        at = pl.ds(pl.multiple_of(piece * quarter, quarter), quarter)
        return [
            pltpu.make_async_copy(first_rows.at[at], last_out.at[pipe, at], load.at[29 + piece]),
            remote(first_rows.at[at], last_out.at[pipe, at], (ls, lr), piece, at_pipe(1 - pipe)),
        ]

    def finish_last(piece):
        job = last_sums(piece)
        job.wait()
        column = row_to_column(scales_later[x, piece, 0:1, :])[:quarter]
        at = pl.ds(pl.multiple_of(piece * quarter, quarter), quarter)
        first_rows[at] = (first_rows[at].astype(F32) + column * job.result()).astype(BF16)
        job.finish()
        for copy in last_copies(piece):
            copy.start()

    def step(op, carry):
        layer, block = at_step(op)
        slot = op % 2

        @pl.when(layer == 0)
        def _():
            job = gather_of(block)
            job.wait(2, 3, 4, 5)
            job.finish()
            scales_of(block).wait()

        @pl.when(op == 4)
        def _():
            for copy in weight_loads(0):
                copy.wait()

        @pl.when((layer == 0) & (block == x))
        def _():
            second_copy.start()
            swap.start()

        for copy in loads_of(op):
            copy.wait()

        @pl.when(op < 7)
        def _():
            for copy in loads_of(op + 1):
                copy.start()

        at = pl.ds(pl.multiple_of(block * ROWS, ROWS), ROWS)

        @pl.when(layer == 0)
        def _():
            e_stage[slot] = errors[at]

        @pl.when(layer == 1)
        def _():
            error_load(op).wait()

        @pl.when(op < 3)
        def _():
            error_load(op + 1).start()

        e = e_stage[slot]
        def serve():
            @pl.when(op >= 1)
            def _():
                sums_of(op - 1).relay()

            @pl.when((op >= 2) & (op < 6))
            def _():
                gather_of(5 - op).relay()

            @pl.when(op == 7)
            def _():
                last_sums(0).relay()
                parts[0].core_sum(0).finish()
                pl.semaphore_wait(y_free, 2)
                parts[0].y_sum(0).start()

            @pl.when(op == 4)
            def _():
                first_load.wait()
                for of_part in parts:
                    of_part.core_sum(1).finish()
                    of_part.y_sum(1).start()
                pl.semaphore_signal(core_free, inc=1, device_id=at_core(1 - core), device_id_type=MESH)

            @pl.when(op == 5)
            def _():
                for of_part in parts:
                    of_part.y_sum(1).relay()

            @pl.when(op == 6)
            def _():
                for of_part in parts:
                    job = of_part.y_sum(1)
                    job.wait()
                    for half in range(2):
                        of_part.middle[half] = job.result(half).astype(BF16)
                    job.finish()
                for device in around(y, at_y):
                    pl.semaphore_signal(y_free, inc=1, device_id=device, device_id_type=MESH)

        turn = ((0,), (0,))

        def add_out():
            for index in range(total.shape[0] // ROWS):
                rows = slice(index * ROWS, (index + 1) * ROWS)
                total[rows, wide:] += mm(e_stage[slot, :, rows], mixed[...], turn)

        def send_on(of_part):
            of_part.flush(total)
            of_part.core_sum(layer).start()

        @pl.when(op == 7)
        def _():
            mix_rows(layer_sizes, scales.at[layer, block], few.at[layer], stage.at[slot], mixed)
            add_out()
            pl.semaphore_wait(core_free, 1)
            send_on(parts[0])

        backward_block(layer_sizes, block == 3, e, scales.at[layer, block], w_in[layer].reshape(e.shape[1], -1),
                       w_out[layer].reshape(e.shape[1], -1), few.at[layer],
                       selector[...], collector[...], stage.at[slot], p_stage.at[slot], state_stage.at[slot],
                       part.at[op % 3], grad, mixed, few_grad.at[layer], state, later, pad, serve)
        sums_of(op).start()

        @pl.when(op >= 6)
        def _():
            last_sums(op - 6).start()

        @pl.when(op < 7)
        def _():
            add_out()

        for index in range(total.shape[0] // ROWS):
            rows = slice(index * ROWS, (index + 1) * ROWS)
            total[rows, middle_at:wide] += mm(norm_stage[slot, :, rows], grad[:, middle_at:], turn)

        @pl.when(op == 3)
        def _():
            send_on(parts[0])

        @pl.when(block == 0)
        def _():
            send_on(parts[1])

        @pl.when(op >= 1)
        def _():
            finish_sums(op - 1)

        for index in range(total.shape[0] // ROWS):
            rows = slice(index * ROWS, (index + 1) * ROWS)
            total[rows, :middle_at] += mm(norm_stage[slot, :, rows], grad[:, :middle_at], turn)

        @pl.when(block == 0)
        def _():
            send_on(parts[2])

        @pl.when(op == 3)
        def _():
            total[...] = jnp.zeros_like(total)

        return carry

    lax.fori_loop(0, 8, step, 0)
    sums_of(7).relay()
    last_sums(1).relay()
    last_sums(2).start()
    last_sums(3).start()
    y_sums = [of_part.y_sum(0) for of_part in parts]
    z_sums = [of_part.z_sum() for of_part in parts]
    for of_part, job in zip(parts[1:], y_sums[1:]):
        of_part.core_sum(0).finish()
        job.start()
    y_sums[0].relay()
    finish_sums(7)
    for layer in range(2):
        width = few_grad.shape[2] - lead
        few_grad[layer, 6:7, lead:] = norm_grad[layer, 0:1, :width]
        few_grad[layer, 7:8, :] = norm_grad[layer, 0:1, width:]
    few_core = remote(few_grad, pair_few, (fs, fr), 0, at_core(1 - core))
    few_core.start()
    y_sums[0].wait()
    parts[0].to_z(y_sums[0])
    z_sums[0].start()
    y_sums[1].relay()
    y_sums[2].relay()
    few_core.wait()
    few_grad[...] = few_grad[...] + pair_few[...]
    few_y = Everyone(y, at_y, lambda to: few_grad, lambda me: y_few.at[me], (hs, hr))
    few_y.start()
    for block in range(4):
        hand_over(block).wait()
    deliveries = [
        Everyone(x, at_x, lambda to, sequence=sequence: both_grad.at[sequence, to],
                 lambda me, sequence=sequence: first_grad.at[sequence, me], [sem.at[sequence] for sem in (ds, dr)])
        for sequence in range(2)
    ]
    kept = [pltpu.make_async_copy(both_grad.at[sequence, x], first_grad.at[sequence, x], load.at[5 + 28 * sequence])
            for sequence in range(2)]
    for copy in deliveries + kept:
        copy.start()
    finish_last(0)
    last_sums(2).relay()
    finish_last(1)
    z_sums[0].relay()
    y_sums[1].wait()
    parts[1].to_z(y_sums[1])
    z_sums[1].start()
    last_sums(3).relay()
    finish_last(2)
    few_y.wait()
    y_few[y] = few_grad[...]
    few_grad[...] = (y_few[0] + y_few[1]) + (y_few[2] + y_few[3])
    few_z = Everyone(z, at_z, lambda to: few_grad.at[to % 2], lambda me: z_few.at[me], (js, jr))
    few_z.start()
    y_sums[2].wait()
    parts[2].to_z(y_sums[2])
    z_sums[2].start()
    z_sums[1].relay()
    finish_last(3)
    few_z.wait()
    z_few[z] = few_grad[pipe]
    few_sum[...] = (z_few[0] + z_few[1]) + (z_few[2] + z_few[3])
    x_few[x] = few_sum[...]
    few_x = Everyone(x, at_x, lambda to: few_sum, lambda me: x_few.at[me], (ks, kr))
    few_x.start()
    rows = parts[0].z_blocks.shape[2]

    def keep(at):
        z_sums[at].wait()
        for half in range(2):
            large[half * rows : (half + 1) * rows, ends[at]] = z_sums[at].result(half)

    keep(0)
    z_sums[2].relay()
    keep(1)
    state_rows = 2 * rows // 4
    for block in range(4):
        state_parts[0, block] = large[block * state_rows : (block + 1) * state_rows, 2 * inner : split]
    state_x = Everyone(x, at_x, lambda to: state_parts.at[0, to], lambda me: state_parts.at[1, me], (ws, wr))
    state_x.start()
    few_x.wait()
    few_shared[...] = (x_few[0] + x_few[1]) + (x_few[2] + x_few[3])
    state_x.wait()
    total_state = state_parts[0, x]
    for step_at in every:
        total_state = total_state + state_parts[1, (x + step_at) % 4]
    state_grad[...] = total_state
    keep(2)
    second_copy.wait()
    swap.wait()
    first_copy.wait()
    first_swap.wait()
    for piece in range(4):
        for copy in last_copies(piece):
            copy.wait()
    for copy in deliveries + kept:
        copy.wait()
    for job in y_sums + z_sums:
        job.finish()


def backward_all(errors, scales, weights_in, weights_out, few, normed, saved, saved_p, states, res, inverses, first_own, last_part,
                 inner, pair, heads, whole_inner):
    length, width = errors.shape
    _, blocks, quarter, _ = res.shape
    conv = inner + pair
    lead = conv - (width - conv)
    split = 2 * inner + pair
    piece = weights_in.shape[4]
    layout = [WeightParts.scratch(piece, columns) for columns in (inner, inner + LANES, inner + pair)]
    columns = weights_in.shape[5] + inner
    chunks = ROWS // CHUNK
    selector, collector = constants(inner, heads)
    shape = jax.ShapeDtypeStruct
    delivered = shape((2, blocks, quarter, width), BF16)
    few_shape = few.shape[1:]
    half = (quarter // 2, width)
    semaphores = lambda *count: [pltpu.SemaphoreType.DMA(count)] * 2
    return pl.pallas_call(
        partial(backward_all_kernel, (inner, pair, heads, lead, whole_inner)),
        out_shape=[
            shape((2, blocks * quarter, width), BF16),
            shape((2, blocks * quarter, width), BF16),
            delivered,
            shape((2, blocks * quarter, width), BF16),
            shape((piece, columns), F32),
            shape(few_shape, F32),
            shape(few_shape, F32),
            shape((piece // 4, pair), F32),
        ],
        in_specs=[ANY, VMEM, ANY, ANY, VMEM, VMEM, VMEM, ANY, ANY, ANY, ANY, VMEM, VMEM, ANY, ANY],
        out_specs=[ANY, ANY, ANY, ANY, VMEM, VMEM, VMEM, VMEM],
        scratch_shapes=[
            pltpu.VMEM((length, width), BF16),
            pltpu.VMEM((2, blocks, 4, 8, LANES), F32),
            pltpu.VMEM(weights_in.shape, BF16),
            pltpu.VMEM(weights_out.shape, BF16),
            pltpu.VMEM((3, ROWS, width), BF16),
            pltpu.VMEM((8, 2) + half, BF16),
            pltpu.VMEM((2, 2) + half, BF16),
            pltpu.VMEM((8, 2, 2) + half, BF16),
            pltpu.VMEM((2, ROWS, saved.shape[2]), F32),
            pltpu.VMEM((2, ROWS, conv), BF16),
            pltpu.VMEM((2, chunks, pair // 2, inner), F32),
            pltpu.VMEM((2, ROWS, width), BF16),
            pltpu.VMEM((2, ROWS, width), BF16),
            pltpu.VMEM((ROWS, split + LANES), BF16),
            pltpu.VMEM((ROWS, inner), BF16),
            pltpu.VMEM((blocks, 8, LANES), F32),
            pltpu.VMEM((blocks, quarter, width), F32),
            pltpu.VMEM((2, blocks, quarter, width), BF16),
            pltpu.VMEM((2,) + few_shape, F32),
            pltpu.VMEM((2, 8, width), F32),
            pltpu.VMEM((width, columns), F32),
        ]
        + [
            pltpu.VMEM((4, 2) + half, BF16),
            pltpu.VMEM((2, 2) + half, BF16),
            pltpu.VMEM((4, 2, 2) + half, BF16),
            pltpu.VMEM((4, 4) + half, BF16),
            pltpu.VMEM((ROWS, width), BF16),
            pltpu.VMEM((2,) + few_shape, F32),
            pltpu.VMEM((4, 2) + few_shape, F32),
            pltpu.VMEM((4,) + few_shape, F32),
            pltpu.VMEM((4,) + few_shape, F32),
            pltpu.VMEM((2, 4, piece // 4, pair), F32),
            pltpu.VMEM((pair // 2, inner), F32),
            pltpu.VMEM((pair // 2, inner), F32),
            pltpu.VMEM((ROWS + 8, conv), F32),
        ]
        + semaphores(8, 6) + semaphores(4, 6) + semaphores(4, 3)
        + semaphores(4, 6) + dma(4) + dma(2) + dma(1) + dma(3) + dma(3) + dma(3) + dma(3)
        + dma(4) + semaphores(2, 3)
        + [pltpu.SemaphoreType.DMA((5, 2)), pltpu.SemaphoreType.DMA((34,))]
        + [pltpu.SemaphoreType.REGULAR, pltpu.SemaphoreType.REGULAR]
        + flat([of_part[0] for of_part in layout])
        + flat([of_part[1] for of_part in layout]),
        compiler_params=pltpu.CompilerParams(collective_id=1, has_side_effects=True, vmem_limit_bytes=62 * 2**20),
        name="backward_layers",
    )(errors, scales, weights_in, weights_out, few, selector, collector, normed, saved, saved_p, states, res, inverses,
      first_own, last_part)


def finish_kernel(sizes, firsts, last_out, first_grad, second_grad, large, few_sum, few_shared, state_grad, few,
                  activations, input_grads, norm, gate_x, read_write, step, main, of_state, bias, rates, skip, gate,
                  out_weight):
    inner, pair, heads, lead = sizes
    first = lax.axis_index("pipe") == 0
    activations[0] = jnp.where(first, firsts[...], last_out[...]).astype(F32)
    input_grads[0] = jnp.where(first, first_grad[...], second_grad[...]).astype(F32)
    split = 2 * inner + pair

    @pl.when(pl.program_id(0) == 0)
    def _():
        norm[:, : few_shared.shape[1] - lead] = few_shared[6:7, lead:]
        norm[:, few_shared.shape[1] - lead :] = few_shared[7:8, :]
        for index in range(2):
            gate_x[0, :, index, :] = large[:, index * inner : (index + 1) * inner]
        read_write[0] = state_grad[...]
        step[0] = mm_exact((iota((heads, LANES), 0) == iota((heads, LANES), 1)).astype(F32),
                           large[:, split : split + LANES], ((1,), (1,)))
        for tap in range(5):
            main[tap] = few_sum[tap : tap + 1, :inner]
            of_state[tap] = few_shared[tap : tap + 1, inner:]
        bias[...] = few_sum[5:6, inner : inner + heads]
        rate = jnp.where(first, few[0, 5:6, inner + LANES :], few[1, 5:6, inner + LANES :])
        rates[...] = (few_sum[5:6, inner + LANES :] * rate)[:, :heads]
        width = inner // heads
        skip[...] = jnp.concatenate(
            [jnp.sum(few_sum[6:7, head * width : (head + 1) * width], 1, keepdims=True) for head in range(heads)], 1
        )
        gate[...] = few_sum[5:6, :inner]
        out_weight[0] = large[:, split + LANES :]


def finish_call(firsts, last_out, first_grad, second_grad, large, few_sum, few_shared, state_grad, few, inner, pair, heads):
    two, part, width = firsts.shape
    conv = few.shape[2]
    lead = conv - (width - conv)
    rows = part // 4
    piece = large.shape[0]
    by_rows = pl.BlockSpec((two, rows, width), lambda i: (0, i, 0))
    out_rows = pl.BlockSpec((1, two, rows, width), lambda i: (0, 0, i, 0))
    shape = lambda *sizes: jax.ShapeDtypeStruct(sizes, F32)
    small = [
        shape(1, width),
        shape(1, piece, 2, inner),
        shape(1, piece // 4, pair),
        shape(1, heads, piece),
        shape(5, 1, inner),
        shape(5, 1, pair),
        shape(1, heads),
        shape(1, heads),
        shape(1, heads),
        shape(1, inner),
        shape(1, piece, inner),
    ]
    return pl.pallas_call(
        partial(finish_kernel, (inner, pair, heads, lead)),
        grid=(4,),
        in_specs=[by_rows] * 4 + [whole(item) for item in (large, few_sum, few_shared, state_grad, few)],
        out_specs=[out_rows] * 2 + [whole(item) for item in small],
        out_shape=[shape(1, two, part, width)] * 2 + small,
        compiler_params=pltpu.CompilerParams(vmem_limit_bytes=60 * 2**20),
        name="outputs",
    )(firsts, last_out, first_grad.reshape(firsts.shape), second_grad, large, few_sum, few_shared, state_grad, few)


def whole(array):
    rank = len(array.shape)
    return pl.BlockSpec(array.shape, lambda i: (0,) * rank)


def body(inputs, out_grad, norm_gain, in_gate_x, in_read_write, in_step, conv_main, conv_state,
         step_bias, log_rate, skip_gain, gate_gain, out_weight):
    inner = out_weight.shape[2]
    pair = in_read_write.shape[2]
    heads = step_bias.shape[1]
    whole_inner = inner * lax.axis_size("tensor")
    few, weights_in, weights_out, errors, normed, saved, saved_p, states, res, inverses, scales, first_own, last_part = (
        forward_all(
            inputs, out_grad, out_weight[0], in_gate_x[0], in_read_write, in_step.transpose(0, 2, 1),
            conv_main.transpose(1, 0, 2), conv_state.transpose(1, 0, 2), step_bias, log_rate, skip_gain, gate_gain, norm_gain, inner, pair, heads, whole_inner
        )
    )
    firsts, last_out, first_grad, second_grad, large, few_sum, few_shared, state_grad = backward_all(
        errors, scales, weights_in, weights_out, few, normed, saved, saved_p, states, res, inverses, first_own, last_part,
        inner, pair, heads, whole_inner
    )
    outputs = finish_call(
        firsts, last_out, first_grad, second_grad, large, few_sum, few_shared, state_grad, few, inner, pair, heads
    )
    turned = [item.transpose(axes) for item, axes in zip(outputs[5:8], ((0, 2, 1), (1, 0, 2), (1, 0, 2)))]
    return (*outputs[:5], *turned, *outputs[8:])


def solution(mesh):
    in_specs = (
        P("dp", "tensor", None),
        P("dp", "tensor", None),
        P("pipe", None),
        P("pipe", "dp", None, "tensor"),
        P("pipe", "dp", None),
        P("pipe", "dp", "tensor"),
        P("pipe", None, "tensor"),
        P("pipe", None, None),
        P("pipe", "tensor"),
        P("pipe", "tensor"),
        P("pipe", "tensor"),
        P("pipe", "tensor"),
        P("pipe", "dp", "tensor"),
    )
    out_specs = (
        P("pipe", "dp", "tensor", None),
        P("pipe", "dp", "tensor", None),
        P("pipe", None),
        P("pipe", "dp", None, "tensor"),
        P("pipe", ("dp", "tensor"), None),
        P("pipe", "dp", "tensor"),
        P("pipe", None, "tensor"),
        P("pipe", None, None),
        P("pipe", "tensor"),
        P("pipe", "tensor"),
        P("pipe", "tensor"),
        P("pipe", "tensor"),
        P("pipe", "dp", "tensor"),
    )
    return jax.shard_map(body, mesh=mesh, in_specs=in_specs, out_specs=out_specs, check_vma=False)
```
